256 devices in a mesh: dp: 16 (over y_lo, z), tensor: 16 (over x, y_hi, core).
Axes of the slice: x: 4, y: 4 (y_hi: 2, y_lo: 2; y = y_hi * 2 + y_lo), z: 8, core: 2. Of those that a mesh axis runs over, the one named last changes fastest.
Arguments:
- tokens: bfloat16 [12288, 8192], P('dp', 'tensor'), may hold values from -40 to 40
- gain: float32 [8192], P('tensor'), may hold values from 0.1 to 1.9
- w_first: bfloat16 [32, 256, 512], P('tensor'), may hold values from -0.375 to 0.375
- w_second: bfloat16 [16, 1024, 1024], P('tensor'), may hold values from -0.1875 to 0.1875
- w_third: bfloat16 [16, 1024, 1024], P('tensor'), may hold values from -0.1875 to 0.1875
- w_fourth: bfloat16 [32, 512, 256], P('tensor'), may hold values from -0.25 to 0.25
- cotangent: bfloat16 [12288, 8192], P('dp', 'tensor'), may hold values from -5 to 5
Outputs:
- output: bfloat16 [12288, 8192], P('dp', 'tensor')
- token_gradient: bfloat16 [12288, 8192], P('dp', 'tensor')
- grad_first: float32 [32, 256, 512], P('tensor', 'dp')
- grad_second: float32 [16, 1024, 1024], P('tensor', 'dp')
- grad_third: float32 [16, 1024, 1024], P('tensor', 'dp')
- grad_fourth: float32 [32, 512, 256], P('tensor', 'dp')
The draws below stay inside these ranges and needn't reach their ends.
All inputs are finite; a program needn't handle non-finite values.
Results may differ from the reference program's by a relative error of at most 0.023.
Values may be sent and summed in bfloat16 or wider, within the bound.
No kernel may reach another device: no remote copies, remote signals or barrier semaphores. Data moves between devices by JAX's collectives and lax.ppermute only.
A program may use at most 128 MiB of HBM per device.

```python
import math
import jax
import jax.numpy as jnp
from jax import lax

MODEL_WIDTH = 8192
DIAGONAL_BLOCKS = 32
HBS = 1024
HB = 16
TOK_DEV = 768
BS = 256
EB = 32
TOKENS = 12288
N_DP = 16


def draw_tokens(key, part):
    key = jax.random.fold_in(key, 11)
    key_base, key_cols, key_rows = jax.random.split(key, 3)
    columns = jnp.arange(MODEL_WIDTH, dtype=jnp.float32) / MODEL_WIDTH
    col_scale = 0.3 * jnp.exp(columns * math.log(3.0)) * jnp.exp(jax.random.uniform(key_cols, (MODEL_WIDTH,), jnp.float32, 0.0, math.log(3.3)))
    row_scale = 0.3 * jnp.exp(jax.random.uniform(key_rows, (TOKENS, 1), jnp.float32, 0.0, math.log(10.0)))
    base = jnp.clip(jax.random.normal(key_base, (TOKENS, MODEL_WIDTH), jnp.float32), -4.0, 4.0)
    return (row_scale * col_scale[None, :] * base).astype(jnp.bfloat16)


def level_of(stream_key, shape, shards, smallest, high):
    level = 1.0
    for position, parts in shards:
        draws = jax.random.uniform(jax.random.fold_in(jax.random.fold_in(stream_key, 6), position), (parts,), jnp.float32, smallest / len(shards), high / len(shards))
        level = level * jnp.repeat(jnp.exp(draws), shape[position] // parts).reshape((-1,) + (1,) * (len(shape) - 1 - position))
    return level


def gaussian(own_key, dims, deviation, most, cuts=(), kind=jnp.bfloat16):
    factor_of = level_of(own_key, dims, cuts, -0.22, 0.18) if cuts else 1.0
    result = jax.random.normal(own_key, dims, jnp.float32) * deviation * factor_of
    return jnp.minimum(jnp.maximum(result, -most), most).astype(kind)


def setup_inputs(seed: int = 0) -> dict:
    key_list = jax.random.split(jax.random.key(seed), 8)
    return {
        "tokens": draw_tokens(jax.random.fold_in(key_list[7], 71), 0),
        "gain": jnp.clip(1.0 + 0.18 * jax.random.normal(key_list[1], (MODEL_WIDTH,), jnp.float32), 0.1, 1.9),
        "w_first": gaussian(key_list[2], (DIAGONAL_BLOCKS, BS, HB * EB), BS ** -0.5, 0.375, ((0, 16),)),
        "w_second": gaussian(key_list[3], (HB, DIAGONAL_BLOCKS * EB, HBS), (DIAGONAL_BLOCKS * EB) ** -0.5, 0.1875, ((0, 16),)),
        "w_third": gaussian(key_list[4], (HB, HBS, DIAGONAL_BLOCKS * EB), HBS ** -0.5, 0.1875, ((0, 16),)),
        "w_fourth": gaussian(key_list[5], (DIAGONAL_BLOCKS, HB * EB, BS), (HB * EB) ** -0.5, 0.25, ((0, 16),)),
        "cotangent": gaussian(key_list[6], (TOKENS, MODEL_WIDTH), 1.0, 5.0, ((0, 16), (1, 16))),
    }


epsilon = 1e-05
root_scale = math.sqrt(2.0 / math.pi)
cubic_term = 0.044715

def gelu_value(value):
    return 0.5 * value * (1.0 + jnp.tanh(root_scale * (value + cubic_term * value * value * value)))

def gelu_slope(value):
    hyper = jnp.tanh(root_scale * (value + cubic_term * value * value * value))
    return 0.5 * (1.0 + hyper) + 0.5 * value * (1.0 - hyper * hyper) * root_scale * (1.0 + 3.0 * cubic_term * value * value)

def to_single_float(array):
    return array.astype(jnp.float32)

def layer_block(x_block, output_gradient_block, gain, w_first, w_second, w_third, w_fourth):
    element_count = x_block.shape[0]
    eb_size = HBS // DIAGONAL_BLOCKS
    complete_input = to_single_float(x_block)
    reciprocal_norm = lax.rsqrt(lax.optimization_barrier(jnp.mean(complete_input * complete_input, axis=1, keepdims=True)) + epsilon)
    centered_input = complete_input * reciprocal_norm
    normalized_input = (centered_input * gain).astype(jnp.bfloat16).reshape(element_count, DIAGONAL_BLOCKS, MODEL_WIDTH // DIAGONAL_BLOCKS)
    first = jnp.einsum('tak,akh->tah', to_single_float(normalized_input), to_single_float(w_first)).astype(jnp.bfloat16)
    mixed = first.reshape(element_count, DIAGONAL_BLOCKS, HB, eb_size).transpose(0, 2, 1, 3).reshape(element_count, HB, DIAGONAL_BLOCKS * eb_size)
    pre = jnp.einsum('tck,ckf->tcf', to_single_float(mixed), to_single_float(w_second))
    act = gelu_value(pre).astype(jnp.bfloat16)
    third = jnp.einsum('tcf,cfm->tcm', to_single_float(act), to_single_float(w_third)).astype(jnp.bfloat16)
    gathered = third.reshape(element_count, HB, DIAGONAL_BLOCKS, eb_size).transpose(0, 2, 1, 3).reshape(element_count, DIAGONAL_BLOCKS, HB * eb_size)
    branch = jnp.einsum('tak,ako->tao', to_single_float(gathered), to_single_float(w_fourth)).reshape(element_count, MODEL_WIDTH)
    output = (complete_input + branch).astype(jnp.bfloat16)
    dy_blocks = output_gradient_block.reshape(element_count, DIAGONAL_BLOCKS, MODEL_WIDTH // DIAGONAL_BLOCKS)
    grad_fourth = jnp.einsum('tak,tao->ako', to_single_float(gathered), to_single_float(dy_blocks))
    dgathered = jnp.einsum('tao,ako->tak', to_single_float(dy_blocks), to_single_float(w_fourth)).astype(jnp.bfloat16)
    dthird = dgathered.reshape(element_count, DIAGONAL_BLOCKS, HB, eb_size).transpose(0, 2, 1, 3).reshape(element_count, HB, DIAGONAL_BLOCKS * eb_size)
    grad_third = jnp.einsum('tcf,tcm->cfm', to_single_float(act), to_single_float(dthird))
    dact = jnp.einsum('tcm,cfm->tcf', to_single_float(dthird), to_single_float(w_third))
    dpre = (dact * gelu_slope(pre)).astype(jnp.bfloat16)
    grad_second = jnp.einsum('tck,tcf->ckf', to_single_float(mixed), to_single_float(dpre))
    dmixed = jnp.einsum('tcf,ckf->tck', to_single_float(dpre), to_single_float(w_second)).astype(jnp.bfloat16)
    dfirst = dmixed.reshape(element_count, HB, DIAGONAL_BLOCKS, eb_size).transpose(0, 2, 1, 3).reshape(element_count, DIAGONAL_BLOCKS, HB * eb_size)
    grad_first = jnp.einsum('tak,tah->akh', to_single_float(normalized_input), to_single_float(dfirst))
    dnormed = jnp.einsum('tah,akh->tak', to_single_float(dfirst), to_single_float(w_first)).reshape(element_count, MODEL_WIDTH)
    scaled_normalized = dnormed * gain
    inner_product = lax.optimization_barrier(jnp.mean(scaled_normalized * centered_input, axis=1, keepdims=True))
    token_gradient = (to_single_float(output_gradient_block) + reciprocal_norm * (scaled_normalized - centered_input * inner_product)).astype(jnp.bfloat16)
    return (output, token_gradient, grad_first, grad_second, grad_third, grad_fourth)

def reference(tokens, gain, w_first, w_second, w_third, w_fourth, cotangent):
    x_blocks = tokens.reshape(N_DP, TOK_DEV, MODEL_WIDTH)
    dy_blocks = cotangent.reshape(N_DP, TOK_DEV, MODEL_WIDTH)
    start = (jnp.zeros(w_first.shape, jnp.float32), jnp.zeros(w_second.shape, jnp.float32), jnp.zeros(w_third.shape, jnp.float32), jnp.zeros(w_fourth.shape, jnp.float32))

    def step_fn(carry, pair):
        output, token_gradient, one, two, three, four = layer_block(pair[0], pair[1], gain, w_first, w_second, w_third, w_fourth)
        return ((carry[0] + one, carry[1] + two, carry[2] + three, carry[3] + four), (output, token_gradient))
    totals, stacked = lax.scan(step_fn, start, (x_blocks, dy_blocks))
    scale = 1.0 / math.sqrt(TOKENS)
    return (stacked[0].reshape(TOKENS, MODEL_WIDTH), stacked[1].reshape(TOKENS, MODEL_WIDTH), totals[0] * scale, totals[1] * scale, totals[2] * scale, totals[3] * scale)
```

```python
import math

import jax
import jax.numpy as jnp
from jax import lax
from jax.experimental import pallas as pl
from jax.experimental.pallas import tpu as pltpu
from jax.sharding import PartitionSpec as P

MODEL_WIDTH = 8192
DIAGONAL_BLOCKS = 32
HBS = 1024
HB = 16
BS = 256
EB = 32
PEERS = 16
PAIR = 2 * EB
LANES = 128
STATS = 16

epsilon = 1e-05
root_scale = math.sqrt(2.0 / math.pi)
cubic_term = 0.044715

F32 = jnp.float32
BF16 = jnp.bfloat16

NN = (((1,), (0,)), ((), ()))
NT = (((1,), (1,)), ((), ()))
TN = (((0,), (0,)), ((), ()))
TT = (((0,), (1,)), ((), ()))


def dot(a, b, dims):
    return lax.dot_general(a, b, dims, preferred_element_type=F32)


def call(kernel, out_shape, args, scratch=(), flops=0, **extra):
    outs = out_shape if isinstance(out_shape, (list, tuple)) else [out_shape]
    moved = sum(a.size * a.dtype.itemsize for a in args) + sum(
        math.prod(o.shape) * o.dtype.itemsize for o in outs
    )
    return pl.pallas_call(
        kernel,
        out_shape=out_shape,
        in_specs=[pl.BlockSpec(memory_space=pltpu.VMEM)] * len(args),
        out_specs=jax.tree.map(lambda _: pl.BlockSpec(memory_space=pltpu.VMEM), out_shape),
        scratch_shapes=list(scratch),
        compiler_params=pltpu.CompilerParams(vmem_limit_bytes=48 * 1024 * 1024),
        cost_estimate=pl.CostEstimate(flops=int(flops), bytes_accessed=int(moved), transcendentals=0),
        **extra,
    )(*args)


def stat_rows(value, chunks):
    high = value.astype(BF16).astype(F32)
    low = value - high
    rows = []
    for i in range(chunks):
        part = slice(i * LANES, (i + 1) * LANES)
        rows += [high[:, part], low[:, part]]
    rows.append(jnp.zeros((STATS - 2 * chunks, LANES), F32))
    return jnp.concatenate(rows, axis=0).astype(BF16)


def stat_sum(rows):
    return jnp.sum(rows.astype(F32), axis=0)


def head_kernel(x_ref, gain_ref, w1_ref, w4_ref, cot_ref, out_ref):
    tokens = x_ref.shape[0]
    chunks = tokens // LANES
    for a in range(2):
        feats = slice(a * BS, (a + 1) * BS)
        scaled = (x_ref[:, feats].astype(F32) * gain_ref[:, feats]).astype(BF16)
        first = dot(w1_ref[a].T, scaled, NT).astype(BF16)
        dgathered = dot(w4_ref[a], cot_ref[:, feats], NT).astype(BF16)
        for i in range(chunks):
            part = slice(i * LANES, (i + 1) * LANES)
            base = i * 2 * PAIR + a * EB
            out_ref[:, base : base + EB, :] = first[:, part].reshape(PEERS, EB, LANES)
            base += PAIR
            out_ref[:, base : base + EB, :] = dgathered[:, part].reshape(PEERS, EB, LANES)
    x = x_ref[...].astype(F32)
    squares = x * x
    width = squares.shape[1]
    folded = squares[:, :LANES]
    for i in range(1, width // LANES):
        folded = folded + squares[:, i * LANES : (i + 1) * LANES]
    total = jnp.sum(folded.T, axis=0, keepdims=True)
    rows = stat_rows(total, chunks)
    out_ref[:, chunks * 2 * PAIR :, :] = jnp.broadcast_to(rows[None], (PEERS, STATS, LANES))


def reciprocals(stats, chunks):
    rows = [stats[2 * i : 2 * i + 1] + stats[2 * i + 1 : 2 * i + 2] for i in range(chunks)]
    return lax.rsqrt(jnp.concatenate(rows, axis=1) / MODEL_WIDTH + epsilon)


def hidden_rows(ref, chunk, offset, stride):
    start = chunk * stride + offset
    return ref[:, start : start + PAIR, :].reshape(HBS, LANES)


def turn_kernel(w2_ref, w3_ref, w2t_ref, w3t_ref):
    w2t_ref[...] = w2_ref[0].T
    w3t_ref[...] = w3_ref[0].T


def forward_kernel(recv_ref, w2t_ref, w3t_ref, pre_ref, act_ref, out_ref):
    chunks = (recv_ref.shape[1] - STATS) // (2 * PAIR)
    stats = stat_sum(recv_ref[:, chunks * 2 * PAIR :, :])
    inverse = reciprocals(stats, chunks)
    for i in range(0, chunks, 2):
        part = slice(i * LANES, (i + 2) * LANES)
        mixed = jnp.concatenate([hidden_rows(recv_ref, i + k, 0, 2 * PAIR) for k in range(2)], axis=1)
        pre = dot(w2t_ref[...], mixed, NN) * inverse[:, part]
        pre_ref[:, part] = pre
        hyper = jnp.tanh(root_scale * (pre + cubic_term * pre * pre * pre))
        act = (0.5 * pre * (1.0 + hyper)).astype(BF16)
        act_ref[:, part] = act
        third = dot(w3t_ref[...], act, NN).astype(BF16)
        for k in range(2):
            rows = slice((i + k) * PAIR, (i + k + 1) * PAIR)
            out_ref[:, rows, :] = third[:, k * LANES : (k + 1) * LANES].reshape(PEERS, PAIR, LANES)


def backward_kernel(recv_ref, pre_ref, w2_ref, w3_ref, dpre_ref, out_ref):
    chunks = (recv_ref.shape[1] - STATS) // (2 * PAIR)
    stats = stat_sum(recv_ref[:, chunks * 2 * PAIR :, :])
    inverse = reciprocals(stats, chunks)
    inner = []
    for i in range(0, chunks, 2):
        part = slice(i * LANES, (i + 2) * LANES)
        dthird = jnp.concatenate([hidden_rows(recv_ref, i + k, PAIR, 2 * PAIR) for k in range(2)], axis=1)
        dact = dot(w3_ref[0], dthird, NN)
        pre = pre_ref[:, part]
        hyper = jnp.tanh(root_scale * (pre + cubic_term * pre * pre * pre))
        slope = 0.5 * (1.0 + hyper) + 0.5 * pre * (1.0 - hyper * hyper) * root_scale * (
            1.0 + 3.0 * cubic_term * pre * pre
        )
        dpre = dact * slope
        inner.append(jnp.sum(dpre * pre, axis=0, keepdims=True))
        dpre_ref[:, part] = (dpre * inverse[:, part]).astype(BF16)
        dmixed = dot(w2_ref[0], dpre.astype(BF16), NN).astype(BF16)
        for k in range(2):
            rows = slice((i + k) * PAIR, (i + k + 1) * PAIR)
            out_ref[:, rows, :] = dmixed[:, k * LANES : (k + 1) * LANES].reshape(PEERS, PAIR, LANES)
    rows = stat_rows(jnp.concatenate(inner, axis=1), chunks)
    out_ref[:, chunks * PAIR :, :] = jnp.broadcast_to(rows[None], (PEERS, STATS, LANES))


def hidden_grads_kernel(recv_ref, act_ref, dpre_ref, out_ref):
    chunks = (recv_ref.shape[1] - STATS) // (2 * PAIR)
    mixed = jnp.concatenate([hidden_rows(recv_ref, i, 0, 2 * PAIR) for i in range(chunks)], axis=1)
    dthird = jnp.concatenate([hidden_rows(recv_ref, i, PAIR, 2 * PAIR) for i in range(chunks)], axis=1)
    z_size, y_size, rows, _ = out_ref.shape
    half = z_size // 2
    step = half * rows
    for i in range(2 * y_size):
        part = slice(i * step, (i + 1) * step)
        z = slice((i % 2) * half, (i % 2 + 1) * half)
        second = dot(mixed[part], dpre_ref[...], NT).astype(BF16)
        out_ref[z, i // 2, :, :HBS] = second.reshape(half, rows, HBS)
        third = dot(act_ref[part, :], dthird, NT).astype(BF16)
        out_ref[z, i // 2, :, HBS:] = third.reshape(half, rows, HBS)


def model_rows(ref, chunks, a, stride):
    parts = []
    for i in range(chunks):
        start = i * stride + a * EB
        parts.append(ref[:, start : start + EB, :].reshape(HB * EB, LANES))
    return jnp.concatenate(parts, axis=1)


def columns(stats, chunks):
    turned = stats.T
    parts = [turned[:, 2 * i : 2 * i + 1] + turned[:, 2 * i + 1 : 2 * i + 2] for i in range(chunks)]
    return jnp.concatenate(parts, axis=0)


def norm_kernel(x_ref, gain_ref, stats_ref, normed_ref):
    chunks = x_ref.shape[0] // LANES
    inverse = lax.rsqrt(columns(stat_sum(stats_ref[...]), chunks) / MODEL_WIDTH + epsilon)
    normed_ref[...] = (x_ref[...].astype(F32) * inverse * gain_ref[...]).astype(BF16)


def output_kernel(recv_ref, x_ref, w4_ref, out_ref):
    chunks = x_ref.shape[0] // LANES
    for a in range(2):
        feats = slice(a * BS, (a + 1) * BS)
        gathered = model_rows(recv_ref, chunks, a, PAIR)
        branch = dot(gathered, w4_ref[a], TN)
        out_ref[:, feats] = (x_ref[:, feats].astype(F32) + branch).astype(BF16)


def grad_fourth_kernel(recv_ref, cot_ref, out_ref):
    chunks = cot_ref.shape[0] // LANES
    for a in range(2):
        gathered = model_rows(recv_ref, chunks, a, PAIR)
        grad = dot(gathered, cot_ref[:, a * BS : (a + 1) * BS], NN).astype(BF16)
        out_ref[:, a, :, :] = grad.reshape(PEERS, HB * EB // PEERS, BS)


def grad_first_kernel(recv_ref, normed_ref, out_ref):
    chunks = normed_ref.shape[0] // LANES
    for a in range(2):
        dfirst = model_rows(recv_ref, chunks, a, PAIR)
        grad = dot(dfirst, normed_ref[:, a * BS : (a + 1) * BS], NN).astype(BF16)
        out_ref[:, a, :, :] = grad.T.reshape(PEERS, BS // PEERS, HB * EB)


def token_kernel(recv_ref, squares_ref, x_ref, gain_ref, w1_ref, cot_ref, out_ref):
    chunks = x_ref.shape[0] // LANES
    inverse = lax.rsqrt(columns(stat_sum(squares_ref[...]), chunks) / MODEL_WIDTH + epsilon)
    inner = columns(stat_sum(recv_ref[:, chunks * PAIR :, :]), chunks) / MODEL_WIDTH
    for a in range(2):
        feats = slice(a * BS, (a + 1) * BS)
        dfirst = model_rows(recv_ref, chunks, a, PAIR)
        dnormed = dot(dfirst, w1_ref[a], TT)
        xhat = x_ref[:, feats].astype(F32) * inverse
        change = dnormed * gain_ref[:, feats] - xhat * inner
        out_ref[:, feats] = (cot_ref[:, feats].astype(F32) + inverse * change).astype(BF16)


def shards(tokens, gain, w_first, w_second, w_third, w_fourth, cotangent):
    element_count, local_width = tokens.shape
    dp = lax.axis_size("dp")
    scale = 1.0 / math.sqrt(element_count * dp)
    chunks = element_count // LANES
    gain_row = gain[None, :]
    z_size = dp // 2
    z_groups = [[y * z_size + z for z in range(z_size)] for y in range(2)]
    y_index = lax.axis_index("dp") // z_size
    shape = jax.ShapeDtypeStruct
    hidden_flops = 2 * HBS * HBS * element_count
    model_flops = 2 * local_width * HB * EB * element_count

    def exchange(value, axis):
        return lax.all_to_all(value, axis, 0, 0, tiled=True)

    send = call(
        head_kernel,
        shape((PEERS, chunks * 2 * PAIR + STATS, LANES), BF16),
        (tokens, gain_row, w_first, w_fourth, cotangent),
        flops=2 * model_flops,
    )
    recv = exchange(send, "tensor")
    turned = shape((HBS, HBS), BF16)
    w_second_t, w_third_t = call(turn_kernel, [turned, turned], (w_second, w_third))
    pre, act, send = call(
        forward_kernel,
        [
            shape((HBS, element_count), F32),
            shape((HBS, element_count), BF16),
            shape((PEERS, chunks * PAIR, LANES), BF16),
        ],
        (recv, w_second_t, w_third_t),
        flops=2 * hidden_flops,
    )
    third = exchange(send, "tensor")
    dpre, send = call(
        backward_kernel,
        [shape((HBS, element_count), BF16), shape((PEERS, chunks * PAIR + STATS, LANES), BF16)],
        (recv, pre, w_second, w_third),
        flops=2 * hidden_flops,
    )
    hidden = call(
        hidden_grads_kernel,
        shape((z_size, 2, HBS // dp, 2 * HBS), BF16),
        (recv, act, dpre),
        flops=2 * hidden_flops,
    )
    hidden = lax.psum_scatter(hidden, "dp", scatter_dimension=0, axis_index_groups=z_groups, tiled=True)[0]
    back = exchange(send, "tensor")

    squares = recv[:, chunks * 2 * PAIR :, :]
    normed = call(norm_kernel, shape(tokens.shape, BF16), (tokens, gain_row, squares))
    output = call(output_kernel, shape(tokens.shape, BF16), (third, tokens, w_fourth), flops=model_flops)
    fourth = call(
        grad_fourth_kernel,
        shape((PEERS, 2, HB * EB // PEERS, BS), BF16),
        (third, cotangent),
        flops=model_flops,
    )
    first = call(
        grad_first_kernel,
        shape((PEERS, 2, BS // PEERS, HB * EB), BF16),
        (back, normed),
        flops=model_flops,
    )
    fourth = exchange(fourth, "dp")
    first = exchange(first, "dp")
    token_gradient = call(
        token_kernel,
        shape(tokens.shape, BF16),
        (back, squares, tokens, gain_row, w_first, cotangent),
        flops=model_flops,
    )
    grad_first = (jnp.sum(first.astype(F32), axis=0)) * scale
    grad_fourth = (jnp.sum(fourth.astype(F32), axis=0)) * scale

    other = lax.ppermute(
        lax.dynamic_index_in_dim(hidden, 1 - y_index, 0, keepdims=False),
        "dp",
        [(i, (i + z_size) % dp) for i in range(dp)],
    )
    own = lax.dynamic_index_in_dim(hidden, y_index, 0, keepdims=False)
    hidden = (own.astype(F32) + other.astype(F32)) * scale
    return (
        output,
        token_gradient,
        grad_first,
        hidden[None, :, :HBS],
        hidden[None, :, HBS:],
        grad_fourth,
    )


def solution(mesh):
    return jax.shard_map(
        shards,
        mesh=mesh,
        in_specs=(
            P("dp", "tensor"),
            P("tensor"),
            P("tensor", None, None),
            P("tensor", None, None),
            P("tensor", None, None),
            P("tensor", None, None),
            P("dp", "tensor"),
        ),
        out_specs=(
            P("dp", "tensor"),
            P("dp", "tensor"),
            P("tensor", "dp", None),
            P("tensor", "dp", None),
            P("tensor", "dp", None),
            P("tensor", "dp", None),
        ),
        check_vma=False,
    )
```

```python
import functools
import math

import jax
import jax.numpy as jnp
from jax import lax
from jax.experimental import pallas as pl
from jax.experimental.pallas import tpu as pltpu
from jax.sharding import PartitionSpec as P

MODEL_WIDTH = 8192
DIAGONAL_BLOCKS = 32
HBS = 1024
HB = 16
BS = 256
EB = 32
PEERS = 16
PAIR = 2 * EB
LANES = 128
STATS = 16
LATE = 1000
VMEM = 58 * 1024 * 1024

epsilon = 1e-05
root_scale = math.sqrt(2.0 / math.pi)
cubic_term = 0.044715

F32 = jnp.float32
BF16 = jnp.bfloat16

NN = (((1,), (0,)), ((), ()))
NT = (((1,), (1,)), ((), ()))
TN = (((0,), (0,)), ((), ()))
TT = (((0,), (1,)), ((), ()))


def dot(a, b, dims):
    return lax.dot_general(a, b, dims, preferred_element_type=F32)


def call(kernel, out_shape, args, scratch=(), flops=0, **extra):
    outs = out_shape if isinstance(out_shape, (list, tuple)) else [out_shape]
    moved = sum(a.size * a.dtype.itemsize for a in args) + sum(
        math.prod(o.shape) * o.dtype.itemsize for o in outs
    )
    return pl.pallas_call(
        kernel,
        out_shape=out_shape,
        in_specs=[pl.BlockSpec(memory_space=pltpu.VMEM)] * len(args),
        out_specs=jax.tree.map(lambda _: pl.BlockSpec(memory_space=pltpu.VMEM), out_shape),
        scratch_shapes=list(scratch),
        compiler_params=pltpu.CompilerParams(vmem_limit_bytes=VMEM),
        cost_estimate=pl.CostEstimate(flops=int(flops), bytes_accessed=int(moved), transcendentals=0),
        **extra,
    )(*args)


def stat_rows(value, chunks):
    high = value.astype(BF16).astype(F32)
    low = value - high
    rows = []
    for i in range(chunks):
        part = slice(i * LANES, (i + 1) * LANES)
        rows += [high[:, part], low[:, part]]
    rows.append(jnp.zeros((STATS - 2 * chunks, LANES), F32))
    return jnp.concatenate(rows, axis=0).astype(BF16)


def stat_sum(rows):
    return jnp.sum(rows.astype(F32), axis=0)


def first_kernel(x_ref, gain_ref, w1_ref, out_ref, squares_ref):
    a = pl.program_id(0)
    chunks = x_ref.shape[0] // LANES
    x = x_ref[...].astype(F32)
    first = dot(w1_ref[0].T, (x * gain_ref[...]).astype(BF16), NT).astype(BF16)
    base = pl.multiple_of(a * EB, EB)
    for i in range(chunks):
        part = slice(i * LANES, (i + 1) * LANES)
        out_ref[:, pl.ds(i * PAIR + base, EB), :] = first[:, part].reshape(PEERS, EB, LANES)
    squares = x * x
    total = jnp.sum((squares[:, :LANES] + squares[:, LANES:]).T, axis=0, keepdims=True)

    @pl.when(a == 0)
    def _():
        squares_ref[...] = total

    @pl.when(a == 1)
    def _():
        rows = stat_rows(squares_ref[...] + total, chunks)
        out_ref[:, chunks * PAIR :, :] = jnp.broadcast_to(rows[None], (PEERS, STATS, LANES))


def dgathered_kernel(w4_ref, cot_ref, out_ref):
    chunks = cot_ref.shape[0] // LANES
    for a in range(2):
        dgathered = dot(w4_ref[a], cot_ref[:, a * BS : (a + 1) * BS], NT).astype(BF16)
        for i in range(chunks):
            part = slice(i * LANES, (i + 1) * LANES)
            base = i * PAIR + a * EB
            out_ref[:, base : base + EB, :] = dgathered[:, part].reshape(PEERS, EB, LANES)


def reciprocals(stats, chunks):
    rows = [stats[2 * i : 2 * i + 1] + stats[2 * i + 1 : 2 * i + 2] for i in range(chunks)]
    return lax.rsqrt(jnp.concatenate(rows, axis=1) / MODEL_WIDTH + epsilon)


def hidden_rows(ref, first, last):
    parts = [ref[:, i * PAIR : (i + 1) * PAIR, :].reshape(HBS, LANES) for i in range(first, last)]
    return jnp.concatenate(parts, axis=1)


def store_rows(ref, value, first):
    for k in range(value.shape[1] // LANES):
        rows = slice((first + k) * PAIR, (first + k + 1) * PAIR)
        ref[:, rows, :] = value[:, k * LANES : (k + 1) * LANES].reshape(PEERS, PAIR, LANES)


def turn_kernel(w2_ref, w3_ref, w2t_ref, w3t_ref):
    w2t_ref[...] = w2_ref[0].T
    w3t_ref[...] = w3_ref[0].T


def forward_kernel(recv_ref, w2t_ref, w3t_ref, pre_ref, act_ref, out_ref):
    chunks = (recv_ref.shape[1] - STATS) // PAIR
    inverse = reciprocals(stat_sum(recv_ref[:, chunks * PAIR :, :]), chunks)
    for i in range(0, chunks, 2):
        part = slice(i * LANES, (i + 2) * LANES)
        pre = dot(w2t_ref[...], hidden_rows(recv_ref, i, i + 2), NN) * inverse[:, part]
        pre_ref[:, part] = pre
        hyper = jnp.tanh(root_scale * (pre + cubic_term * pre * pre * pre))
        act = (0.5 * pre * (1.0 + hyper)).astype(BF16)
        act_ref[:, part] = act
        store_rows(out_ref, dot(w3t_ref[...], act, NN).astype(BF16), i)


def backward_kernel(recv_ref, stats_ref, pre_ref, w2_ref, w3_ref, scaled_ref, out_ref):
    chunks = recv_ref.shape[1] // PAIR
    inverse = reciprocals(stat_sum(stats_ref[...]), chunks)
    inner = []
    for i in range(0, chunks, 2):
        part = slice(i * LANES, (i + 2) * LANES)
        dact = dot(w3_ref[0], hidden_rows(recv_ref, i, i + 2), NN)
        pre = pre_ref[:, part]
        hyper = jnp.tanh(root_scale * (pre + cubic_term * pre * pre * pre))
        slope = 0.5 * (1.0 + hyper) + 0.5 * pre * (1.0 - hyper * hyper) * root_scale * (
            1.0 + 3.0 * cubic_term * pre * pre
        )
        dpre = dact * slope
        inner.append(jnp.sum(dpre * pre, axis=0, keepdims=True))
        scaled_ref[:, part] = (dpre * inverse[:, part]).astype(BF16)
        store_rows(out_ref, dot(w2_ref[0], dpre.astype(BF16), NN).astype(BF16), i)
    rows = stat_rows(jnp.concatenate(inner, axis=1), chunks)
    out_ref[:, chunks * PAIR :, :] = jnp.broadcast_to(rows[None], (PEERS, STATS, LANES))


def hidden_grads_kernel(recv_ref, dthird_ref, act_ref, scaled_ref, out_ref):
    chunks = dthird_ref.shape[1] // PAIR
    mixed = hidden_rows(recv_ref, 0, chunks)
    dthird = hidden_rows(dthird_ref, 0, chunks)
    z_size, y_size, rows, _ = out_ref.shape
    half = z_size // 2
    step = half * rows
    for i in range(2 * y_size):
        part = slice(i * step, (i + 1) * step)
        z = slice((i % 2) * half, (i % 2 + 1) * half)
        second = dot(mixed[part], scaled_ref[...], NT).astype(BF16)
        out_ref[z, i // 2, :, :HBS] = second.reshape(half, rows, HBS)
        third = dot(act_ref[part, :], dthird, NT).astype(BF16)
        out_ref[z, i // 2, :, HBS:] = third.reshape(half, rows, HBS)


def model_rows(ref, chunks, a, stride):
    parts = []
    for i in range(chunks):
        start = i * stride + a * EB
        parts.append(ref[:, start : start + EB, :].reshape(HB * EB, LANES))
    return jnp.concatenate(parts, axis=1)


def columns(stats, chunks):
    turned = stats.T
    parts = [turned[:, 2 * i : 2 * i + 1] + turned[:, 2 * i + 1 : 2 * i + 2] for i in range(chunks)]
    return jnp.concatenate(parts, axis=0)


def norm_kernel(x_ref, gain_ref, stats_ref, normed_ref):
    chunks = x_ref.shape[0] // LANES
    inverse = lax.rsqrt(columns(stat_sum(stats_ref[...]), chunks) / MODEL_WIDTH + epsilon)
    normed_ref[...] = (x_ref[...].astype(F32) * inverse * gain_ref[...]).astype(BF16)


def output_kernel(recv_ref, x_ref, w4_ref, out_ref):
    chunks = x_ref.shape[0] // LANES
    for a in range(2):
        feats = slice(a * BS, (a + 1) * BS)
        gathered = model_rows(recv_ref, chunks, a, PAIR)
        branch = dot(gathered, w4_ref[a], TN)
        out_ref[:, feats] = (x_ref[:, feats].astype(F32) + branch).astype(BF16)


def grad_fourth_kernel(recv_ref, cot_ref, out_ref):
    chunks = cot_ref.shape[0] // LANES
    rows = HB * EB // PEERS
    for a in range(2):
        gathered = model_rows(recv_ref, chunks, a, PAIR)
        grad = dot(gathered, cot_ref[:, a * BS : (a + 1) * BS], NN).astype(BF16)
        out_ref[:, a * rows : (a + 1) * rows, :] = grad.reshape(PEERS, rows, BS)


def grad_first_kernel(recv_ref, normed_ref, fourth_ref, out_ref):
    chunks = normed_ref.shape[0] // LANES
    rows = BS // PEERS
    for a in range(2):
        dfirst = model_rows(recv_ref, chunks, a, PAIR)
        grad = dot(dfirst, normed_ref[:, a * BS : (a + 1) * BS], NN).astype(BF16).T
        for half in range(2):
            base = (2 * a + half) * rows
            part = grad[:, half * BS : (half + 1) * BS]
            out_ref[:, base : base + rows, :] = part.reshape(PEERS, rows, BS)
    out_ref[:, 4 * rows :, :] = fourth_ref[...]


def sum_kernel(scale, recv_ref, first_ref, fourth_ref):
    total = jnp.sum(recv_ref[...].astype(F32), axis=0) * scale
    _, rows, _ = first_ref.shape
    for a in range(2):
        for half in range(2):
            base = (2 * a + half) * rows
            first_ref[a, :, half * BS : (half + 1) * BS] = total[base : base + rows]
    fourth_ref[...] = total[4 * rows :].reshape(fourth_ref.shape)


def finish_kernel(scale, own_ref, other_ref, second_ref, third_ref):
    total = (own_ref[...].astype(F32) + other_ref[...].astype(F32)) * scale
    second_ref[0] = total[:, :HBS]
    third_ref[0] = total[:, HBS:]


def token_kernel(recv_ref, squares_ref, x_ref, gain_ref, w1_ref, cot_ref, out_ref):
    chunks = x_ref.shape[0] // LANES
    inverse = lax.rsqrt(columns(stat_sum(squares_ref[...]), chunks) / MODEL_WIDTH + epsilon)
    inner = columns(stat_sum(recv_ref[:, chunks * PAIR :, :]), chunks) / MODEL_WIDTH
    for a in range(2):
        feats = slice(a * BS, (a + 1) * BS)
        dfirst = model_rows(recv_ref, chunks, a, PAIR)
        dnormed = dot(dfirst, w1_ref[a], TT)
        xhat = x_ref[:, feats].astype(F32) * inverse
        change = dnormed * gain_ref[:, feats] - xhat * inner
        out_ref[:, feats] = (cot_ref[:, feats].astype(F32) + inverse * change).astype(BF16)


def shards(tokens, gain, w_first, w_second, w_third, w_fourth, cotangent):
    element_count, local_width = tokens.shape
    dp = lax.axis_size("dp")
    scale = 1.0 / math.sqrt(element_count * dp)
    chunks = element_count // LANES
    gain_row = gain[None, :]
    z_size = dp // 2
    z_groups = [[y * z_size + z for z in range(z_size)] for y in range(2)]
    y_index = lax.axis_index("dp") // z_size
    shape = jax.ShapeDtypeStruct
    hidden_flops = 2 * HBS * HBS * element_count
    model_flops = 2 * local_width * HB * EB * element_count

    def exchange(value, axis):
        return lax.all_to_all(value, axis, 0, 0, tiled=True)

    def after(value, other):
        return lax.optimization_barrier((value, other))[0]

    rows = chunks * PAIR
    send = pl.pallas_call(
        first_kernel,
        out_shape=shape((PEERS, rows + STATS, LANES), BF16),
        grid=(2,),
        in_specs=[
            pl.BlockSpec((element_count, BS), lambda a: (0, a)),
            pl.BlockSpec((1, BS), lambda a: (0, a)),
            pl.BlockSpec((1, BS, HB * EB), lambda a: (a, 0, 0)),
        ],
        out_specs=pl.BlockSpec((PEERS, rows + STATS, LANES), lambda a: (0, 0, 0)),
        scratch_shapes=[pltpu.VMEM((1, element_count), F32)],
        compiler_params=pltpu.CompilerParams(vmem_limit_bytes=VMEM),
    )(tokens, gain_row, w_first)
    first = exchange(send, "tensor")
    send = call(dgathered_kernel, shape((PEERS, rows, LANES), BF16), (w_fourth, cotangent), flops=model_flops)
    dthird = exchange(after(send, first), "tensor")
    turned = shape((HBS, HBS), BF16)
    w_second_t, w_third_t = call(turn_kernel, [turned, turned], (w_second, w_third))
    wide = (HBS, element_count)
    pre, act, send = call(
        forward_kernel,
        [shape(wide, F32), shape(wide, BF16), shape((PEERS, rows, LANES), BF16)],
        (first, w_second_t, w_third_t),
        flops=2 * hidden_flops,
    )
    third = exchange(after(send, dthird), "tensor")
    squares = first[:, rows:, :]
    scaled, send = call(
        backward_kernel,
        [shape(wide, BF16), shape((PEERS, rows + STATS, LANES), BF16)],
        (dthird, squares, pre, w_second, w_third),
        flops=2 * hidden_flops,
    )
    hidden = call(
        hidden_grads_kernel,
        shape((z_size, 2, HBS // dp, 2 * HBS), BF16),
        (first, dthird, act, scaled),
        flops=2 * hidden_flops,
    )
    hidden = lax.psum_scatter(hidden, "dp", scatter_dimension=0, axis_index_groups=z_groups, tiled=True)[0]
    back = exchange(after(send, third), "tensor")

    normed = call(norm_kernel, shape(tokens.shape, BF16), (tokens, gain_row, after(squares, third)))
    output = call(
        output_kernel, shape(tokens.shape, BF16), (third, tokens, w_fourth), flops=LATE * model_flops
    )
    fourth = call(
        grad_fourth_kernel, shape((PEERS, 64, BS), BF16), (third, cotangent), flops=model_flops
    )
    both = call(
        grad_first_kernel, shape((PEERS, 128, BS), BF16), (back, normed, fourth), flops=model_flops
    )
    both = exchange(both, "dp")
    token_gradient = call(
        token_kernel,
        shape(tokens.shape, BF16),
        (back, squares, tokens, gain_row, w_first, cotangent),
        flops=LATE * model_flops,
    )
    grad_first, grad_fourth = call(
        functools.partial(sum_kernel, scale),
        [shape((2, BS // dp, HB * EB), F32), shape((2, HB * EB // dp, BS), F32)],
        (both,),
    )
    other = lax.ppermute(
        lax.dynamic_index_in_dim(hidden, 1 - y_index, 0, keepdims=False),
        "dp",
        [(i, (i + z_size) % dp) for i in range(dp)],
    )
    own = lax.dynamic_index_in_dim(hidden, y_index, 0, keepdims=False)
    part = shape((1, HBS // dp, HBS), F32)
    grad_second, grad_third = call(functools.partial(finish_kernel, scale), [part, part], (own, other))
    return output, token_gradient, grad_first, grad_second, grad_third, grad_fourth


def solution(mesh):
    return jax.shard_map(
        shards,
        mesh=mesh,
        in_specs=(
            P("dp", "tensor"),
            P("tensor"),
            P("tensor", None, None),
            P("tensor", None, None),
            P("tensor", None, None),
            P("tensor", None, None),
            P("dp", "tensor"),
        ),
        out_specs=(
            P("dp", "tensor"),
            P("dp", "tensor"),
            P("tensor", "dp", None),
            P("tensor", "dp", None),
            P("tensor", "dp", None),
            P("tensor", "dp", None),
        ),
        check_vma=False,
    )
```

```python
import functools
import math

import jax
import jax.numpy as jnp
from jax import lax
from jax.experimental import pallas as pl
from jax.experimental.pallas import tpu as pltpu
from jax.sharding import PartitionSpec as P

MODEL_WIDTH = 8192
DIAGONAL_BLOCKS = 32
HBS = 1024
HB = 16
BS = 256
EB = 32
PEERS = 16
PAIR = 2 * EB
LANES = 128
STATS = 16
LATE = 1000
VMEM = 58 * 1024 * 1024

epsilon = 1e-05
root_scale = math.sqrt(2.0 / math.pi)
cubic_term = 0.044715

F32 = jnp.float32
BF16 = jnp.bfloat16

NN = (((1,), (0,)), ((), ()))
NT = (((1,), (1,)), ((), ()))
TN = (((0,), (0,)), ((), ()))
TT = (((0,), (1,)), ((), ()))


def dot(a, b, dims):
    return lax.dot_general(a, b, dims, preferred_element_type=F32)


def call(kernel, out_shape, args, scratch=(), flops=0, **extra):
    outs = out_shape if isinstance(out_shape, (list, tuple)) else [out_shape]
    moved = sum(a.size * a.dtype.itemsize for a in args) + sum(
        math.prod(o.shape) * o.dtype.itemsize for o in outs
    )
    return pl.pallas_call(
        kernel,
        out_shape=out_shape,
        in_specs=[pl.BlockSpec(memory_space=pltpu.VMEM)] * len(args),
        out_specs=jax.tree.map(lambda _: pl.BlockSpec(memory_space=pltpu.VMEM), out_shape),
        scratch_shapes=list(scratch),
        compiler_params=pltpu.CompilerParams(vmem_limit_bytes=VMEM),
        cost_estimate=pl.CostEstimate(flops=int(flops), bytes_accessed=int(moved), transcendentals=0),
        **extra,
    )(*args)


def stat_rows(value, chunks):
    high = value.astype(BF16).astype(F32)
    low = value - high
    rows = []
    for i in range(chunks):
        part = slice(i * LANES, (i + 1) * LANES)
        rows += [high[:, part], low[:, part]]
    rows.append(jnp.zeros((STATS - 2 * chunks, LANES), F32))
    return jnp.concatenate(rows, axis=0).astype(BF16)


def stat_sum(rows):
    return jnp.sum(rows.astype(F32), axis=0)


def head_kernel(x_ref, gain_ref, w1_ref, w4_ref, cot_ref, out_ref, squares_ref):
    a = pl.program_id(0)
    chunks = x_ref.shape[0] // LANES
    x = x_ref[...].astype(F32)
    first = dot(w1_ref[0].T, (x * gain_ref[...]).astype(BF16), NT).astype(BF16)
    dgathered = dot(w4_ref[0], cot_ref[...], NT).astype(BF16)
    base = pl.multiple_of(a * EB, EB)
    for i in range(chunks):
        part = slice(i * LANES, (i + 1) * LANES)
        out_ref[:, pl.ds(i * PAIR + base, EB), :] = first[:, part].reshape(PEERS, EB, LANES)
        out_ref[:, pl.ds((chunks + i) * PAIR + base, EB), :] = dgathered[:, part].reshape(PEERS, EB, LANES)
    squares = x * x
    total = jnp.sum((squares[:, :LANES] + squares[:, LANES:]).T, axis=0, keepdims=True)

    @pl.when(a == 0)
    def _():
        squares_ref[...] = total

    @pl.when(a == 1)
    def _():
        rows = stat_rows(squares_ref[...] + total, chunks)
        out_ref[:, 2 * chunks * PAIR :, :] = jnp.broadcast_to(rows[None], (PEERS, STATS, LANES))


def reciprocal(stats, i):
    rows = stats[pl.ds(4 * i, 4), :]
    total = jnp.concatenate([rows[0:1] + rows[1:2], rows[2:3] + rows[3:4]], axis=1)
    return lax.rsqrt(total / MODEL_WIDTH + epsilon)


def hidden_rows(ref):
    sources, rows, _ = ref.shape
    parts = [
        ref[:, i * PAIR : (i + 1) * PAIR, :].reshape(sources * PAIR, LANES) for i in range(rows // PAIR)
    ]
    return jnp.concatenate(parts, axis=1)


def turn_kernel(w2_ref, w3_ref, w2t_ref, w3t_ref):
    w2t_ref[...] = w2_ref[0].T
    w3t_ref[...] = w3_ref[0].T


def by_peer(value):
    parts = [value[:, k * LANES : (k + 1) * LANES].reshape(PEERS, PAIR, LANES) for k in range(2)]
    return jnp.concatenate(parts, axis=1)


def forward_kernel(recv_ref, stats_ref, w2t_ref, w3t_ref, pre_ref, act_ref, out_ref, total_ref):
    i = pl.program_id(0)

    @pl.when(i == 0)
    def _():
        total_ref[...] = stat_sum(stats_ref[...])

    pre = dot(w2t_ref[...], hidden_rows(recv_ref), NN) * reciprocal(total_ref, i)
    pre_ref[...] = pre
    hyper = jnp.tanh(root_scale * (pre + cubic_term * pre * pre * pre))
    act = (0.5 * pre * (1.0 + hyper)).astype(BF16)
    act_ref[...] = act
    out_ref[...] = by_peer(dot(w3t_ref[...], act, NN).astype(BF16))


def backward_kernel(recv_ref, stats_ref, pre_ref, w2_ref, w3_ref, scaled_ref, out_ref, total_ref, inner_ref):
    i = pl.program_id(0)
    steps = pl.num_programs(0)

    @pl.when(i == 0)
    def _():
        total_ref[...] = stat_sum(stats_ref[...])
        inner_ref[...] = jnp.zeros_like(inner_ref)

    dact = dot(w3_ref[0], hidden_rows(recv_ref), NN)
    pre = pre_ref[...]
    hyper = jnp.tanh(root_scale * (pre + cubic_term * pre * pre * pre))
    slope = 0.5 * (1.0 + hyper) + 0.5 * pre * (1.0 - hyper * hyper) * root_scale * (
        1.0 + 3.0 * cubic_term * pre * pre
    )
    dpre = dact * slope
    inner = jnp.sum(dpre * pre, axis=0, keepdims=True)
    scaled_ref[...] = (dpre * reciprocal(total_ref, i)).astype(BF16)
    dmixed = dot(w2_ref[0], dpre.astype(BF16), NN).astype(BF16)
    out_ref[:, pl.ds(pl.multiple_of(i * 2 * PAIR, 2 * PAIR), 2 * PAIR), :] = by_peer(dmixed)
    high = inner.astype(BF16).astype(F32)
    low = inner - high
    rows = [high[:, :LANES], low[:, :LANES], high[:, LANES:], low[:, LANES:]]
    inner_ref[pl.ds(4 * i, 4), :] = jnp.concatenate(rows, axis=0)

    @pl.when(i == steps - 1)
    def _():
        stats = jnp.broadcast_to(inner_ref[...].astype(BF16)[None], (PEERS, STATS, LANES))
        out_ref[:, out_ref.shape[1] - STATS :, :] = stats


def hidden_grads_kernel(y_ref, mixed_ref, dthird_ref, act_ref, scaled_ref, out_ref, turned_ref):
    del y_ref

    @pl.when(pl.program_id(0) == 0)
    def _():
        turned_ref[...] = hidden_rows(dthird_ref)

    shape = (out_ref.shape[0], out_ref.shape[2], HBS)
    second = dot(hidden_rows(mixed_ref), scaled_ref[...], NT).astype(BF16)
    out_ref[:, 0, :, :HBS] = second.reshape(shape)
    third = dot(act_ref[...], turned_ref[...], NT).astype(BF16)
    out_ref[:, 0, :, HBS:] = third.reshape(shape)


def model_rows(ref, chunks, a, stride):
    parts = []
    for i in range(chunks):
        start = i * stride + a * EB
        parts.append(ref[:, start : start + EB, :].reshape(HB * EB, LANES))
    return jnp.concatenate(parts, axis=1)


def columns(stats, chunks):
    turned = stats.T
    parts = [turned[:, 2 * i : 2 * i + 1] + turned[:, 2 * i + 1 : 2 * i + 2] for i in range(chunks)]
    return jnp.concatenate(parts, axis=0)


def norm_kernel(x_ref, gain_ref, stats_ref, normed_ref):
    chunks = x_ref.shape[0] // LANES
    inverse = lax.rsqrt(columns(stat_sum(stats_ref[...]), chunks) / MODEL_WIDTH + epsilon)
    normed_ref[...] = (x_ref[...].astype(F32) * inverse * gain_ref[...]).astype(BF16)


def output_kernel(recv_ref, x_ref, w4_ref, out_ref):
    chunks = x_ref.shape[0] // LANES
    for a in range(2):
        feats = slice(a * BS, (a + 1) * BS)
        gathered = model_rows(recv_ref, chunks, a, PAIR)
        branch = dot(gathered, w4_ref[a], TN)
        out_ref[:, feats] = (x_ref[:, feats].astype(F32) + branch).astype(BF16)


def grad_fourth_kernel(recv_ref, cot_ref, out_ref):
    chunks = cot_ref.shape[0] // LANES
    rows = HB * EB // PEERS
    for a in range(2):
        gathered = model_rows(recv_ref, chunks, a, PAIR)
        grad = dot(gathered, cot_ref[:, a * BS : (a + 1) * BS], NN).astype(BF16)
        out_ref[:, a * rows : (a + 1) * rows, :] = grad.reshape(PEERS, rows, BS)


def grad_first_kernel(recv_ref, normed_ref, fourth_ref, out_ref):
    chunks = normed_ref.shape[0] // LANES
    rows = BS // PEERS
    for a in range(2):
        dfirst = model_rows(recv_ref, chunks, a, PAIR)
        grad = dot(dfirst, normed_ref[:, a * BS : (a + 1) * BS], NN).astype(BF16).T
        for half in range(2):
            base = (2 * a + half) * rows
            part = grad[:, half * BS : (half + 1) * BS]
            out_ref[:, base : base + rows, :] = part.reshape(PEERS, rows, BS)
    out_ref[:, 4 * rows :, :] = fourth_ref[...]


def sum_kernel(scale, recv_ref, first_ref, fourth_ref):
    total = jnp.sum(recv_ref[...].astype(F32), axis=0) * scale
    _, rows, _ = first_ref.shape
    for a in range(2):
        for half in range(2):
            base = (2 * a + half) * rows
            first_ref[a, :, half * BS : (half + 1) * BS] = total[base : base + rows]
    fourth_ref[...] = total[4 * rows :].reshape(fourth_ref.shape)


def finish_kernel(scale, own_ref, other_ref, second_ref, third_ref):
    total = (own_ref[0, 0].astype(F32) + other_ref[...].astype(F32)) * scale
    second_ref[0] = total[:, :HBS]
    third_ref[0] = total[:, HBS:]


def token_kernel(recv_ref, squares_ref, x_ref, gain_ref, w1_ref, cot_ref, out_ref):
    chunks = x_ref.shape[0] // LANES
    inverse = lax.rsqrt(columns(stat_sum(squares_ref[...]), chunks) / MODEL_WIDTH + epsilon)
    inner = columns(stat_sum(recv_ref[:, chunks * PAIR :, :]), chunks) / MODEL_WIDTH
    for a in range(2):
        feats = slice(a * BS, (a + 1) * BS)
        dfirst = model_rows(recv_ref, chunks, a, PAIR)
        dnormed = dot(dfirst, w1_ref[a], TT)
        xhat = x_ref[:, feats].astype(F32) * inverse
        change = dnormed * gain_ref[:, feats] - xhat * inner
        out_ref[:, feats] = (cot_ref[:, feats].astype(F32) + inverse * change).astype(BF16)


def shards(tokens, gain, w_first, w_second, w_third, w_fourth, cotangent):
    element_count, local_width = tokens.shape
    dp = lax.axis_size("dp")
    scale = 1.0 / math.sqrt(element_count * dp)
    chunks = element_count // LANES
    gain_row = gain[None, :]
    z_size = dp // 2
    z_groups = [[y * z_size + z for z in range(z_size)] for y in range(2)]
    y_index = lax.axis_index("dp") // z_size
    shape = jax.ShapeDtypeStruct
    hidden_flops = 2 * HBS * HBS * element_count
    model_flops = 2 * local_width * HB * EB * element_count

    def exchange(value, axis):
        return lax.all_to_all(value, axis, 0, 0, tiled=True)

    def after(value, other):
        return lax.optimization_barrier((value, other))[0]

    rows = chunks * PAIR
    wide = (HBS, element_count)
    step = 2 * LANES
    steps = element_count // step
    params = pltpu.CompilerParams(vmem_limit_bytes=VMEM)

    def cost(flops):
        return pl.CostEstimate(flops=int(flops), bytes_accessed=8 << 20, transcendentals=0)

    def whole(*dims):
        return pl.BlockSpec(dims, lambda i, *_: (0,) * len(dims))

    send = pl.pallas_call(
        head_kernel,
        out_shape=shape((PEERS, 2 * rows + STATS, LANES), BF16),
        grid=(2,),
        in_specs=[
            pl.BlockSpec((element_count, BS), lambda a: (0, a)),
            pl.BlockSpec((1, BS), lambda a: (0, a)),
            pl.BlockSpec((1, BS, HB * EB), lambda a: (a, 0, 0)),
            pl.BlockSpec((1, HB * EB, BS), lambda a: (a, 0, 0)),
            pl.BlockSpec((element_count, BS), lambda a: (0, a)),
        ],
        out_specs=whole(PEERS, 2 * rows + STATS, LANES),
        scratch_shapes=[pltpu.VMEM((1, element_count), F32)],
        compiler_params=params,
        cost_estimate=cost(2 * model_flops),
    )(tokens, gain_row, w_first, w_fourth, cotangent)
    recv = exchange(send, "tensor")
    turned = shape((HBS, HBS), BF16)
    w_second_t, w_third_t = call(turn_kernel, [turned, turned], (w_second, w_third))
    by_tokens = pl.BlockSpec((HBS, step), lambda i: (0, i))
    peer_rows = pl.BlockSpec((PEERS, 2 * PAIR, LANES), lambda i: (0, i, 0))
    stats_spec = pl.BlockSpec((PEERS, STATS, LANES), lambda i: (0, 2 * rows // STATS, 0))
    pre, act, send = pl.pallas_call(
        forward_kernel,
        out_shape=[shape(wide, F32), shape(wide, BF16), shape((PEERS, rows, LANES), BF16)],
        grid=(steps,),
        in_specs=[peer_rows, stats_spec, whole(HBS, HBS), whole(HBS, HBS)],
        out_specs=[by_tokens, by_tokens, peer_rows],
        scratch_shapes=[pltpu.VMEM((STATS, LANES), F32)],
        compiler_params=params,
        cost_estimate=cost(2 * hidden_flops),
    )(recv, recv, w_second_t, w_third_t)
    third = exchange(send, "tensor")
    scaled, send = pl.pallas_call(
        backward_kernel,
        out_shape=[shape(wide, BF16), shape((PEERS, rows + STATS, LANES), BF16)],
        grid=(steps,),
        in_specs=[
            pl.BlockSpec((PEERS, 2 * PAIR, LANES), lambda i: (0, steps + i, 0)),
            stats_spec,
            by_tokens,
            whole(1, HBS, HBS),
            whole(1, HBS, HBS),
        ],
        out_specs=[by_tokens, whole(PEERS, rows + STATS, LANES)],
        scratch_shapes=[pltpu.VMEM((STATS, LANES), F32)] * 2,
        compiler_params=params,
        cost_estimate=cost(2 * hidden_flops),
    )(recv, recv, pre, w_second, w_third)
    quarter = z_size // 2
    hidden = pl.pallas_call(
        hidden_grads_kernel,
        out_shape=shape((z_size, 2, HBS // dp, 2 * HBS), BF16),
        grid_spec=pltpu.PrefetchScalarGridSpec(
            num_scalar_prefetch=1,
            grid=(4,),
            in_specs=[
                pl.BlockSpec((PEERS // 4, rows, LANES), lambda i, y: (i, 0, 0)),
                pl.BlockSpec((PEERS, rows, LANES), lambda i, y: (0, 1, 0)),
                pl.BlockSpec((HBS // 4, element_count), lambda i, y: (i, 0)),
                whole(*wide),
            ],
            out_specs=pl.BlockSpec(
                (quarter, 1, HBS // dp, 2 * HBS), lambda i, y: (i % 2, (i // 2 + y[0]) % 2, 0, 0)
            ),
            scratch_shapes=[pltpu.VMEM(wide, BF16)],
        ),
        compiler_params=params,
        cost_estimate=cost(2 * hidden_flops),
    )(y_index.astype(jnp.int32)[None], recv, recv, act, scaled)
    hidden = lax.psum_scatter(hidden, "dp", scatter_dimension=0, axis_index_groups=z_groups, tiled=True)
    squares = recv[:, 2 * rows :, :]
    back = exchange(after(send, third), "tensor")

    normed = call(norm_kernel, shape(tokens.shape, BF16), (tokens, gain_row, after(squares, third)))
    output = call(
        output_kernel, shape(tokens.shape, BF16), (third, tokens, w_fourth), flops=LATE * model_flops
    )
    fourth = call(
        grad_fourth_kernel, shape((PEERS, 64, BS), BF16), (third, cotangent), flops=model_flops
    )
    both = call(
        grad_first_kernel, shape((PEERS, 128, BS), BF16), (back, normed, fourth), flops=model_flops
    )
    both = exchange(both, "dp")
    token_gradient = call(
        token_kernel,
        shape(tokens.shape, BF16),
        (back, squares, tokens, gain_row, w_first, cotangent),
        flops=LATE * model_flops,
    )
    grad_first, grad_fourth = call(
        functools.partial(sum_kernel, scale),
        [shape((2, BS // dp, HB * EB), F32), shape((2, HB * EB // dp, BS), F32)],
        (both,),
    )
    other = lax.ppermute(hidden[0, 1], "dp", [(i, (i + z_size) % dp) for i in range(dp)])
    part = shape((1, HBS // dp, HBS), F32)
    grad_second, grad_third = call(functools.partial(finish_kernel, scale), [part, part], (hidden, other))
    return output, token_gradient, grad_first, grad_second, grad_third, grad_fourth


def solution(mesh):
    return jax.shard_map(
        shards,
        mesh=mesh,
        in_specs=(
            P("dp", "tensor"),
            P("tensor"),
            P("tensor", None, None),
            P("tensor", None, None),
            P("tensor", None, None),
            P("tensor", None, None),
            P("dp", "tensor"),
        ),
        out_specs=(
            P("dp", "tensor"),
            P("dp", "tensor"),
            P("tensor", "dp", None),
            P("tensor", "dp", None),
            P("tensor", "dp", None),
            P("tensor", "dp", None),
        ),
        check_vma=False,
    )
```

```python
import functools
import math

import jax
import jax.numpy as jnp
from jax import lax
from jax.experimental import pallas as pl
from jax.experimental.pallas import tpu as pltpu
from jax.sharding import PartitionSpec as P

MODEL_WIDTH = 8192
DIAGONAL_BLOCKS = 32
HBS = 1024
HB = 16
BS = 256
EB = 32
PEERS = 16
PAIR = 2 * EB
LANES = 128
STATS = 16
STEP = 256
LATE = 1000
VMEM = 58 * 1024 * 1024
ROOM = 3407872

epsilon = 1e-05
root_scale = math.sqrt(2.0 / math.pi)
cubic_term = 0.044715

F32 = jnp.float32
BF16 = jnp.bfloat16

NN = (((1,), (0,)), ((), ()))
NT = (((1,), (1,)), ((), ()))
TN = (((0,), (0,)), ((), ()))
TT = (((0,), (1,)), ((), ()))


def dot(a, b, dims):
    return lax.dot_general(a, b, dims, preferred_element_type=F32)


def call(kernel, out_shape, args, scratch=(), flops=0, **extra):
    outs = out_shape if isinstance(out_shape, (list, tuple)) else [out_shape]
    moved = sum(a.size * a.dtype.itemsize for a in args) + sum(
        math.prod(o.shape) * o.dtype.itemsize for o in outs
    )
    return pl.pallas_call(
        kernel,
        out_shape=out_shape,
        in_specs=[pl.BlockSpec(memory_space=pltpu.VMEM)] * len(args),
        out_specs=jax.tree.map(lambda _: pl.BlockSpec(memory_space=pltpu.VMEM), out_shape),
        scratch_shapes=list(scratch),
        compiler_params=pltpu.CompilerParams(vmem_limit_bytes=VMEM),
        cost_estimate=pl.CostEstimate(flops=int(flops), bytes_accessed=int(moved), transcendentals=0),
        **extra,
    )(*args)


def stat_rows(value, chunks):
    high = value.astype(BF16).astype(F32)
    low = value - high
    rows = []
    for i in range(chunks):
        part = slice(i * LANES, (i + 1) * LANES)
        rows += [high[:, part], low[:, part]]
    rows.append(jnp.zeros((STATS - 2 * chunks, LANES), F32))
    return jnp.concatenate(rows, axis=0).astype(BF16)


def stat_sum(rows):
    return jnp.sum(rows.astype(F32), axis=0)


def head_kernel(
    x_hbm, cot_hbm, gain_ref, w1_hbm, w4_hbm, out_hbm, x_ref, cot_ref, w1_ref, w4_ref, out_ref, in_sems, out_sems
):
    steps = x_ref.shape[0] // STEP
    rows = steps * 2 * PAIR
    loads, stores = [], []
    weights = [
        pltpu.make_async_copy(source, target, in_sems.at[2 * steps + k])
        for k, (source, target) in enumerate(((w1_hbm, w1_ref), (w4_hbm, w4_ref)))
    ]
    weights[0].start()
    for i in range(steps):
        part = pl.ds(i * STEP, STEP)
        for k, (source, target) in enumerate(((x_hbm, x_ref), (cot_hbm, cot_ref))):
            loads.append(pltpu.make_async_copy(source.at[part], target.at[part], in_sems.at[2 * i + k]))
    loads[0].start()

    def store(base, size):
        part = pl.ds(base, size)
        copy = pltpu.make_async_copy(out_ref.at[:, part], out_hbm.at[:, part], out_sems.at[len(stores)])
        copy.start()
        stores.append(copy)

    weights[0].wait()
    weights[1].start()
    for copy in loads[1:]:
        copy.start()
    turned = [w1_ref[a].T for a in range(2)]
    totals = []
    for i in range(steps):
        part = slice(i * STEP, (i + 1) * STEP)
        loads[2 * i].wait()
        x = x_ref[part, :].astype(F32)
        scaled = (x * gain_ref[...]).astype(BF16)
        base = i * 2 * PAIR
        for a in range(2):
            first = dot(turned[a], scaled[:, a * BS : (a + 1) * BS], NT).astype(BF16)
            for k in range(2):
                start = base + k * PAIR + a * EB
                value = first[:, k * LANES : (k + 1) * LANES]
                out_ref[:, start : start + EB, :] = value.reshape(PEERS, EB, LANES)
        store(base, 2 * PAIR)
        loads[2 * i + 1].wait()
        if i == 0:
            weights[1].wait()
        for a in range(2):
            dgathered = dot(w4_ref[a], cot_ref[part, a * BS : (a + 1) * BS], NT).astype(BF16)
            for k in range(2):
                start = rows + base + k * PAIR + a * EB
                value = dgathered[:, k * LANES : (k + 1) * LANES]
                out_ref[:, start : start + EB, :] = value.reshape(PEERS, EB, LANES)
        store(rows + base, 2 * PAIR)
        squares = x * x
        folded = squares[:, :LANES]
        for k in range(1, squares.shape[1] // LANES):
            folded = folded + squares[:, k * LANES : (k + 1) * LANES]
        totals.append(jnp.sum(folded.T, axis=0, keepdims=True))
    stats = stat_rows(jnp.concatenate(totals, axis=1), 2 * steps)
    out_ref[:, 2 * rows :, :] = jnp.broadcast_to(stats[None], (PEERS, STATS, LANES))
    store(2 * rows, STATS)
    for copy in stores:
        copy.wait()


def reciprocal(stats, i):
    rows = stats[4 * i : 4 * i + 4]
    total = jnp.concatenate([rows[0:1] + rows[1:2], rows[2:3] + rows[3:4]], axis=1)
    return lax.rsqrt(total / MODEL_WIDTH + epsilon)


def hidden_rows(ref):
    sources, rows, _ = ref.shape
    parts = [
        ref[:, i * PAIR : (i + 1) * PAIR, :].reshape(sources * PAIR, LANES) for i in range(rows // PAIR)
    ]
    return jnp.concatenate(parts, axis=1)


def turn_kernel(w2_ref, w3_ref, w2t_ref, w3t_ref):
    w2t_ref[...] = w2_ref[0].T
    w3t_ref[...] = w3_ref[0].T


def by_peer(value):
    parts = [value[:, k * LANES : (k + 1) * LANES].reshape(PEERS, PAIR, LANES) for k in range(2)]
    return jnp.concatenate(parts, axis=1)


def middle_kernel(
    recv_hbm, w2t_hbm, w3t_hbm, w2_hbm, w3_hbm, act_hbm, scaled_hbm, out_hbm,
    recv_ref, w2t_ref, w3t_ref, w2_ref, w3_ref, pre_ref, act_ref, dpre_ref, scaled_ref, out_ref, in_sems, out_sems,
):
    steps = act_ref.shape[0]
    rows = steps * 2 * PAIR
    loads, stores = {}, []

    def load(key, source, target):
        copy = pltpu.make_async_copy(source, target, in_sems.at[len(loads)])
        copy.start()
        loads[key] = copy

    def load_rows(base, size):
        part = pl.ds(base, size)
        load(base, recv_hbm.at[:, part], recv_ref.at[:, part])

    def store(source, target):
        copy = pltpu.make_async_copy(source, target, out_sems.at[len(stores)])
        copy.start()
        stores.append(copy)

    def peer_rows(base):
        return hidden_rows(recv_ref.at[:, pl.ds(base, 2 * PAIR)])

    def send_rows(base, value):
        out_ref[:, base : base + 2 * PAIR, :] = by_peer(value.astype(BF16))
        part = pl.ds(base, 2 * PAIR)
        store(out_ref.at[:, part], out_hbm.at[:, part])

    load_rows(2 * rows, STATS)
    load_rows(0, 2 * PAIR)
    load("w2t", w2t_hbm, w2t_ref)
    for i in range(1, steps):
        load_rows(i * 2 * PAIR, 2 * PAIR)
    load("w3", w3_hbm, w3_ref)
    for i in range(steps):
        load_rows(rows + i * 2 * PAIR, 2 * PAIR)
    load("w3t", w3t_hbm, w3t_ref)
    load("w2", w2_hbm, w2_ref)
    loads[2 * rows].wait()
    stats = stat_sum(recv_ref[:, 2 * rows :, :])
    inverses = [reciprocal(stats, i) for i in range(steps)]
    loads["w2t"].wait()
    for i in range(steps):
        loads[i * 2 * PAIR].wait()
        pre_ref[i] = dot(w2t_ref[...], peer_rows(i * 2 * PAIR), NN) * inverses[i]
    loads["w3"].wait()
    for i in range(steps):
        loads[rows + i * 2 * PAIR].wait()
    inner = []
    for i in range(steps):
        dact = dot(w3_ref[0], peer_rows(rows + i * 2 * PAIR), NN)
        pre = pre_ref[i]
        square = pre * pre
        hyper = jnp.tanh(pre * (root_scale + (root_scale * cubic_term) * square))
        half = 0.5 * pre
        act_ref[i] = (half + half * hyper).astype(BF16)
        slope = (0.5 + 0.5 * hyper) + half * (1.0 - hyper * hyper) * (
            root_scale + (3.0 * root_scale * cubic_term) * square
        )
        dpre = dact * slope
        inner.append(jnp.sum(dpre * pre, axis=0, keepdims=True))
        dpre_ref[i] = dpre.astype(BF16)
        scaled_ref[i] = (dpre * inverses[i]).astype(BF16)
    store(act_ref, act_hbm)
    store(scaled_ref, scaled_hbm)
    loads["w3t"].wait()
    for i in range(steps):
        send_rows(i * 2 * PAIR, dot(w3t_ref[...], act_ref[i], NN))
    loads["w2"].wait()
    for i in range(steps):
        send_rows(rows + i * 2 * PAIR, dot(w2_ref[0], dpre_ref[i], NN))
    rest = stat_rows(jnp.concatenate(inner, axis=1), 2 * steps)
    out_ref[:, 2 * rows :, :] = jnp.broadcast_to(rest[None], (PEERS, STATS, LANES))
    part = pl.ds(2 * rows, STATS)
    store(out_ref.at[:, part], out_hbm.at[:, part])
    for copy in stores:
        copy.wait()


def hidden_grads_kernel(y_ref, mixed_ref, dthird_ref, act_ref, scaled_ref, out_ref, turned_ref):
    del y_ref

    @pl.when(pl.program_id(0) == 0)
    def _():
        turned_ref[...] = hidden_rows(dthird_ref)

    shape = (out_ref.shape[0], out_ref.shape[2], HBS)
    scaled = jnp.concatenate([scaled_ref[i] for i in range(scaled_ref.shape[0])], axis=1)
    act = jnp.concatenate([act_ref[i] for i in range(act_ref.shape[0])], axis=1)
    second = dot(hidden_rows(mixed_ref), scaled, NT).astype(BF16)
    out_ref[:, 0, :, :HBS] = second.reshape(shape)
    third = dot(act, turned_ref[...], NT).astype(BF16)
    out_ref[:, 0, :, HBS:] = third.reshape(shape)


def model_rows(ref, chunks, a, offset):
    parts = []
    for i in range(chunks):
        start = offset + i * PAIR + a * EB
        parts.append(ref[:, start : start + EB, :].reshape(HB * EB, LANES))
    return jnp.concatenate(parts, axis=1)


def columns(stats, chunks):
    turned = stats.T
    parts = [turned[:, 2 * i : 2 * i + 1] + turned[:, 2 * i + 1 : 2 * i + 2] for i in range(chunks)]
    return jnp.concatenate(parts, axis=0)


def norm_kernel(x_ref, gain_ref, stats_ref, normed_ref):
    chunks = x_ref.shape[0] // LANES
    inverse = lax.rsqrt(columns(stat_sum(stats_ref[...]), chunks) / MODEL_WIDTH + epsilon)
    normed_ref[...] = (x_ref[...].astype(F32) * inverse * gain_ref[...]).astype(BF16)


def output_kernel(recv_ref, x_ref, w4_ref, out_ref):
    chunks = x_ref.shape[0] // LANES
    for a in range(2):
        feats = slice(a * BS, (a + 1) * BS)
        gathered = model_rows(recv_ref, chunks, a, 0)
        branch = dot(gathered, w4_ref[a], TN)
        out_ref[:, feats] = (x_ref[:, feats].astype(F32) + branch).astype(BF16)


def model_grads_kernel(
    recv_hbm, normed_hbm, cot_hbm, out_hbm, recv_ref, normed_ref, cot_ref, out_ref, sems, out_sems
):
    chunks = normed_ref.shape[0] // LANES
    rows = chunks * PAIR
    loads = []
    for source, target in (
        (recv_hbm.at[:, pl.ds(rows, rows)], recv_ref.at[:, pl.ds(rows, rows)]),
        (normed_hbm, normed_ref),
        (recv_hbm.at[:, pl.ds(0, rows)], recv_ref.at[:, pl.ds(0, rows)]),
        (cot_hbm, cot_ref),
    ):
        loads.append(pltpu.make_async_copy(source, target, sems.at[len(loads)]))
        loads[-1].start()
    first_rows, fourth_rows = BS // PEERS, HB * EB // PEERS
    stores = []

    def store(k):
        part = pl.ds(k * 4 * first_rows, 4 * first_rows)
        copy = pltpu.make_async_copy(out_ref.at[:, part], out_hbm.at[:, part], out_sems.at[k])
        copy.start()
        stores.append(copy)

    loads[0].wait()
    loads[1].wait()
    for a in range(2):
        dfirst = model_rows(recv_ref, chunks, a, rows)
        grad = dot(dfirst, normed_ref[:, a * BS : (a + 1) * BS], NN).astype(BF16).T
        for half in range(2):
            part = grad[:, half * BS : (half + 1) * BS]
            base = (2 * a + half) * first_rows
            out_ref[:, base : base + first_rows, :] = part.reshape(PEERS, first_rows, BS)
    store(0)
    loads[2].wait()
    loads[3].wait()
    for a in range(2):
        gathered = model_rows(recv_ref, chunks, a, 0)
        grad = dot(gathered, cot_ref[:, a * BS : (a + 1) * BS], NN).astype(BF16)
        base = 4 * first_rows + a * fourth_rows
        out_ref[:, base : base + fourth_rows, :] = grad.reshape(PEERS, fourth_rows, BS)
    store(1)
    for copy in stores:
        copy.wait()


def token_kernel(recv_ref, stats_ref, x_ref, gain_ref, w1_ref, cot_ref, out_ref):
    chunks = x_ref.shape[0] // LANES
    inverse = lax.rsqrt(columns(stat_sum(stats_ref[...]), chunks) / MODEL_WIDTH + epsilon)
    inner = columns(stat_sum(recv_ref[:, 2 * chunks * PAIR :, :]), chunks) / MODEL_WIDTH
    for a in range(2):
        feats = slice(a * BS, (a + 1) * BS)
        dfirst = model_rows(recv_ref, chunks, a, chunks * PAIR)
        dnormed = dot(dfirst, w1_ref[a], TT)
        xhat = x_ref[:, feats].astype(F32) * inverse
        change = dnormed * gain_ref[:, feats] - xhat * inner
        out_ref[:, feats] = (cot_ref[:, feats].astype(F32) + inverse * change).astype(BF16)


def sum_kernel(scale, recv_ref, first_ref, fourth_ref):
    total = jnp.sum(recv_ref[...].astype(F32), axis=0) * scale
    _, rows, _ = first_ref.shape
    for a in range(2):
        for half in range(2):
            base = (2 * a + half) * rows
            first_ref[a, :, half * BS : (half + 1) * BS] = total[base : base + rows]
    fourth_ref[...] = total[4 * rows :].reshape(fourth_ref.shape)


def finish_kernel(scale, own_ref, other_ref, second_ref, third_ref):
    total = (own_ref[0, 0].astype(F32) + other_ref[...].astype(F32)) * scale
    second_ref[0] = total[:, :HBS]
    third_ref[0] = total[:, HBS:]


def shards(tokens, gain, w_first, w_second, w_third, w_fourth, cotangent):
    element_count, local_width = tokens.shape
    dp = lax.axis_size("dp")
    scale = 1.0 / math.sqrt(element_count * dp)
    gain_row = gain[None, :]
    z_size = dp // 2
    z_groups = [[y * z_size + z for z in range(z_size)] for y in range(2)]
    y_pairs = [(i, (i + z_size) % dp) for i in range(dp)]
    y_index = (lax.axis_index("dp") // z_size).astype(jnp.int32)[None]
    shape = jax.ShapeDtypeStruct
    hidden_flops = 2 * HBS * HBS * element_count
    model_flops = 2 * local_width * HB * EB * element_count
    steps = element_count // STEP
    rows = steps * 2 * PAIR
    sent = shape((PEERS, 2 * rows + STATS, LANES), BF16)
    stepped = shape((steps, HBS, STEP), BF16)
    hbm = pl.BlockSpec(memory_space=pltpu.HBM)
    vmem = pl.BlockSpec(memory_space=pltpu.VMEM)
    params = pltpu.CompilerParams(vmem_limit_bytes=VMEM)
    beside = pltpu.CompilerParams(vmem_limit_bytes=VMEM - ROOM)

    def cost(flops):
        return pl.CostEstimate(flops=int(flops), bytes_accessed=8 << 20, transcendentals=0)

    def whole(*dims):
        return pl.BlockSpec(dims, lambda i, *_: (0,) * len(dims))

    send = pl.pallas_call(
        head_kernel,
        out_shape=sent,
        in_specs=[hbm, hbm, vmem, hbm, hbm],
        out_specs=hbm,
        scratch_shapes=[
            pltpu.VMEM(tokens.shape, BF16),
            pltpu.VMEM(tokens.shape, BF16),
            pltpu.VMEM(w_first.shape, BF16),
            pltpu.VMEM(w_fourth.shape, BF16),
            pltpu.VMEM(sent.shape, BF16),
            pltpu.SemaphoreType.DMA((2 * steps + 2,)),
            pltpu.SemaphoreType.DMA((2 * steps + 1,)),
        ],
        compiler_params=params,
        cost_estimate=cost(2 * model_flops),
    )(tokens, cotangent, gain_row, w_first, w_fourth)
    recv = lax.all_to_all(send, "tensor", 0, 0, tiled=True)
    turned = shape((HBS, HBS), BF16)
    w_second_t, w_third_t = call(turn_kernel, [turned, turned], (w_second, w_third))
    act, scaled, send = pl.pallas_call(
        middle_kernel,
        out_shape=[stepped, stepped, sent],
        in_specs=[hbm] * 5,
        out_specs=[hbm, hbm, hbm],
        scratch_shapes=[
            pltpu.VMEM(sent.shape, BF16),
            pltpu.VMEM(turned.shape, BF16),
            pltpu.VMEM(turned.shape, BF16),
            pltpu.VMEM(w_second.shape, BF16),
            pltpu.VMEM(w_third.shape, BF16),
            pltpu.VMEM(stepped.shape, F32),
            pltpu.VMEM(stepped.shape, BF16),
            pltpu.VMEM(stepped.shape, BF16),
            pltpu.VMEM(stepped.shape, BF16),
            pltpu.VMEM(sent.shape, BF16),
            pltpu.SemaphoreType.DMA((2 * steps + 5,)),
            pltpu.SemaphoreType.DMA((2 * steps + 3,)),
        ],
        compiler_params=beside,
        cost_estimate=cost(4 * hidden_flops),
    )(recv, w_second_t, w_third_t, w_second, w_third)
    back = lax.all_to_all(send, "tensor", 0, 0, tiled=True)
    quarter = z_size // 2
    hidden = pl.pallas_call(
        hidden_grads_kernel,
        out_shape=shape((z_size, 2, HBS // dp, 2 * HBS), BF16),
        grid_spec=pltpu.PrefetchScalarGridSpec(
            num_scalar_prefetch=1,
            grid=(4,),
            in_specs=[
                pl.BlockSpec((PEERS // 4, rows, LANES), lambda i, y: (i, 0, 0)),
                pl.BlockSpec((PEERS, rows, LANES), lambda i, y: (0, 1, 0)),
                pl.BlockSpec((steps, HBS // 4, STEP), lambda i, y: (0, i, 0)),
                whole(steps, HBS, STEP),
            ],
            out_specs=pl.BlockSpec(
                (quarter, 1, HBS // dp, 2 * HBS), lambda i, y: (i % 2, (i // 2 + y[0]) % 2, 0, 0)
            ),
            scratch_shapes=[pltpu.VMEM((HBS, element_count), BF16)],
        ),
        compiler_params=params,
        cost_estimate=cost(2 * hidden_flops),
    )(y_index, recv, recv, act, scaled)
    hidden = lax.psum_scatter(hidden, "dp", scatter_dimension=0, axis_index_groups=z_groups, tiled=True)

    stats_spec = pl.BlockSpec((PEERS, STATS, LANES), lambda i: (0, 2 * rows // STATS, 0))
    normed = pl.pallas_call(
        norm_kernel,
        out_shape=shape(tokens.shape, BF16),
        grid=(1,),
        in_specs=[whole(*tokens.shape), whole(1, local_width), stats_spec],
        out_specs=whole(*tokens.shape),
        compiler_params=params,
        cost_estimate=cost(model_flops),
    )(tokens, gain_row, recv)
    both = shape((PEERS, 2 * PAIR, BS), BF16)
    both = pl.pallas_call(
        model_grads_kernel,
        out_shape=both,
        in_specs=[hbm, hbm, hbm],
        out_specs=hbm,
        scratch_shapes=[
            pltpu.VMEM((PEERS, 2 * rows, LANES), BF16),
            pltpu.VMEM(tokens.shape, BF16),
            pltpu.VMEM(tokens.shape, BF16),
            pltpu.VMEM(both.shape, BF16),
            pltpu.SemaphoreType.DMA((4,)),
            pltpu.SemaphoreType.DMA((2,)),
        ],
        compiler_params=beside,
        cost_estimate=cost(2 * model_flops),
    )(back, normed, cotangent)
    both = lax.all_to_all(both, "dp", 0, 0, tiled=True)
    output = call(output_kernel, shape(tokens.shape, BF16), (back, tokens, w_fourth), flops=LATE * model_flops)
    token_gradient = pl.pallas_call(
        token_kernel,
        out_shape=shape(tokens.shape, BF16),
        grid=(1,),
        in_specs=[
            whole(*sent.shape),
            stats_spec,
            whole(*tokens.shape),
            whole(1, local_width),
            whole(*w_first.shape),
            whole(*tokens.shape),
        ],
        out_specs=whole(*tokens.shape),
        compiler_params=params,
        cost_estimate=cost(LATE * model_flops),
    )(back, recv, tokens, gain_row, w_first, cotangent)
    grad_first, grad_fourth = call(
        functools.partial(sum_kernel, scale),
        [shape((2, BS // dp, HB * EB), F32), shape((2, HB * EB // dp, BS), F32)],
        (both,),
    )
    other = lax.ppermute(hidden[0, 1], "dp", y_pairs)
    part = shape((1, HBS // dp, HBS), F32)
    grad_second, grad_third = call(functools.partial(finish_kernel, scale), [part, part], (hidden, other))
    return output, token_gradient, grad_first, grad_second, grad_third, grad_fourth


def solution(mesh):
    return jax.shard_map(
        shards,
        mesh=mesh,
        in_specs=(
            P("dp", "tensor"),
            P("tensor"),
            P("tensor", None, None),
            P("tensor", None, None),
            P("tensor", None, None),
            P("tensor", None, None),
            P("dp", "tensor"),
        ),
        out_specs=(
            P("dp", "tensor"),
            P("dp", "tensor"),
            P("tensor", "dp", None),
            P("tensor", "dp", None),
            P("tensor", "dp", None),
            P("tensor", "dp", None),
        ),
        check_vma=False,
    )
```

```python
import functools
import math

import jax
import jax.numpy as jnp
from jax import lax
from jax.experimental import pallas as pl
from jax.experimental.pallas import tpu as pltpu
from jax.sharding import PartitionSpec as P

MODEL_WIDTH = 8192
DIAGONAL_BLOCKS = 32
HBS = 1024
HB = 16
BS = 256
EB = 32
PEERS = 16
PAIR = 2 * EB
LANES = 128
STATS = 16
STEP = 256
LATE = 1000
VMEM = 58 * 1024 * 1024

epsilon = 1e-05
root_scale = math.sqrt(2.0 / math.pi)
cubic_term = 0.044715

F32 = jnp.float32
BF16 = jnp.bfloat16

NN = (((1,), (0,)), ((), ()))
NT = (((1,), (1,)), ((), ()))
TN = (((0,), (0,)), ((), ()))
TT = (((0,), (1,)), ((), ()))


def dot(a, b, dims):
    return lax.dot_general(a, b, dims, preferred_element_type=F32)


def call(kernel, out_shape, args, scratch=(), flops=0, **extra):
    outs = out_shape if isinstance(out_shape, (list, tuple)) else [out_shape]
    moved = sum(a.size * a.dtype.itemsize for a in args) + sum(
        math.prod(o.shape) * o.dtype.itemsize for o in outs
    )
    return pl.pallas_call(
        kernel,
        out_shape=out_shape,
        in_specs=[pl.BlockSpec(memory_space=pltpu.VMEM)] * len(args),
        out_specs=jax.tree.map(lambda _: pl.BlockSpec(memory_space=pltpu.VMEM), out_shape),
        scratch_shapes=list(scratch),
        compiler_params=pltpu.CompilerParams(vmem_limit_bytes=VMEM),
        cost_estimate=pl.CostEstimate(flops=int(flops), bytes_accessed=int(moved), transcendentals=0),
        **extra,
    )(*args)


def stat_rows(value, chunks):
    high = value.astype(BF16).astype(F32)
    low = value - high
    rows = []
    for i in range(chunks):
        part = slice(i * LANES, (i + 1) * LANES)
        rows += [high[:, part], low[:, part]]
    rows.append(jnp.zeros((STATS - 2 * chunks, LANES), F32))
    return jnp.concatenate(rows, axis=0).astype(BF16)


def stat_sum(rows):
    return jnp.sum(rows.astype(F32), axis=0)


def head_kernel(
    x_hbm, cot_hbm, gain_ref, w1_hbm, w4_hbm, out_hbm, x_ref, cot_ref, w1_ref, w4_ref, out_ref, in_sems, out_sems
):
    steps = x_ref.shape[0] // STEP
    rows = steps * 2 * PAIR
    loads, stores = [], []
    weights = [
        pltpu.make_async_copy(source, target, in_sems.at[2 * steps + k])
        for k, (source, target) in enumerate(((w1_hbm, w1_ref), (w4_hbm, w4_ref)))
    ]
    weights[0].start()
    for i in range(steps):
        part = pl.ds(i * STEP, STEP)
        for k, (source, target) in enumerate(((x_hbm, x_ref), (cot_hbm, cot_ref))):
            loads.append(pltpu.make_async_copy(source.at[part], target.at[part], in_sems.at[2 * i + k]))
    loads[0].start()

    def store(base, size):
        part = pl.ds(base, size)
        copy = pltpu.make_async_copy(out_ref.at[:, part], out_hbm.at[:, part], out_sems.at[len(stores)])
        copy.start()
        stores.append(copy)

    weights[0].wait()
    weights[1].start()
    for copy in loads[1:]:
        copy.start()
    turned = [w1_ref[a].T for a in range(2)]
    totals = []
    for i in range(steps):
        part = slice(i * STEP, (i + 1) * STEP)
        loads[2 * i].wait()
        x = x_ref[part, :].astype(F32)
        scaled = (x * gain_ref[...]).astype(BF16)
        base = i * 2 * PAIR
        for a in range(2):
            first = dot(turned[a], scaled[:, a * BS : (a + 1) * BS], NT).astype(BF16)
            for k in range(2):
                start = base + k * PAIR + a * EB
                value = first[:, k * LANES : (k + 1) * LANES]
                out_ref[:, start : start + EB, :] = value.reshape(PEERS, EB, LANES)
        store(base, 2 * PAIR)
        loads[2 * i + 1].wait()
        if i == 0:
            weights[1].wait()
        for a in range(2):
            dgathered = dot(w4_ref[a], cot_ref[part, a * BS : (a + 1) * BS], NT).astype(BF16)
            for k in range(2):
                start = rows + base + k * PAIR + a * EB
                value = dgathered[:, k * LANES : (k + 1) * LANES]
                out_ref[:, start : start + EB, :] = value.reshape(PEERS, EB, LANES)
        store(rows + base, 2 * PAIR)
        squares = x * x
        folded = squares[:, :LANES]
        for k in range(1, squares.shape[1] // LANES):
            folded = folded + squares[:, k * LANES : (k + 1) * LANES]
        totals.append(jnp.sum(folded.T, axis=0, keepdims=True))
    stats = stat_rows(jnp.concatenate(totals, axis=1), 2 * steps)
    out_ref[:, 2 * rows :, :] = jnp.broadcast_to(stats[None], (PEERS, STATS, LANES))
    store(2 * rows, STATS)
    for copy in stores:
        copy.wait()


def reciprocal(stats, i):
    rows = stats[4 * i : 4 * i + 4]
    total = jnp.concatenate([rows[0:1] + rows[1:2], rows[2:3] + rows[3:4]], axis=1)
    return lax.rsqrt(total / MODEL_WIDTH + epsilon)


def hidden_rows(ref):
    sources, rows, _ = ref.shape
    parts = [
        ref[:, i * PAIR : (i + 1) * PAIR, :].reshape(sources * PAIR, LANES) for i in range(rows // PAIR)
    ]
    return jnp.concatenate(parts, axis=1)


def turn_kernel(w2_ref, w3_ref, w2t_ref, w3t_ref):
    w2t_ref[...] = w2_ref[0].T
    w3t_ref[...] = w3_ref[0].T


def by_peer(value):
    parts = [value[:, k * LANES : (k + 1) * LANES].reshape(PEERS, PAIR, LANES) for k in range(2)]
    return jnp.concatenate(parts, axis=1)


class Copies:
    def __init__(self, sems):
        self.sems = sems
        self.started = []

    def start(self, source, target):
        copy = pltpu.make_async_copy(source, target, self.sems.at[len(self.started)])
        copy.start()
        self.started.append(copy)
        return copy

    def wait(self):
        for copy in self.started:
            copy.wait()


def forward_kernel(
    recv_hbm, w2t_hbm, w3t_hbm, pre_hbm, act_hbm, out_hbm,
    recv_ref, w2t_ref, w3t_ref, pre_ref, act_ref, out_ref, in_sems, out_sems,
):
    steps = act_ref.shape[0]
    rows = steps * 2 * PAIR
    loads, stores = Copies(in_sems), Copies(out_sems)
    parts = [pl.ds(i * 2 * PAIR, 2 * PAIR) for i in range(steps)]
    rest = pl.ds(2 * rows, STATS)
    stats_load = loads.start(recv_hbm.at[:, rest], recv_ref.at[:, pl.ds(rows, STATS)])
    row_loads = [loads.start(recv_hbm.at[:, parts[0]], recv_ref.at[:, parts[0]])]
    w2t_load = loads.start(w2t_hbm, w2t_ref)
    for part in parts[1:]:
        row_loads.append(loads.start(recv_hbm.at[:, part], recv_ref.at[:, part]))
    w3t_load = loads.start(w3t_hbm, w3t_ref)
    stats_load.wait()
    stats = stat_sum(recv_ref[:, rows:, :])
    w2t_load.wait()
    for i in range(steps):
        row_loads[i].wait()
        pre = dot(w2t_ref[...], hidden_rows(recv_ref.at[:, parts[i]]), NN) * reciprocal(stats, i)
        pre_ref[i] = pre
        stores.start(pre_ref.at[i], pre_hbm.at[i])
        hyper = jnp.tanh(pre * (root_scale + (root_scale * cubic_term) * (pre * pre)))
        half = 0.5 * pre
        act_ref[i] = (half + half * hyper).astype(BF16)
    w3t_load.wait()
    for i in range(steps):
        third = dot(w3t_ref[...], act_ref[i], NN).astype(BF16)
        out_ref[:, i * 2 * PAIR : (i + 1) * 2 * PAIR, :] = by_peer(third)
        stores.start(out_ref.at[:, parts[i]], out_hbm.at[:, parts[i]])
    stores.start(act_ref, act_hbm)
    stores.wait()


def backward_kernel(
    y_ref, recv_hbm, pre_hbm, act_hbm, w3_hbm, grads_hbm, dpre_hbm, inner_ref,
    recv_ref, pre_ref, act_ref, w3_ref, dpre_ref, scaled_ref, grads_ref, in_sems, out_sems,
):
    steps = act_ref.shape[0]
    rows = steps * 2 * PAIR
    y = y_ref[0]
    loads, stores = Copies(in_sems), Copies(out_sems)

    def load_rows(base, size):
        part = pl.ds(base, size)
        return loads.start(recv_hbm.at[:, part], recv_ref.at[:, part])

    stats_load = load_rows(2 * rows, STATS)
    w3_load = loads.start(w3_hbm, w3_ref)
    third_loads = [load_rows(rows + i * 2 * PAIR, 2 * PAIR) for i in range(steps)]
    pre_loads = [loads.start(pre_hbm.at[i], pre_ref.at[i]) for i in range(steps)]
    act_load = loads.start(act_hbm, act_ref)
    mixed_load = load_rows(0, rows)
    stats_load.wait()
    stats = stat_sum(recv_ref[:, 2 * rows :, :])
    w3_load.wait()
    for i in range(steps):
        third_loads[i].wait()
        pre_loads[i].wait()
        dact = dot(w3_ref[0], hidden_rows(recv_ref.at[:, pl.ds(rows + i * 2 * PAIR, 2 * PAIR)]), NN)
        pre = pre_ref[i]
        square = pre * pre
        hyper = jnp.tanh(pre * (root_scale + (root_scale * cubic_term) * square))
        slope = (0.5 + 0.5 * hyper) + (0.5 * pre) * (1.0 - hyper * hyper) * (
            root_scale + (3.0 * root_scale * cubic_term) * square
        )
        dpre = dact * slope
        inner_ref[:, i * STEP : (i + 1) * STEP] = jnp.sum(dpre * pre, axis=0, keepdims=True)
        dpre_ref[i] = dpre.astype(BF16)
        scaled_ref[i] = (dpre * reciprocal(stats, i)).astype(BF16)
    act_load.wait()
    mixed_load.wait()
    dthird = hidden_rows(recv_ref.at[:, pl.ds(rows, rows)])
    scaled = jnp.concatenate([scaled_ref[i] for i in range(steps)], axis=1)
    z_size, y_size, part_rows, _ = grads_ref.shape
    half = z_size // 2
    size = half * part_rows
    for r in range(2 * y_size):
        z = pl.ds(r % 2 * half, half)
        act = jnp.concatenate([act_ref[i, r * size : (r + 1) * size, :] for i in range(steps)], axis=1)
        third = dot(act, dthird, NT).astype(BF16)
        grads_ref[z, r // 2, :, HBS:] = third.reshape(half, part_rows, HBS)
        sources = pl.ds(r * (size // PAIR), size // PAIR)
        mixed = hidden_rows(recv_ref.at[sources, pl.ds(0, rows)])
        second = dot(mixed, scaled, NT).astype(BF16)
        grads_ref[z, r // 2, :, :HBS] = second.reshape(half, part_rows, HBS)
        stores.start(grads_ref.at[z, r // 2], grads_hbm.at[z, lax.rem(r // 2 + y, y_size)])
    stores.start(dpre_ref, dpre_hbm)
    stores.wait()


def dmixed_kernel(dpre_ref, inner_ref, w2_ref, out_ref):
    steps = dpre_ref.shape[0]
    for i in range(steps):
        dmixed = dot(w2_ref[0], dpre_ref[i], NN).astype(BF16)
        out_ref[:, i * 2 * PAIR : (i + 1) * 2 * PAIR, :] = by_peer(dmixed)
    rest = stat_rows(inner_ref[...], 2 * steps)
    out_ref[:, steps * 2 * PAIR :, :] = jnp.broadcast_to(rest[None], (PEERS, STATS, LANES))


def model_rows(ref, chunks, a):
    parts = []
    for i in range(chunks):
        start = i * PAIR + a * EB
        parts.append(ref[:, start : start + EB, :].reshape(HB * EB, LANES))
    return jnp.concatenate(parts, axis=1)


def columns(stats, chunks):
    turned = stats.T
    parts = [turned[:, 2 * i : 2 * i + 1] + turned[:, 2 * i + 1 : 2 * i + 2] for i in range(chunks)]
    return jnp.concatenate(parts, axis=0)


def output_kernel(recv_ref, x_ref, w4_ref, out_ref):
    chunks = x_ref.shape[0] // LANES
    for a in range(2):
        feats = slice(a * BS, (a + 1) * BS)
        branch = dot(model_rows(recv_ref, chunks, a), w4_ref[a], TN)
        out_ref[:, feats] = (x_ref[:, feats].astype(F32) + branch).astype(BF16)


def fourth_kernel(y_ref, recv_ref, cot_ref, x_ref, gain_ref, stats_ref, own_ref, other_ref, normed_ref):
    chunks = cot_ref.shape[0] // LANES
    z_size = own_ref.shape[0]
    rows = HB * EB // PEERS
    for a in range(2):
        grad = dot(model_rows(recv_ref, chunks, a), cot_ref[:, a * BS : (a + 1) * BS], NN).astype(BF16)
        grad = grad.reshape(PEERS, rows, BS)
        part = slice(a * rows, (a + 1) * rows)
        own_ref[:, part, :] = jnp.where(y_ref[0] == 0, grad[:z_size], grad[z_size:])
        other_ref[:, part, :] = jnp.where(y_ref[0] == 0, grad[z_size:], grad[:z_size])
    inverse = lax.rsqrt(columns(stat_sum(stats_ref[...]), chunks) / MODEL_WIDTH + epsilon)
    normed_ref[...] = (x_ref[...].astype(F32) * inverse * gain_ref[...]).astype(BF16)


def pair_kernel(z_ref, own_ref, other_ref, *out_refs):
    size = len(out_refs)
    for k, out_ref in enumerate(out_refs):
        z = lax.rem(z_ref[0] + k, size)
        out_ref[...] = (own_ref[z].astype(F32) + other_ref[z].astype(F32)).astype(BF16)


def fourth_sum_kernel(scale, *refs):
    total = refs[0][...].astype(F32)
    for ref in refs[1:-1]:
        total = total + ref[...].astype(F32)
    refs[-1][...] = (total * scale).reshape(refs[-1].shape)


def first_kernel(recv_hbm, normed_hbm, out_ref, recv_ref, normed_ref, sems):
    chunks = normed_ref.shape[0] // LANES
    loads = Copies(sems)
    for a in range(2):
        feats = pl.ds(a * BS, BS)
        loads.start(normed_hbm.at[:, feats], normed_ref.at[:, feats])
    part = pl.ds(0, chunks * PAIR)
    loads.start(recv_hbm.at[:, part], recv_ref)
    loads.wait()
    rows = BS // PEERS
    for a in range(2):
        dfirst = model_rows(recv_ref, chunks, a)
        grad = dot(dfirst, normed_ref[:, a * BS : (a + 1) * BS], NN).astype(BF16).T
        for half in range(2):
            base = (2 * a + half) * rows
            value = grad[:, half * BS : (half + 1) * BS]
            out_ref[:, base : base + rows, :] = value.reshape(PEERS, rows, BS)


def token_kernel(recv_ref, stats_ref, x_ref, gain_ref, w1_ref, cot_ref, out_ref):
    chunks = x_ref.shape[0] // LANES
    inverse = lax.rsqrt(columns(stat_sum(stats_ref[...]), chunks) / MODEL_WIDTH + epsilon)
    inner = columns(stat_sum(recv_ref[:, chunks * PAIR :, :]), chunks) / MODEL_WIDTH
    for a in range(2):
        feats = slice(a * BS, (a + 1) * BS)
        dfirst = model_rows(recv_ref, chunks, a)
        dnormed = dot(dfirst, w1_ref[a], TT)
        xhat = x_ref[:, feats].astype(F32) * inverse
        change = dnormed * gain_ref[:, feats] - xhat * inner
        out_ref[:, feats] = (cot_ref[:, feats].astype(F32) + inverse * change).astype(BF16)


def first_sum_kernel(scale, recv_ref, first_ref):
    total = jnp.sum(recv_ref[...].astype(F32), axis=0) * scale
    _, rows, _ = first_ref.shape
    for a in range(2):
        for half in range(2):
            base = (2 * a + half) * rows
            first_ref[a, :, half * BS : (half + 1) * BS] = total[base : base + rows]


def finish_kernel(scale, own_ref, other_ref, second_ref, third_ref):
    total = (own_ref[0, 0].astype(F32) + other_ref[...].astype(F32)) * scale
    second_ref[0] = total[:, :HBS]
    third_ref[0] = total[:, HBS:]


def shards(tokens, gain, w_first, w_second, w_third, w_fourth, cotangent):
    element_count, local_width = tokens.shape
    dp = lax.axis_size("dp")
    scale = 1.0 / math.sqrt(element_count * dp)
    gain_row = gain[None, :]
    z_size = dp // 2
    z_groups = [[y * z_size + z for z in range(z_size)] for y in range(2)]
    y_pairs = [(i, (i + z_size) % dp) for i in range(dp)]
    y_index = (lax.axis_index("dp") // z_size).astype(jnp.int32)[None]
    z_index = (lax.axis_index("dp") % z_size).astype(jnp.int32)[None]
    shape = jax.ShapeDtypeStruct
    hidden_flops = 2 * HBS * HBS * element_count
    model_flops = 2 * local_width * HB * EB * element_count
    steps = element_count // STEP
    rows = steps * 2 * PAIR
    sent = shape((PEERS, 2 * rows + STATS, LANES), BF16)
    stepped = shape((steps, HBS, STEP), BF16)
    hbm = pl.BlockSpec(memory_space=pltpu.HBM)
    vmem = pl.BlockSpec(memory_space=pltpu.VMEM)
    smem = pl.BlockSpec(memory_space=pltpu.SMEM)
    params = pltpu.CompilerParams(vmem_limit_bytes=VMEM)

    def cost(flops):
        return pl.CostEstimate(flops=int(flops), bytes_accessed=8 << 20, transcendentals=0)

    def whole(*dims):
        return pl.BlockSpec(dims, lambda i, *_: (0,) * len(dims))

    send = pl.pallas_call(
        head_kernel,
        out_shape=sent,
        in_specs=[hbm, hbm, vmem, hbm, hbm],
        out_specs=hbm,
        scratch_shapes=[
            pltpu.VMEM(tokens.shape, BF16),
            pltpu.VMEM(tokens.shape, BF16),
            pltpu.VMEM(w_first.shape, BF16),
            pltpu.VMEM(w_fourth.shape, BF16),
            pltpu.VMEM(sent.shape, BF16),
            pltpu.SemaphoreType.DMA((2 * steps + 2,)),
            pltpu.SemaphoreType.DMA((2 * steps + 1,)),
        ],
        compiler_params=params,
        cost_estimate=cost(2 * model_flops),
    )(tokens, cotangent, gain_row, w_first, w_fourth)
    recv = lax.all_to_all(send, "tensor", 0, 0, tiled=True)
    turned = shape((HBS, HBS), BF16)
    w_second_t, w_third_t = call(turn_kernel, [turned, turned], (w_second, w_third))
    third_sent = shape((PEERS, rows, LANES), BF16)
    back_sent = shape((PEERS, rows + STATS, LANES), BF16)
    pre_shape = shape(stepped.shape, F32)
    pre, act, send = pl.pallas_call(
        forward_kernel,
        out_shape=[pre_shape, stepped, third_sent],
        in_specs=[hbm] * 3,
        out_specs=[hbm] * 3,
        scratch_shapes=[
            pltpu.VMEM(back_sent.shape, BF16),
            pltpu.VMEM(turned.shape, BF16),
            pltpu.VMEM(turned.shape, BF16),
            pltpu.VMEM(stepped.shape, F32),
            pltpu.VMEM(stepped.shape, BF16),
            pltpu.VMEM(third_sent.shape, BF16),
            pltpu.SemaphoreType.DMA((steps + 3,)),
            pltpu.SemaphoreType.DMA((2 * steps + 1,)),
        ],
        compiler_params=params,
        cost_estimate=cost(2 * hidden_flops),
    )(recv, w_second_t, w_third_t)
    third = lax.all_to_all(send, "tensor", 0, 0, tiled=True)
    grads = shape((z_size, 2, HBS // dp, 2 * HBS), BF16)
    hidden, dpre, inner = pl.pallas_call(
        backward_kernel,
        out_shape=[grads, stepped, shape((1, element_count), F32)],
        in_specs=[smem] + [hbm] * 4,
        out_specs=[hbm, hbm, vmem],
        scratch_shapes=[
            pltpu.VMEM(sent.shape, BF16),
            pltpu.VMEM(stepped.shape, F32),
            pltpu.VMEM(stepped.shape, BF16),
            pltpu.VMEM(w_third.shape, BF16),
            pltpu.VMEM(stepped.shape, BF16),
            pltpu.VMEM(stepped.shape, BF16),
            pltpu.VMEM(grads.shape, BF16),
            pltpu.SemaphoreType.DMA((2 * steps + 4,)),
            pltpu.SemaphoreType.DMA((5,)),
        ],
        compiler_params=params,
        cost_estimate=cost(3 * hidden_flops),
    )(y_index, recv, pre, act, w_third)
    hidden = lax.psum_scatter(hidden, "dp", scatter_dimension=0, axis_index_groups=z_groups, tiled=True)
    send = call(dmixed_kernel, back_sent, (dpre, inner, w_second), flops=hidden_flops)
    send, third = lax.optimization_barrier((send, third))
    back = lax.all_to_all(send, "tensor", 0, 0, tiled=True)

    stats_spec = pl.BlockSpec((PEERS, STATS, LANES), lambda i: (0, 2 * rows // STATS, 0))
    all_tokens = whole(*tokens.shape)
    row = whole(1, local_width)
    part = shape((z_size, PAIR, BS), BF16)
    own, other, normed = pl.pallas_call(
        fourth_kernel,
        out_shape=[part, part, shape(tokens.shape, BF16)],
        grid=(1,),
        in_specs=[smem, whole(*third_sent.shape), all_tokens, all_tokens, row, stats_spec],
        out_specs=[whole(*part.shape), whole(*part.shape), all_tokens],
        compiler_params=params,
        cost_estimate=cost(model_flops),
    )(y_index, third, cotangent, tokens, gain_row, recv)
    other = lax.ppermute(other, "dp", y_pairs)
    block = shape((PAIR, BS), BF16)
    blocks = pl.pallas_call(
        pair_kernel,
        out_shape=[block] * z_size,
        in_specs=[smem, vmem, vmem],
        out_specs=[vmem] * z_size,
        compiler_params=params,
        cost_estimate=cost(0),
    )(z_index, own, other)
    blocks, back = lax.optimization_barrier((blocks, back))
    blocks = [blocks[0]] + [
        lax.ppermute(
            blocks[k], "dp", [(g[z], g[(z + k) % z_size]) for g in z_groups for z in range(z_size)]
        )
        for k in range(1, z_size)
    ]
    output = call(output_kernel, shape(tokens.shape, BF16), (third, tokens, w_fourth), flops=LATE * model_flops)
    first = shape((PEERS, PAIR, BS), BF16)
    first = pl.pallas_call(
        first_kernel,
        out_shape=first,
        in_specs=[hbm, hbm],
        out_specs=vmem,
        scratch_shapes=[
            pltpu.VMEM(third_sent.shape, BF16),
            pltpu.VMEM(tokens.shape, BF16),
            pltpu.SemaphoreType.DMA((3,)),
        ],
        compiler_params=params,
        cost_estimate=cost(model_flops),
    )(back, normed)
    first = lax.all_to_all(first, "dp", 0, 0, tiled=True)
    token_gradient = pl.pallas_call(
        token_kernel,
        out_shape=shape(tokens.shape, BF16),
        grid=(1,),
        in_specs=[whole(*back_sent.shape), stats_spec, all_tokens, row, whole(*w_first.shape), all_tokens],
        out_specs=all_tokens,
        compiler_params=params,
        cost_estimate=cost(LATE * model_flops),
    )(back, recv, tokens, gain_row, w_first, cotangent)
    grad_fourth = call(
        functools.partial(fourth_sum_kernel, scale), shape((2, HB * EB // dp, BS), F32), tuple(blocks)
    )
    grad_first = call(functools.partial(first_sum_kernel, scale), shape((2, BS // dp, HB * EB), F32), (first,))
    hidden, grad_fourth = lax.optimization_barrier((hidden, grad_fourth))
    other = lax.ppermute(hidden[0, 1], "dp", y_pairs)
    part = shape((1, HBS // dp, HBS), F32)
    grad_second, grad_third = call(functools.partial(finish_kernel, scale), [part, part], (hidden, other))
    return output, token_gradient, grad_first, grad_second, grad_third, grad_fourth


def solution(mesh):
    return jax.shard_map(
        shards,
        mesh=mesh,
        in_specs=(
            P("dp", "tensor"),
            P("tensor"),
            P("tensor", None, None),
            P("tensor", None, None),
            P("tensor", None, None),
            P("tensor", None, None),
            P("dp", "tensor"),
        ),
        out_specs=(
            P("dp", "tensor"),
            P("dp", "tensor"),
            P("tensor", "dp", None),
            P("tensor", "dp", None),
            P("tensor", "dp", None),
            P("tensor", "dp", None),
        ),
        check_vma=False,
    )
```

```python
import functools
import math

import jax
import jax.numpy as jnp
from jax import lax
from jax.experimental import pallas as pl
from jax.experimental.pallas import tpu as pltpu
from jax.sharding import PartitionSpec as P

MODEL_WIDTH = 8192
DIAGONAL_BLOCKS = 32
HBS = 1024
HB = 16
BS = 256
EB = 32
PEERS = 16
PAIR = 2 * EB
LANES = 128
STATS = 16
STEP = 256
LATE = 160
VMEM = 58 * 1024 * 1024

epsilon = 1e-05
root_scale = math.sqrt(2.0 / math.pi)
cubic_term = 0.044715

F32 = jnp.float32
BF16 = jnp.bfloat16

NN = (((1,), (0,)), ((), ()))
NT = (((1,), (1,)), ((), ()))
TN = (((0,), (0,)), ((), ()))
TT = (((0,), (1,)), ((), ()))


def dot(a, b, dims):
    return lax.dot_general(a, b, dims, preferred_element_type=F32)


def call(kernel, out_shape, args, scratch=(), flops=0, **extra):
    outs = out_shape if isinstance(out_shape, (list, tuple)) else [out_shape]
    moved = sum(a.size * a.dtype.itemsize for a in args) + sum(
        math.prod(o.shape) * o.dtype.itemsize for o in outs
    )
    return pl.pallas_call(
        kernel,
        out_shape=out_shape,
        in_specs=[pl.BlockSpec(memory_space=pltpu.VMEM)] * len(args),
        out_specs=jax.tree.map(lambda _: pl.BlockSpec(memory_space=pltpu.VMEM), out_shape),
        scratch_shapes=list(scratch),
        compiler_params=pltpu.CompilerParams(vmem_limit_bytes=VMEM),
        cost_estimate=pl.CostEstimate(flops=int(flops), bytes_accessed=int(moved), transcendentals=0),
        **extra,
    )(*args)


def stat_rows(value, chunks):
    high = value.astype(BF16).astype(F32)
    low = value - high
    rows = []
    for i in range(chunks):
        part = slice(i * LANES, (i + 1) * LANES)
        rows += [high[:, part], low[:, part]]
    rows.append(jnp.zeros((STATS - 2 * chunks, LANES), F32))
    return jnp.concatenate(rows, axis=0).astype(BF16)


def stat_sum(rows):
    return jnp.sum(rows.astype(F32), axis=0)


def head_kernel(
    x_hbm, cot_hbm, gain_ref, w1_hbm, w4_hbm, out_hbm, x_ref, cot_ref, w1_ref, w4_ref, out_ref, in_sems, out_sems
):
    steps = x_ref.shape[0] // STEP
    rows = steps * 2 * PAIR
    loads, stores = [], []
    weights = [
        pltpu.make_async_copy(source, target, in_sems.at[2 * steps + k])
        for k, (source, target) in enumerate(((w1_hbm, w1_ref), (w4_hbm, w4_ref)))
    ]
    weights[0].start()
    for i in range(steps):
        part = pl.ds(i * STEP, STEP)
        for k, (source, target) in enumerate(((x_hbm, x_ref), (cot_hbm, cot_ref))):
            loads.append(pltpu.make_async_copy(source.at[part], target.at[part], in_sems.at[2 * i + k]))
    for copy in loads[:1] + weights[1:] + loads[1:]:
        copy.start()

    def store(base, size):
        part = pl.ds(base, size)
        copy = pltpu.make_async_copy(out_ref.at[:, part], out_hbm.at[:, part], out_sems.at[len(stores)])
        copy.start()
        stores.append(copy)

    weights[0].wait()
    turned = [w1_ref[a].T for a in range(2)]
    totals = []
    for i in range(steps):
        part = slice(i * STEP, (i + 1) * STEP)
        loads[2 * i].wait()
        x = x_ref[part, :].astype(F32)
        scaled = (x * gain_ref[...]).astype(BF16)
        base = i * 2 * PAIR
        for a in range(2):
            first = dot(turned[a], scaled[:, a * BS : (a + 1) * BS], NT).astype(BF16)
            for k in range(2):
                start = base + k * PAIR + a * EB
                value = first[:, k * LANES : (k + 1) * LANES]
                out_ref[:, start : start + EB, :] = value.reshape(PEERS, EB, LANES)
        store(base, 2 * PAIR)
        loads[2 * i + 1].wait()
        if i == 0:
            weights[1].wait()
        for a in range(2):
            dgathered = dot(w4_ref[a], cot_ref[part, a * BS : (a + 1) * BS], NT).astype(BF16)
            for k in range(2):
                start = rows + base + k * PAIR + a * EB
                value = dgathered[:, k * LANES : (k + 1) * LANES]
                out_ref[:, start : start + EB, :] = value.reshape(PEERS, EB, LANES)
        store(rows + base, 2 * PAIR)
        squares = x * x
        folded = squares[:, :LANES]
        for k in range(1, squares.shape[1] // LANES):
            folded = folded + squares[:, k * LANES : (k + 1) * LANES]
        totals.append(jnp.sum(folded.T, axis=0, keepdims=True))
    stats = stat_rows(jnp.concatenate(totals, axis=1), 2 * steps)
    out_ref[:, 2 * rows :, :] = jnp.broadcast_to(stats[None], (PEERS, STATS, LANES))
    store(2 * rows, STATS)
    for copy in stores:
        copy.wait()


def reciprocal(stats, i):
    rows = stats[4 * i : 4 * i + 4]
    total = jnp.concatenate([rows[0:1] + rows[1:2], rows[2:3] + rows[3:4]], axis=1)
    return lax.rsqrt(total / MODEL_WIDTH + epsilon)


def hidden_rows(ref):
    sources, rows, _ = ref.shape
    parts = [
        ref[:, i * PAIR : (i + 1) * PAIR, :].reshape(sources * PAIR, LANES) for i in range(rows // PAIR)
    ]
    return jnp.concatenate(parts, axis=1)


def turn_kernel(w2_ref, w3_ref, w2t_ref, w3t_ref):
    w2t_ref[...] = w2_ref[0].T
    w3t_ref[...] = w3_ref[0].T


def by_peer(value):
    parts = [value[:, k * LANES : (k + 1) * LANES].reshape(PEERS, PAIR, LANES) for k in range(2)]
    return jnp.concatenate(parts, axis=1)


class Copies:
    def __init__(self, sems):
        self.sems = sems
        self.started = []

    def start(self, source, target):
        copy = pltpu.make_async_copy(source, target, self.sems.at[len(self.started)])
        copy.start()
        self.started.append(copy)
        return copy

    def wait(self):
        for copy in self.started:
            copy.wait()


def forward_kernel(
    recv_hbm, w2t_hbm, w3t_hbm, pre_hbm, act_hbm, out_hbm,
    recv_ref, w2t_ref, w3t_ref, pre_ref, act_ref, out_ref, in_sems, out_sems,
):
    steps = act_ref.shape[0]
    rows = steps * 2 * PAIR
    loads, stores = Copies(in_sems), Copies(out_sems)
    parts = [pl.ds(i * 2 * PAIR, 2 * PAIR) for i in range(steps)]
    rest = pl.ds(2 * rows, STATS)
    stats_load = loads.start(recv_hbm.at[:, rest], recv_ref.at[:, pl.ds(rows, STATS)])
    row_loads = [loads.start(recv_hbm.at[:, parts[0]], recv_ref.at[:, parts[0]])]
    w2t_load = loads.start(w2t_hbm, w2t_ref)
    for part in parts[1:]:
        row_loads.append(loads.start(recv_hbm.at[:, part], recv_ref.at[:, part]))
    w3t_load = loads.start(w3t_hbm, w3t_ref)
    stats_load.wait()
    stats = stat_sum(recv_ref[:, rows:, :])
    w2t_load.wait()
    for i in range(steps):
        row_loads[i].wait()
        pre = dot(w2t_ref[...], hidden_rows(recv_ref.at[:, parts[i]]), NN) * reciprocal(stats, i)
        pre_ref[i] = pre
        stores.start(pre_ref.at[i], pre_hbm.at[i])
        hyper = jnp.tanh(pre * (root_scale + (root_scale * cubic_term) * (pre * pre)))
        half = 0.5 * pre
        act_ref[i] = (half + half * hyper).astype(BF16)
    w3t_load.wait()
    for i in range(steps):
        third = dot(w3t_ref[...], act_ref[i], NN).astype(BF16)
        out_ref[:, i * 2 * PAIR : (i + 1) * 2 * PAIR, :] = by_peer(third)
        stores.start(out_ref.at[:, parts[i]], out_hbm.at[:, parts[i]])
    stores.start(act_ref, act_hbm)
    stores.wait()


def backward_kernel(
    y_ref, recv_hbm, pre_hbm, act_hbm, w3_hbm, grads_hbm, dpre_hbm, inner_ref,
    recv_ref, pre_ref, act_ref, w3_ref, dpre_ref, scaled_ref, grads_ref, in_sems, out_sems,
):
    steps = act_ref.shape[0]
    rows = steps * 2 * PAIR
    y = y_ref[0]
    loads, stores = Copies(in_sems), Copies(out_sems)

    def load_rows(base, size):
        part = pl.ds(base, size)
        return loads.start(recv_hbm.at[:, part], recv_ref.at[:, part])

    stats_load = load_rows(2 * rows, STATS)
    w3_load = loads.start(w3_hbm, w3_ref)
    third_loads = [load_rows(rows + i * 2 * PAIR, 2 * PAIR) for i in range(steps)]
    pre_loads = [loads.start(pre_hbm.at[i], pre_ref.at[i]) for i in range(steps)]
    act_load = loads.start(act_hbm, act_ref)
    mixed_load = load_rows(0, rows)
    stats_load.wait()
    stats = stat_sum(recv_ref[:, 2 * rows :, :])
    w3_load.wait()
    for i in range(steps):
        third_loads[i].wait()
        pre_loads[i].wait()
        dact = dot(w3_ref[0], hidden_rows(recv_ref.at[:, pl.ds(rows + i * 2 * PAIR, 2 * PAIR)]), NN)
        pre = pre_ref[i]
        square = pre * pre
        hyper = jnp.tanh(pre * (root_scale + (root_scale * cubic_term) * square))
        slope = (0.5 + 0.5 * hyper) + (0.5 * pre) * (1.0 - hyper * hyper) * (
            root_scale + (3.0 * root_scale * cubic_term) * square
        )
        dpre = dact * slope
        inner_ref[:, i * STEP : (i + 1) * STEP] = jnp.sum(dpre * pre, axis=0, keepdims=True)
        dpre_ref[i] = dpre.astype(BF16)
        scaled_ref[i] = (dpre * reciprocal(stats, i)).astype(BF16)
    act_load.wait()
    mixed_load.wait()
    dthird = hidden_rows(recv_ref.at[:, pl.ds(rows, rows)])
    scaled = jnp.concatenate([scaled_ref[i] for i in range(steps)], axis=1)
    z_size, y_size, part_rows, _ = grads_ref.shape
    half = z_size // 2
    size = half * part_rows
    for r in range(2 * y_size):
        z = pl.ds(r % 2 * half, half)
        act = jnp.concatenate([act_ref[i, r * size : (r + 1) * size, :] for i in range(steps)], axis=1)
        third = dot(act, dthird, NT).astype(BF16)
        grads_ref[z, r // 2, :, HBS:] = third.reshape(half, part_rows, HBS)
        sources = pl.ds(r * (size // PAIR), size // PAIR)
        mixed = hidden_rows(recv_ref.at[sources, pl.ds(0, rows)])
        second = dot(mixed, scaled, NT).astype(BF16)
        grads_ref[z, r // 2, :, :HBS] = second.reshape(half, part_rows, HBS)
        stores.start(grads_ref.at[z, r // 2], grads_hbm.at[z, lax.rem(r // 2 + y, y_size)])
    stores.start(dpre_ref, dpre_hbm)
    stores.wait()


def dmixed_kernel(dpre_ref, inner_ref, w2_ref, out_ref):
    steps = dpre_ref.shape[0]
    for i in range(steps):
        dmixed = dot(w2_ref[0], dpre_ref[i], NN).astype(BF16)
        out_ref[:, i * 2 * PAIR : (i + 1) * 2 * PAIR, :] = by_peer(dmixed)
    rest = stat_rows(inner_ref[...], 2 * steps)
    out_ref[:, steps * 2 * PAIR :, :] = jnp.broadcast_to(rest[None], (PEERS, STATS, LANES))


def model_rows(ref, chunks, a):
    parts = []
    for i in range(chunks):
        start = i * PAIR + a * EB
        parts.append(ref[:, start : start + EB, :].reshape(HB * EB, LANES))
    return jnp.concatenate(parts, axis=1)


def columns(stats, chunks):
    turned = stats.T
    parts = [turned[:, 2 * i : 2 * i + 1] + turned[:, 2 * i + 1 : 2 * i + 2] for i in range(chunks)]
    return jnp.concatenate(parts, axis=0)


def output_kernel(recv_ref, x_ref, w4_ref, out_ref):
    chunks = x_ref.shape[0] // LANES
    for a in range(2):
        feats = slice(a * BS, (a + 1) * BS)
        branch = dot(model_rows(recv_ref, chunks, a), w4_ref[a], TN)
        out_ref[:, feats] = (x_ref[:, feats].astype(F32) + branch).astype(BF16)


def fourth_kernel(y_ref, recv_ref, cot_ref, x_ref, gain_ref, stats_ref, own_ref, other_ref, normed_ref):
    chunks = cot_ref.shape[0] // LANES
    z_size = own_ref.shape[0]
    rows = HB * EB // PEERS
    for a in range(2):
        grad = dot(model_rows(recv_ref, chunks, a), cot_ref[:, a * BS : (a + 1) * BS], NN).astype(BF16)
        grad = grad.reshape(PEERS, rows, BS)
        part = slice(a * rows, (a + 1) * rows)
        own_ref[:, part, :] = jnp.where(y_ref[0] == 0, grad[:z_size], grad[z_size:])
        other_ref[:, part, :] = jnp.where(y_ref[0] == 0, grad[z_size:], grad[:z_size])
    inverse = lax.rsqrt(columns(stat_sum(stats_ref[...]), chunks) / MODEL_WIDTH + epsilon)
    normed_ref[...] = (x_ref[...].astype(F32) * inverse * gain_ref[...]).astype(BF16)


def pair_kernel(first_own, first_other, fourth_own, fourth_other, out_ref):
    out_ref[:, :PAIR, :] = (first_own[...].astype(F32) + first_other[...].astype(F32)).astype(BF16)
    out_ref[:, PAIR:, :] = (fourth_own[...].astype(F32) + fourth_other[...].astype(F32)).astype(BF16)


def first_kernel(y_ref, recv_hbm, normed_hbm, own_ref, other_ref, recv_ref, normed_ref, sems):
    chunks = normed_ref.shape[0] // LANES
    z_size = own_ref.shape[0]
    loads = Copies(sems)
    loads.start(normed_hbm, normed_ref)
    loads.start(recv_hbm.at[:, pl.ds(0, chunks * PAIR)], recv_ref)
    loads.wait()
    rows = BS // PEERS
    for a in range(2):
        dfirst = model_rows(recv_ref, chunks, a)
        grad = dot(dfirst, normed_ref[:, a * BS : (a + 1) * BS], NN).astype(BF16).T
        for half in range(2):
            base = (2 * a + half) * rows
            value = grad[:, half * BS : (half + 1) * BS].reshape(PEERS, rows, BS)
            part = slice(base, base + rows)
            own_ref[:, part, :] = jnp.where(y_ref[0] == 0, value[:z_size], value[z_size:])
            other_ref[:, part, :] = jnp.where(y_ref[0] == 0, value[z_size:], value[:z_size])


def token_kernel(recv_ref, stats_ref, x_ref, gain_ref, w1_ref, cot_ref, out_ref):
    chunks = x_ref.shape[0] // LANES
    inverse = lax.rsqrt(columns(stat_sum(stats_ref[...]), chunks) / MODEL_WIDTH + epsilon)
    inner = columns(stat_sum(recv_ref[:, chunks * PAIR :, :]), chunks) / MODEL_WIDTH
    for a in range(2):
        feats = slice(a * BS, (a + 1) * BS)
        dfirst = model_rows(recv_ref, chunks, a)
        dnormed = dot(dfirst, w1_ref[a], TT)
        xhat = x_ref[:, feats].astype(F32) * inverse
        change = dnormed * gain_ref[:, feats] - xhat * inner
        out_ref[:, feats] = (cot_ref[:, feats].astype(F32) + inverse * change).astype(BF16)


def sum_kernel(scale, recv_ref, first_ref, fourth_ref):
    total = jnp.sum(recv_ref[...].astype(F32), axis=0) * scale
    _, rows, _ = first_ref.shape
    for a in range(2):
        for half in range(2):
            base = (2 * a + half) * rows
            first_ref[a, :, half * BS : (half + 1) * BS] = total[base : base + rows]
    fourth_ref[...] = total[PAIR:].reshape(fourth_ref.shape)


def finish_kernel(scale, own_ref, other_ref, second_ref, third_ref):
    total = (own_ref[0, 0].astype(F32) + other_ref[...].astype(F32)) * scale
    second_ref[0] = total[:, :HBS]
    third_ref[0] = total[:, HBS:]


def shards(tokens, gain, w_first, w_second, w_third, w_fourth, cotangent):
    element_count, local_width = tokens.shape
    dp = lax.axis_size("dp")
    scale = 1.0 / math.sqrt(element_count * dp)
    gain_row = gain[None, :]
    z_size = dp // 2
    z_groups = [[y * z_size + z for z in range(z_size)] for y in range(2)]
    y_pairs = [(i, (i + z_size) % dp) for i in range(dp)]
    y_index = (lax.axis_index("dp") // z_size).astype(jnp.int32)[None]
    shape = jax.ShapeDtypeStruct
    hidden_flops = 2 * HBS * HBS * element_count
    model_flops = 2 * local_width * HB * EB * element_count
    steps = element_count // STEP
    rows = steps * 2 * PAIR
    sent = shape((PEERS, 2 * rows + STATS, LANES), BF16)
    stepped = shape((steps, HBS, STEP), BF16)
    hbm = pl.BlockSpec(memory_space=pltpu.HBM)
    vmem = pl.BlockSpec(memory_space=pltpu.VMEM)
    smem = pl.BlockSpec(memory_space=pltpu.SMEM)
    params = pltpu.CompilerParams(vmem_limit_bytes=VMEM)

    def cost(flops):
        return pl.CostEstimate(flops=int(flops), bytes_accessed=8 << 20, transcendentals=0)

    def whole(*dims):
        return pl.BlockSpec(dims, lambda i, *_: (0,) * len(dims))

    send = pl.pallas_call(
        head_kernel,
        out_shape=sent,
        in_specs=[hbm, hbm, vmem, hbm, hbm],
        out_specs=hbm,
        scratch_shapes=[
            pltpu.VMEM(tokens.shape, BF16),
            pltpu.VMEM(tokens.shape, BF16),
            pltpu.VMEM(w_first.shape, BF16),
            pltpu.VMEM(w_fourth.shape, BF16),
            pltpu.VMEM(sent.shape, BF16),
            pltpu.SemaphoreType.DMA((2 * steps + 2,)),
            pltpu.SemaphoreType.DMA((2 * steps + 1,)),
        ],
        compiler_params=params,
        cost_estimate=cost(2 * model_flops),
    )(tokens, cotangent, gain_row, w_first, w_fourth)
    recv = lax.all_to_all(send, "tensor", 0, 0, tiled=True)
    turned = shape((HBS, HBS), BF16)
    w_second_t, w_third_t = call(turn_kernel, [turned, turned], (w_second, w_third))
    third_sent = shape((PEERS, rows, LANES), BF16)
    back_sent = shape((PEERS, rows + STATS, LANES), BF16)
    pre_shape = shape(stepped.shape, F32)
    pre, act, send = pl.pallas_call(
        forward_kernel,
        out_shape=[pre_shape, stepped, third_sent],
        in_specs=[hbm] * 3,
        out_specs=[hbm] * 3,
        scratch_shapes=[
            pltpu.VMEM(back_sent.shape, BF16),
            pltpu.VMEM(turned.shape, BF16),
            pltpu.VMEM(turned.shape, BF16),
            pltpu.VMEM(stepped.shape, F32),
            pltpu.VMEM(stepped.shape, BF16),
            pltpu.VMEM(third_sent.shape, BF16),
            pltpu.SemaphoreType.DMA((steps + 3,)),
            pltpu.SemaphoreType.DMA((2 * steps + 1,)),
        ],
        compiler_params=params,
        cost_estimate=cost(2 * hidden_flops),
    )(recv, w_second_t, w_third_t)
    third = lax.all_to_all(send, "tensor", 0, 0, tiled=True)
    grads = shape((z_size, 2, HBS // dp, 2 * HBS), BF16)
    hidden, dpre, inner = pl.pallas_call(
        backward_kernel,
        out_shape=[grads, stepped, shape((1, element_count), F32)],
        in_specs=[smem] + [hbm] * 4,
        out_specs=[hbm, hbm, vmem],
        scratch_shapes=[
            pltpu.VMEM(sent.shape, BF16),
            pltpu.VMEM(stepped.shape, F32),
            pltpu.VMEM(stepped.shape, BF16),
            pltpu.VMEM(w_third.shape, BF16),
            pltpu.VMEM(stepped.shape, BF16),
            pltpu.VMEM(stepped.shape, BF16),
            pltpu.VMEM(grads.shape, BF16),
            pltpu.SemaphoreType.DMA((2 * steps + 4,)),
            pltpu.SemaphoreType.DMA((5,)),
        ],
        compiler_params=params,
        cost_estimate=cost(3 * hidden_flops),
    )(y_index, recv, pre, act, w_third)
    hidden = lax.psum_scatter(hidden, "dp", scatter_dimension=0, axis_index_groups=z_groups, tiled=True)
    send = call(dmixed_kernel, back_sent, (dpre, inner, w_second), flops=hidden_flops)
    send, third = lax.optimization_barrier((send, third))
    back = lax.all_to_all(send, "tensor", 0, 0, tiled=True)

    stats_spec = pl.BlockSpec((PEERS, STATS, LANES), lambda i: (0, 2 * rows // STATS, 0))
    all_tokens = whole(*tokens.shape)
    row = whole(1, local_width)
    part = shape((z_size, PAIR, BS), BF16)
    own, other, normed = pl.pallas_call(
        fourth_kernel,
        out_shape=[part, part, shape(tokens.shape, BF16)],
        grid=(1,),
        in_specs=[smem, whole(*third_sent.shape), all_tokens, all_tokens, row, stats_spec],
        out_specs=[whole(*part.shape), whole(*part.shape), all_tokens],
        compiler_params=params,
        cost_estimate=cost(model_flops),
    )(y_index, third, cotangent, tokens, gain_row, recv)
    fourths = (own, lax.ppermute(other, "dp", y_pairs))
    output = call(output_kernel, shape(tokens.shape, BF16), (third, tokens, w_fourth), flops=LATE * model_flops)
    own, other = pl.pallas_call(
        first_kernel,
        out_shape=[part, part],
        in_specs=[smem, hbm, hbm],
        out_specs=[vmem, vmem],
        scratch_shapes=[
            pltpu.VMEM(third_sent.shape, BF16),
            pltpu.VMEM(tokens.shape, BF16),
            pltpu.SemaphoreType.DMA((2,)),
        ],
        compiler_params=params,
        cost_estimate=cost(model_flops),
    )(y_index, back, normed)
    firsts = (own, lax.ppermute(other, "dp", y_pairs))
    both = call(pair_kernel, shape((z_size, 2 * PAIR, BS), BF16), firsts + fourths)
    both = lax.all_to_all(both, "dp", 0, 0, axis_index_groups=z_groups, tiled=True)
    token_gradient = pl.pallas_call(
        token_kernel,
        out_shape=shape(tokens.shape, BF16),
        grid=(1,),
        in_specs=[whole(*back_sent.shape), stats_spec, all_tokens, row, whole(*w_first.shape), all_tokens],
        out_specs=all_tokens,
        compiler_params=params,
        cost_estimate=cost(LATE * model_flops),
    )(back, recv, tokens, gain_row, w_first, cotangent)
    grad_first, grad_fourth = call(
        functools.partial(sum_kernel, scale),
        [shape((2, BS // dp, HB * EB), F32), shape((2, HB * EB // dp, BS), F32)],
        (both,),
    )
    other = lax.ppermute(hidden[0, 1], "dp", y_pairs)
    part = shape((1, HBS // dp, HBS), F32)
    grad_second, grad_third = call(functools.partial(finish_kernel, scale), [part, part], (hidden, other))
    return output, token_gradient, grad_first, grad_second, grad_third, grad_fourth


def solution(mesh):
    return jax.shard_map(
        shards,
        mesh=mesh,
        in_specs=(
            P("dp", "tensor"),
            P("tensor"),
            P("tensor", None, None),
            P("tensor", None, None),
            P("tensor", None, None),
            P("tensor", None, None),
            P("dp", "tensor"),
        ),
        out_specs=(
            P("dp", "tensor"),
            P("dp", "tensor"),
            P("tensor", "dp", None),
            P("tensor", "dp", None),
            P("tensor", "dp", None),
            P("tensor", "dp", None),
        ),
        check_vma=False,
    )
```

```python
import functools
import math

import jax
import jax.numpy as jnp
from jax import lax
from jax.experimental import pallas as pl
from jax.experimental.pallas import tpu as pltpu
from jax.sharding import PartitionSpec as P

MODEL_WIDTH = 8192
DIAGONAL_BLOCKS = 32
HBS = 1024
HB = 16
BS = 256
EB = 32
PEERS = 16
PAIR = 2 * EB
LANES = 128
STATS = 16
STEP = 256
LATE = 160
VMEM = 58 * 1024 * 1024

epsilon = 1e-05
root_scale = math.sqrt(2.0 / math.pi)
cubic_term = 0.044715

F32 = jnp.float32
BF16 = jnp.bfloat16

NN = (((1,), (0,)), ((), ()))
NT = (((1,), (1,)), ((), ()))
TN = (((0,), (0,)), ((), ()))
TT = (((0,), (1,)), ((), ()))


def dot(a, b, dims):
    return lax.dot_general(a, b, dims, preferred_element_type=F32)


def call(kernel, out_shape, args, scratch=(), flops=0, **extra):
    outs = out_shape if isinstance(out_shape, (list, tuple)) else [out_shape]
    moved = sum(a.size * a.dtype.itemsize for a in args) + sum(
        math.prod(o.shape) * o.dtype.itemsize for o in outs
    )
    return pl.pallas_call(
        kernel,
        out_shape=out_shape,
        in_specs=[pl.BlockSpec(memory_space=pltpu.VMEM)] * len(args),
        out_specs=jax.tree.map(lambda _: pl.BlockSpec(memory_space=pltpu.VMEM), out_shape),
        scratch_shapes=list(scratch),
        compiler_params=pltpu.CompilerParams(vmem_limit_bytes=VMEM),
        cost_estimate=pl.CostEstimate(flops=int(flops), bytes_accessed=int(moved), transcendentals=0),
        **extra,
    )(*args)


def stat_rows(value, chunks):
    high = value.astype(BF16).astype(F32)
    low = value - high
    rows = []
    for i in range(chunks):
        part = slice(i * LANES, (i + 1) * LANES)
        rows += [high[:, part], low[:, part]]
    rows.append(jnp.zeros((STATS - 2 * chunks, LANES), F32))
    return jnp.concatenate(rows, axis=0).astype(BF16)


def stat_sum(rows):
    return jnp.sum(rows.astype(F32), axis=0)


class Copies:
    def __init__(self, sems):
        self.sems = sems
        self.started = []

    def start(self, source, target):
        copy = pltpu.make_async_copy(source, target, self.sems.at[len(self.started)])
        copy.start()
        self.started.append(copy)
        return copy

    def wait(self):
        for copy in self.started:
            copy.wait()


def head_kernel(x_hbm, gain_ref, w1_hbm, out_hbm, x_ref, w1_ref, out_ref, in_sems, out_sems):
    steps = x_ref.shape[0] // STEP
    loads, stores = Copies(in_sems), Copies(out_sems)
    w1_load = loads.start(w1_hbm, w1_ref)
    parts = [pl.ds(i * STEP, STEP) for i in range(steps)]
    x_loads = [loads.start(x_hbm.at[part], x_ref.at[part]) for part in parts]
    w1_load.wait()
    turned = [w1_ref[a].T for a in range(2)]
    totals = []
    for i in range(steps):
        x_loads[i].wait()
        x = x_ref[parts[i], :].astype(F32)
        scaled = (x * gain_ref[...]).astype(BF16)
        base = i * 2 * PAIR
        for a in range(2):
            first = dot(turned[a], scaled[:, a * BS : (a + 1) * BS], NT).astype(BF16)
            for k in range(2):
                start = base + k * PAIR + a * EB
                value = first[:, k * LANES : (k + 1) * LANES]
                out_ref[:, start : start + EB, :] = value.reshape(PEERS, EB, LANES)
        part = pl.ds(base, 2 * PAIR)
        stores.start(out_ref.at[:, part], out_hbm.at[:, part])
        squares = x * x
        folded = squares[:, :LANES]
        for k in range(1, squares.shape[1] // LANES):
            folded = folded + squares[:, k * LANES : (k + 1) * LANES]
        totals.append(jnp.sum(folded.T, axis=0, keepdims=True))
    rows = steps * 2 * PAIR
    stats = stat_rows(jnp.concatenate(totals, axis=1), 2 * steps)
    out_ref[:, rows:, :] = jnp.broadcast_to(stats[None], (PEERS, STATS, LANES))
    part = pl.ds(rows, STATS)
    stores.start(out_ref.at[:, part], out_hbm.at[:, part])
    stores.wait()


def dgathered_kernel(w4_ref, cot_ref, out_ref):
    chunks = cot_ref.shape[0] // LANES
    for a in range(2):
        dgathered = dot(w4_ref[a], cot_ref[:, a * BS : (a + 1) * BS], NT).astype(BF16)
        for i in range(chunks):
            start = i * PAIR + a * EB
            value = dgathered[:, i * LANES : (i + 1) * LANES]
            out_ref[:, start : start + EB, :] = value.reshape(PEERS, EB, LANES)


def reciprocal(stats, i):
    rows = stats[4 * i : 4 * i + 4]
    total = jnp.concatenate([rows[0:1] + rows[1:2], rows[2:3] + rows[3:4]], axis=1)
    return lax.rsqrt(total / MODEL_WIDTH + epsilon)


def hidden_rows(ref):
    sources, rows, _ = ref.shape
    parts = [
        ref[:, i * PAIR : (i + 1) * PAIR, :].reshape(sources * PAIR, LANES) for i in range(rows // PAIR)
    ]
    return jnp.concatenate(parts, axis=1)


def turn_kernel(w2_ref, w3_ref, w2t_ref, w3t_ref):
    w2t_ref[...] = w2_ref[0].T
    w3t_ref[...] = w3_ref[0].T


def by_peer(value):
    parts = [value[:, k * LANES : (k + 1) * LANES].reshape(PEERS, PAIR, LANES) for k in range(2)]
    return jnp.concatenate(parts, axis=1)


def forward_kernel(
    recv_hbm, w2t_hbm, w3t_hbm, pre_hbm, act_hbm, out_hbm,
    recv_ref, w2t_ref, w3t_ref, pre_ref, act_ref, out_ref, in_sems, out_sems,
):
    steps = act_ref.shape[0]
    rows = steps * 2 * PAIR
    loads, stores = Copies(in_sems), Copies(out_sems)
    parts = [pl.ds(i * 2 * PAIR, 2 * PAIR) for i in range(steps)]
    rest = pl.ds(rows, STATS)
    stats_load = loads.start(recv_hbm.at[:, rest], recv_ref.at[:, rest])
    row_loads = [loads.start(recv_hbm.at[:, parts[0]], recv_ref.at[:, parts[0]])]
    w2t_load = loads.start(w2t_hbm, w2t_ref)
    for part in parts[1:]:
        row_loads.append(loads.start(recv_hbm.at[:, part], recv_ref.at[:, part]))
    w3t_load = loads.start(w3t_hbm, w3t_ref)
    stats_load.wait()
    stats = stat_sum(recv_ref[:, rows:, :])
    w2t_load.wait()
    for i in range(steps):
        row_loads[i].wait()
        pre = dot(w2t_ref[...], hidden_rows(recv_ref.at[:, parts[i]]), NN) * reciprocal(stats, i)
        pre_ref[i] = pre
        stores.start(pre_ref.at[i], pre_hbm.at[i])
        hyper = jnp.tanh(pre * (root_scale + (root_scale * cubic_term) * (pre * pre)))
        half = 0.5 * pre
        act_ref[i] = (half + half * hyper).astype(BF16)
    stores.start(act_ref, act_hbm)
    w3t_load.wait()
    for i in range(steps):
        third = dot(w3t_ref[...], act_ref[i], NN).astype(BF16)
        out_ref[:, i * 2 * PAIR : (i + 1) * 2 * PAIR, :] = by_peer(third)
        stores.start(out_ref.at[:, parts[i]], out_hbm.at[:, parts[i]])
    stores.wait()


def backward_kernel(
    y_ref, recv_hbm, dthird_hbm, pre_hbm, act_hbm, w3_hbm, grads_hbm, dpre_hbm, inner_ref,
    recv_ref, dthird_ref, pre_ref, act_ref, w3_ref, dpre_ref, scaled_ref, grads_ref, in_sems, out_sems,
):
    steps = act_ref.shape[0]
    rows = steps * 2 * PAIR
    y = y_ref[0]
    loads, stores = Copies(in_sems), Copies(out_sems)

    parts = [pl.ds(i * 2 * PAIR, 2 * PAIR) for i in range(steps)]
    rest = pl.ds(rows, STATS)
    stats_load = loads.start(recv_hbm.at[:, rest], recv_ref.at[:, rest])
    w3_load = loads.start(w3_hbm, w3_ref)
    third_loads = [loads.start(dthird_hbm.at[:, part], dthird_ref.at[:, part]) for part in parts]
    pre_loads = [loads.start(pre_hbm.at[i], pre_ref.at[i]) for i in range(steps)]
    act_load = loads.start(act_hbm, act_ref)
    mixed_load = loads.start(recv_hbm.at[:, pl.ds(0, rows)], recv_ref.at[:, pl.ds(0, rows)])
    stats_load.wait()
    stats = stat_sum(recv_ref[:, rows:, :])
    w3_load.wait()
    for i in range(steps):
        third_loads[i].wait()
        pre_loads[i].wait()
        dact = dot(w3_ref[0], hidden_rows(dthird_ref.at[:, parts[i]]), NN)
        pre = pre_ref[i]
        square = pre * pre
        hyper = jnp.tanh(pre * (root_scale + (root_scale * cubic_term) * square))
        slope = (0.5 + 0.5 * hyper) + (0.5 * pre) * (1.0 - hyper * hyper) * (
            root_scale + (3.0 * root_scale * cubic_term) * square
        )
        dpre = dact * slope
        inner_ref[:, i * STEP : (i + 1) * STEP] = jnp.sum(dpre * pre, axis=0, keepdims=True)
        dpre_ref[i] = dpre.astype(BF16)
        scaled_ref[i] = (dpre * reciprocal(stats, i)).astype(BF16)
    act_load.wait()
    mixed_load.wait()
    dthird = hidden_rows(dthird_ref)
    scaled = jnp.concatenate([scaled_ref[i] for i in range(steps)], axis=1)
    z_size, y_size, part_rows, _ = grads_ref.shape
    half = z_size // 2
    size = half * part_rows
    for r in range(2 * y_size):
        z = pl.ds(r % 2 * half, half)
        act = jnp.concatenate([act_ref[i, r * size : (r + 1) * size, :] for i in range(steps)], axis=1)
        third = dot(act, dthird, NT).astype(BF16)
        grads_ref[z, r // 2, :, HBS:] = third.reshape(half, part_rows, HBS)
        sources = pl.ds(r * (size // PAIR), size // PAIR)
        mixed = hidden_rows(recv_ref.at[sources, pl.ds(0, rows)])
        second = dot(mixed, scaled, NT).astype(BF16)
        grads_ref[z, r // 2, :, :HBS] = second.reshape(half, part_rows, HBS)
        stores.start(grads_ref.at[z, r // 2], grads_hbm.at[z, lax.rem(r // 2 + y, y_size)])
    stores.start(dpre_ref, dpre_hbm)
    stores.wait()


def dmixed_kernel(dpre_ref, inner_ref, w2_ref, out_ref):
    steps = dpre_ref.shape[0]
    for i in range(steps):
        dmixed = dot(w2_ref[0], dpre_ref[i], NN).astype(BF16)
        out_ref[:, i * 2 * PAIR : (i + 1) * 2 * PAIR, :] = by_peer(dmixed)
    rest = stat_rows(inner_ref[...], 2 * steps)
    out_ref[:, steps * 2 * PAIR :, :] = jnp.broadcast_to(rest[None], (PEERS, STATS, LANES))


def model_rows(ref, chunks, a):
    parts = []
    for i in range(chunks):
        start = i * PAIR + a * EB
        parts.append(ref[:, start : start + EB, :].reshape(HB * EB, LANES))
    return jnp.concatenate(parts, axis=1)


def columns(stats, chunks):
    turned = stats.T
    parts = [turned[:, 2 * i : 2 * i + 1] + turned[:, 2 * i + 1 : 2 * i + 2] for i in range(chunks)]
    return jnp.concatenate(parts, axis=0)


def output_kernel(recv_ref, x_ref, w4_ref, out_ref):
    chunks = x_ref.shape[0] // LANES
    for a in range(2):
        feats = slice(a * BS, (a + 1) * BS)
        branch = dot(model_rows(recv_ref, chunks, a), w4_ref[a], TN)
        out_ref[:, feats] = (x_ref[:, feats].astype(F32) + branch).astype(BF16)


def fourth_kernel(y_ref, recv_ref, cot_ref, x_ref, gain_ref, stats_ref, own_ref, other_ref, normed_ref):
    chunks = cot_ref.shape[0] // LANES
    z_size = own_ref.shape[0]
    rows = HB * EB // PEERS
    for a in range(2):
        grad = dot(model_rows(recv_ref, chunks, a), cot_ref[:, a * BS : (a + 1) * BS], NN).astype(BF16)
        grad = grad.reshape(PEERS, rows, BS)
        part = slice(a * rows, (a + 1) * rows)
        own_ref[:, part, :] = jnp.where(y_ref[0] == 0, grad[:z_size], grad[z_size:])
        other_ref[:, part, :] = jnp.where(y_ref[0] == 0, grad[z_size:], grad[:z_size])
    inverse = lax.rsqrt(columns(stat_sum(stats_ref[...]), chunks) / MODEL_WIDTH + epsilon)
    normed_ref[...] = (x_ref[...].astype(F32) * inverse * gain_ref[...]).astype(BF16)


def pair_kernel(first_own, first_other, fourth_own, fourth_other, out_ref):
    out_ref[:, :PAIR, :] = (first_own[...].astype(F32) + first_other[...].astype(F32)).astype(BF16)
    out_ref[:, PAIR:, :] = (fourth_own[...].astype(F32) + fourth_other[...].astype(F32)).astype(BF16)


def first_kernel(y_ref, recv_hbm, normed_hbm, own_ref, other_ref, recv_ref, normed_ref, sems):
    chunks = normed_ref.shape[0] // LANES
    z_size = own_ref.shape[0]
    loads = Copies(sems)
    loads.start(normed_hbm, normed_ref)
    loads.start(recv_hbm.at[:, pl.ds(0, chunks * PAIR)], recv_ref)
    loads.wait()
    rows = BS // PEERS
    for a in range(2):
        dfirst = model_rows(recv_ref, chunks, a)
        grad = dot(dfirst, normed_ref[:, a * BS : (a + 1) * BS], NN).astype(BF16).T
        for half in range(2):
            base = (2 * a + half) * rows
            value = grad[:, half * BS : (half + 1) * BS].reshape(PEERS, rows, BS)
            part = slice(base, base + rows)
            own_ref[:, part, :] = jnp.where(y_ref[0] == 0, value[:z_size], value[z_size:])
            other_ref[:, part, :] = jnp.where(y_ref[0] == 0, value[z_size:], value[:z_size])


def token_kernel(recv_ref, stats_ref, x_ref, gain_ref, w1_ref, cot_ref, out_ref):
    chunks = x_ref.shape[0] // LANES
    inverse = lax.rsqrt(columns(stat_sum(stats_ref[...]), chunks) / MODEL_WIDTH + epsilon)
    inner = columns(stat_sum(recv_ref[:, chunks * PAIR :, :]), chunks) / MODEL_WIDTH
    for a in range(2):
        feats = slice(a * BS, (a + 1) * BS)
        dfirst = model_rows(recv_ref, chunks, a)
        dnormed = dot(dfirst, w1_ref[a], TT)
        xhat = x_ref[:, feats].astype(F32) * inverse
        change = dnormed * gain_ref[:, feats] - xhat * inner
        out_ref[:, feats] = (cot_ref[:, feats].astype(F32) + inverse * change).astype(BF16)


def sum_kernel(scale, recv_ref, first_ref, fourth_ref):
    total = jnp.sum(recv_ref[...].astype(F32), axis=0) * scale
    _, rows, _ = first_ref.shape
    for a in range(2):
        for half in range(2):
            base = (2 * a + half) * rows
            first_ref[a, :, half * BS : (half + 1) * BS] = total[base : base + rows]
    fourth_ref[...] = total[PAIR:].reshape(fourth_ref.shape)


def finish_kernel(scale, own_ref, other_ref, second_ref, third_ref):
    total = (own_ref[0, 0].astype(F32) + other_ref[...].astype(F32)) * scale
    second_ref[0] = total[:, :HBS]
    third_ref[0] = total[:, HBS:]


def shards(tokens, gain, w_first, w_second, w_third, w_fourth, cotangent):
    element_count, local_width = tokens.shape
    dp = lax.axis_size("dp")
    scale = 1.0 / math.sqrt(element_count * dp)
    gain_row = gain[None, :]
    z_size = dp // 2
    z_groups = [[y * z_size + z for z in range(z_size)] for y in range(2)]
    y_pairs = [(i, (i + z_size) % dp) for i in range(dp)]
    y_index = (lax.axis_index("dp") // z_size).astype(jnp.int32)[None]
    shape = jax.ShapeDtypeStruct
    hidden_flops = 2 * HBS * HBS * element_count
    model_flops = 2 * local_width * HB * EB * element_count
    steps = element_count // STEP
    rows = steps * 2 * PAIR
    plain_sent = shape((PEERS, rows, LANES), BF16)
    stats_sent = shape((PEERS, rows + STATS, LANES), BF16)
    stepped = shape((steps, HBS, STEP), BF16)
    hbm = pl.BlockSpec(memory_space=pltpu.HBM)
    vmem = pl.BlockSpec(memory_space=pltpu.VMEM)
    smem = pl.BlockSpec(memory_space=pltpu.SMEM)
    params = pltpu.CompilerParams(vmem_limit_bytes=VMEM)

    def cost(flops):
        return pl.CostEstimate(flops=int(flops), bytes_accessed=8 << 20, transcendentals=0)

    def whole(*dims):
        return pl.BlockSpec(dims, lambda i, *_: (0,) * len(dims))

    def exchange(value):
        return lax.all_to_all(value, "tensor", 0, 0, tiled=True)

    send = pl.pallas_call(
        head_kernel,
        out_shape=stats_sent,
        in_specs=[hbm, vmem, hbm],
        out_specs=hbm,
        scratch_shapes=[
            pltpu.VMEM(tokens.shape, BF16),
            pltpu.VMEM(w_first.shape, BF16),
            pltpu.VMEM(stats_sent.shape, BF16),
            pltpu.SemaphoreType.DMA((steps + 1,)),
            pltpu.SemaphoreType.DMA((steps + 1,)),
        ],
        compiler_params=params,
        cost_estimate=cost(model_flops),
    )(tokens, gain_row, w_first)
    recv = exchange(send)
    send = call(dgathered_kernel, plain_sent, (w_fourth, cotangent), flops=model_flops)
    dthird = exchange(lax.optimization_barrier((send, recv))[0])
    turned = shape((HBS, HBS), BF16)
    w_second_t, w_third_t = call(turn_kernel, [turned, turned], (w_second, w_third))
    pre_shape = shape(stepped.shape, F32)
    pre, act, send = pl.pallas_call(
        forward_kernel,
        out_shape=[pre_shape, stepped, plain_sent],
        in_specs=[hbm] * 3,
        out_specs=[hbm] * 3,
        scratch_shapes=[
            pltpu.VMEM(stats_sent.shape, BF16),
            pltpu.VMEM(turned.shape, BF16),
            pltpu.VMEM(turned.shape, BF16),
            pltpu.VMEM(stepped.shape, F32),
            pltpu.VMEM(stepped.shape, BF16),
            pltpu.VMEM(plain_sent.shape, BF16),
            pltpu.SemaphoreType.DMA((steps + 3,)),
            pltpu.SemaphoreType.DMA((2 * steps + 1,)),
        ],
        compiler_params=params,
        cost_estimate=cost(2 * hidden_flops),
    )(recv, w_second_t, w_third_t)
    third = exchange(lax.optimization_barrier((send, dthird))[0])
    grads = shape((z_size, 2, HBS // dp, 2 * HBS), BF16)
    hidden, dpre, inner = pl.pallas_call(
        backward_kernel,
        out_shape=[grads, stepped, shape((1, element_count), F32)],
        in_specs=[smem] + [hbm] * 5,
        out_specs=[hbm, hbm, vmem],
        scratch_shapes=[
            pltpu.VMEM(stats_sent.shape, BF16),
            pltpu.VMEM(plain_sent.shape, BF16),
            pltpu.VMEM(stepped.shape, F32),
            pltpu.VMEM(stepped.shape, BF16),
            pltpu.VMEM(w_third.shape, BF16),
            pltpu.VMEM(stepped.shape, BF16),
            pltpu.VMEM(stepped.shape, BF16),
            pltpu.VMEM(grads.shape, BF16),
            pltpu.SemaphoreType.DMA((2 * steps + 4,)),
            pltpu.SemaphoreType.DMA((5,)),
        ],
        compiler_params=params,
        cost_estimate=cost(3 * hidden_flops),
    )(y_index, recv, dthird, pre, act, w_third)
    hidden = lax.psum_scatter(hidden, "dp", scatter_dimension=0, axis_index_groups=z_groups, tiled=True)
    send = call(dmixed_kernel, stats_sent, (dpre, inner, w_second), flops=hidden_flops)
    send, third = lax.optimization_barrier((send, third))
    back = exchange(send)

    stats_spec = pl.BlockSpec((PEERS, STATS, LANES), lambda i: (0, rows // STATS, 0))
    all_tokens = whole(*tokens.shape)
    row = whole(1, local_width)
    part = shape((z_size, PAIR, BS), BF16)
    own, other, normed = pl.pallas_call(
        fourth_kernel,
        out_shape=[part, part, shape(tokens.shape, BF16)],
        grid=(1,),
        in_specs=[smem, whole(*plain_sent.shape), all_tokens, all_tokens, row, stats_spec],
        out_specs=[whole(*part.shape), whole(*part.shape), all_tokens],
        compiler_params=params,
        cost_estimate=cost(model_flops),
    )(y_index, third, cotangent, tokens, gain_row, recv)
    fourths = (own, lax.ppermute(other, "dp", y_pairs))
    output = call(output_kernel, shape(tokens.shape, BF16), (third, tokens, w_fourth), flops=LATE * model_flops)
    own, other = pl.pallas_call(
        first_kernel,
        out_shape=[part, part],
        in_specs=[smem, hbm, hbm],
        out_specs=[vmem, vmem],
        scratch_shapes=[
            pltpu.VMEM(plain_sent.shape, BF16),
            pltpu.VMEM(tokens.shape, BF16),
            pltpu.SemaphoreType.DMA((2,)),
        ],
        compiler_params=params,
        cost_estimate=cost(model_flops),
    )(y_index, back, normed)
    firsts = (own, lax.ppermute(other, "dp", y_pairs))
    both = call(pair_kernel, shape((z_size, 2 * PAIR, BS), BF16), firsts + fourths)
    both = lax.all_to_all(both, "dp", 0, 0, axis_index_groups=z_groups, tiled=True)
    token_gradient = pl.pallas_call(
        token_kernel,
        out_shape=shape(tokens.shape, BF16),
        grid=(1,),
        in_specs=[whole(*stats_sent.shape), stats_spec, all_tokens, row, whole(*w_first.shape), all_tokens],
        out_specs=all_tokens,
        compiler_params=params,
        cost_estimate=cost(LATE * model_flops),
    )(back, recv, tokens, gain_row, w_first, cotangent)
    other = lax.ppermute(hidden[0, 1], "dp", y_pairs)
    part = shape((1, HBS // dp, HBS), F32)
    grad_second, grad_third = call(functools.partial(finish_kernel, scale), [part, part], (hidden, other))
    both, grad_second, grad_third = lax.optimization_barrier((both, grad_second, grad_third))
    grad_first, grad_fourth = call(
        functools.partial(sum_kernel, scale),
        [shape((2, BS // dp, HB * EB), F32), shape((2, HB * EB // dp, BS), F32)],
        (both,),
    )
    return output, token_gradient, grad_first, grad_second, grad_third, grad_fourth


def solution(mesh):
    return jax.shard_map(
        shards,
        mesh=mesh,
        in_specs=(
            P("dp", "tensor"),
            P("tensor"),
            P("tensor", None, None),
            P("tensor", None, None),
            P("tensor", None, None),
            P("tensor", None, None),
            P("dp", "tensor"),
        ),
        out_specs=(
            P("dp", "tensor"),
            P("dp", "tensor"),
            P("tensor", "dp", None),
            P("tensor", "dp", None),
            P("tensor", "dp", None),
            P("tensor", "dp", None),
        ),
        check_vma=False,
    )
```

```python
import functools
import math

import jax
import jax.numpy as jnp
from jax import lax
from jax.experimental import pallas as pl
from jax.experimental.pallas import tpu as pltpu
from jax.sharding import PartitionSpec as P

MODEL_WIDTH = 8192
DIAGONAL_BLOCKS = 32
HBS = 1024
HB = 16
BS = 256
EB = 32
PEERS = 16
PAIR = 2 * EB
LANES = 128
STATS = 16
STEP = 256
LATE = 160
TOKEN = 1
FOURTH = 200
TIE = 6
VMEM = 58 * 1024 * 1024
SMALL = 16 * 1024 * 1024

epsilon = 1e-05
root_scale = math.sqrt(2.0 / math.pi)
cubic_term = 0.044715

F32 = jnp.float32
BF16 = jnp.bfloat16

NN = (((1,), (0,)), ((), ()))
NT = (((1,), (1,)), ((), ()))
TN = (((0,), (0,)), ((), ()))
TT = (((0,), (1,)), ((), ()))


def dot(a, b, dims):
    return lax.dot_general(a, b, dims, preferred_element_type=F32)


def call(kernel, out_shape, args, scratch=(), flops=0, limit=None, **extra):
    outs = out_shape if isinstance(out_shape, (list, tuple)) else [out_shape]
    moved = sum(a.size * a.dtype.itemsize for a in args) + sum(
        math.prod(o.shape) * o.dtype.itemsize for o in outs
    )
    return pl.pallas_call(
        kernel,
        out_shape=out_shape,
        in_specs=[pl.BlockSpec(memory_space=pltpu.VMEM)] * len(args),
        out_specs=jax.tree.map(lambda _: pl.BlockSpec(memory_space=pltpu.VMEM), out_shape),
        scratch_shapes=list(scratch),
        compiler_params=pltpu.CompilerParams(vmem_limit_bytes=limit or VMEM),
        cost_estimate=pl.CostEstimate(flops=int(flops), bytes_accessed=int(moved), transcendentals=0),
        **extra,
    )(*args)


def stat_rows(value, chunks):
    high = value.astype(BF16).astype(F32)
    low = value - high
    rows = []
    for i in range(chunks):
        part = slice(i * LANES, (i + 1) * LANES)
        rows += [high[:, part], low[:, part]]
    rows.append(jnp.zeros((STATS - 2 * chunks, LANES), F32))
    return jnp.concatenate(rows, axis=0).astype(BF16)


def stat_sum(rows):
    return jnp.sum(rows.astype(F32), axis=0)


class Copies:
    def __init__(self, sems):
        self.sems = sems
        self.started = []

    def start(self, source, target):
        copy = pltpu.make_async_copy(source, target, self.sems.at[len(self.started)])
        copy.start()
        self.started.append(copy)
        return copy

    def wait(self):
        for copy in self.started:
            copy.wait()


def head_kernel(x_hbm, gain_ref, w1_hbm, out_hbm, x_ref, w1_ref, out_ref, in_sems, out_sems):
    steps = x_ref.shape[0] // STEP
    loads, stores = Copies(in_sems), Copies(out_sems)
    w1_load = loads.start(w1_hbm, w1_ref)
    parts = [pl.ds(i * STEP, STEP) for i in range(steps)]
    x_loads = [loads.start(x_hbm.at[part], x_ref.at[part]) for part in parts]
    w1_load.wait()
    turned = [w1_ref[a].T for a in range(2)]
    totals = []
    for i in range(steps):
        x_loads[i].wait()
        x = x_ref[parts[i], :].astype(F32)
        scaled = (x * gain_ref[...]).astype(BF16)
        base = i * 2 * PAIR
        for a in range(2):
            first = dot(turned[a], scaled[:, a * BS : (a + 1) * BS], NT).astype(BF16)
            for k in range(2):
                start = base + k * PAIR + a * EB
                value = first[:, k * LANES : (k + 1) * LANES]
                out_ref[:, start : start + EB, :] = value.reshape(PEERS, EB, LANES)
        part = pl.ds(base, 2 * PAIR)
        stores.start(out_ref.at[:, part], out_hbm.at[:, part])
        squares = x * x
        folded = squares[:, :LANES]
        for k in range(1, squares.shape[1] // LANES):
            folded = folded + squares[:, k * LANES : (k + 1) * LANES]
        totals.append(jnp.sum(folded.T, axis=0, keepdims=True))
    rows = steps * 2 * PAIR
    stats = stat_rows(jnp.concatenate(totals, axis=1), 2 * steps)
    out_ref[:, rows:, :] = jnp.broadcast_to(stats[None], (PEERS, STATS, LANES))
    part = pl.ds(rows, STATS)
    stores.start(out_ref.at[:, part], out_hbm.at[:, part])
    stores.wait()


def dgathered_kernel(w4_ref, cot_ref, out_ref):
    chunks = cot_ref.shape[0] // LANES
    for a in range(2):
        dgathered = dot(w4_ref[a], cot_ref[:, a * BS : (a + 1) * BS], NT).astype(BF16)
        for i in range(chunks):
            start = i * PAIR + a * EB
            value = dgathered[:, i * LANES : (i + 1) * LANES]
            out_ref[:, start : start + EB, :] = value.reshape(PEERS, EB, LANES)


def reciprocal(stats, i):
    rows = stats[4 * i : 4 * i + 4]
    total = jnp.concatenate([rows[0:1] + rows[1:2], rows[2:3] + rows[3:4]], axis=1)
    return lax.rsqrt(total / MODEL_WIDTH + epsilon)


def hidden_rows(ref):
    sources, rows, _ = ref.shape
    parts = [
        ref[:, i * PAIR : (i + 1) * PAIR, :].reshape(sources * PAIR, LANES) for i in range(rows // PAIR)
    ]
    return jnp.concatenate(parts, axis=1)


def turn_kernel(w2_ref, w3_ref, w2t_ref, w3t_ref):
    w2t_ref[...] = w2_ref[0].T
    w3t_ref[...] = w3_ref[0].T


def by_peer(value):
    parts = [value[:, k * LANES : (k + 1) * LANES].reshape(PEERS, PAIR, LANES) for k in range(2)]
    return jnp.concatenate(parts, axis=1)


def forward_kernel(
    recv_hbm, w2t_hbm, w3t_hbm, pre_hbm, act_hbm, out_hbm,
    recv_ref, w2t_ref, w3t_ref, pre_ref, act_ref, out_ref, in_sems, out_sems,
):
    steps = act_ref.shape[0]
    rows = steps * 2 * PAIR
    loads, stores = Copies(in_sems), Copies(out_sems)
    parts = [pl.ds(i * 2 * PAIR, 2 * PAIR) for i in range(steps)]
    rest = pl.ds(rows, STATS)
    stats_load = loads.start(recv_hbm.at[:, rest], recv_ref.at[:, rest])
    row_loads = [loads.start(recv_hbm.at[:, parts[0]], recv_ref.at[:, parts[0]])]
    w2t_load = loads.start(w2t_hbm, w2t_ref)
    for part in parts[1:]:
        row_loads.append(loads.start(recv_hbm.at[:, part], recv_ref.at[:, part]))
    w3t_load = loads.start(w3t_hbm, w3t_ref)
    stats_load.wait()
    stats = stat_sum(recv_ref[:, rows:, :])
    w2t_load.wait()
    for i in range(steps):
        row_loads[i].wait()
        pre = dot(w2t_ref[...], hidden_rows(recv_ref.at[:, parts[i]]), NN) * reciprocal(stats, i)
        pre_ref[i] = pre
        stores.start(pre_ref.at[i], pre_hbm.at[i])
        hyper = jnp.tanh(pre * (root_scale + (root_scale * cubic_term) * (pre * pre)))
        half = 0.5 * pre
        act_ref[i] = (half + half * hyper).astype(BF16)
    stores.start(act_ref, act_hbm)
    w3t_load.wait()
    for i in range(steps):
        third = dot(w3t_ref[...], act_ref[i], NN).astype(BF16)
        out_ref[:, i * 2 * PAIR : (i + 1) * 2 * PAIR, :] = by_peer(third)
        stores.start(out_ref.at[:, parts[i]], out_hbm.at[:, parts[i]])
    stores.wait()


def backward_kernel(
    y_ref, recv_hbm, dthird_hbm, pre_hbm, act_hbm, w3_hbm, grads_hbm, dpre_hbm, inner_ref,
    recv_ref, dthird_ref, pre_ref, act_ref, w3_ref, dpre_ref, scaled_ref, grads_ref, in_sems, out_sems,
):
    steps = act_ref.shape[0]
    rows = steps * 2 * PAIR
    y = y_ref[0]
    loads, stores = Copies(in_sems), Copies(out_sems)

    parts = [pl.ds(i * 2 * PAIR, 2 * PAIR) for i in range(steps)]
    rest = pl.ds(rows, STATS)
    stats_load = loads.start(recv_hbm.at[:, rest], recv_ref.at[:, rest])
    w3_load = loads.start(w3_hbm, w3_ref)
    third_loads = [loads.start(dthird_hbm.at[:, part], dthird_ref.at[:, part]) for part in parts]
    pre_loads = [loads.start(pre_hbm.at[i], pre_ref.at[i]) for i in range(steps)]
    act_load = loads.start(act_hbm, act_ref)
    mixed_load = loads.start(recv_hbm.at[:, pl.ds(0, rows)], recv_ref.at[:, pl.ds(0, rows)])
    stats_load.wait()
    stats = stat_sum(recv_ref[:, rows:, :])
    w3_load.wait()
    for i in range(steps):
        third_loads[i].wait()
        pre_loads[i].wait()
        dact = dot(w3_ref[0], hidden_rows(dthird_ref.at[:, parts[i]]), NN)
        pre = pre_ref[i]
        square = pre * pre
        hyper = jnp.tanh(pre * (root_scale + (root_scale * cubic_term) * square))
        slope = (0.5 + 0.5 * hyper) + (0.5 * pre) * (1.0 - hyper * hyper) * (
            root_scale + (3.0 * root_scale * cubic_term) * square
        )
        dpre = dact * slope
        inner_ref[:, i * STEP : (i + 1) * STEP] = jnp.sum(dpre * pre, axis=0, keepdims=True)
        dpre_ref[i] = dpre.astype(BF16)
        scaled_ref[i] = (dpre * reciprocal(stats, i)).astype(BF16)
    act_load.wait()
    mixed_load.wait()
    dthird = hidden_rows(dthird_ref)
    scaled = jnp.concatenate([scaled_ref[i] for i in range(steps)], axis=1)
    z_size, y_size, part_rows, _ = grads_ref.shape
    half = z_size // 2
    size = half * part_rows
    for r in range(2 * y_size):
        z = pl.ds(r % 2 * half, half)
        act = jnp.concatenate([act_ref[i, r * size : (r + 1) * size, :] for i in range(steps)], axis=1)
        third = dot(act, dthird, NT).astype(BF16)
        grads_ref[z, r // 2, :, HBS:] = third.reshape(half, part_rows, HBS)
        sources = pl.ds(r * (size // PAIR), size // PAIR)
        mixed = hidden_rows(recv_ref.at[sources, pl.ds(0, rows)])
        second = dot(mixed, scaled, NT).astype(BF16)
        grads_ref[z, r // 2, :, :HBS] = second.reshape(half, part_rows, HBS)
        stores.start(grads_ref.at[z, r // 2], grads_hbm.at[z, lax.rem(r // 2 + y, y_size)])
    stores.start(dpre_ref, dpre_hbm)
    stores.wait()


def dmixed_kernel(dpre_ref, inner_ref, w2_ref, out_ref):
    steps = dpre_ref.shape[0]
    for i in range(steps):
        dmixed = dot(w2_ref[0], dpre_ref[i], NN).astype(BF16)
        out_ref[:, i * 2 * PAIR : (i + 1) * 2 * PAIR, :] = by_peer(dmixed)
    rest = stat_rows(inner_ref[...], 2 * steps)
    out_ref[:, steps * 2 * PAIR :, :] = jnp.broadcast_to(rest[None], (PEERS, STATS, LANES))


def model_rows(ref, chunks, a):
    parts = []
    for i in range(chunks):
        start = i * PAIR + a * EB
        parts.append(ref[:, start : start + EB, :].reshape(HB * EB, LANES))
    return jnp.concatenate(parts, axis=1)


def columns(stats, chunks):
    turned = stats.T
    parts = [turned[:, 2 * i : 2 * i + 1] + turned[:, 2 * i + 1 : 2 * i + 2] for i in range(chunks)]
    return jnp.concatenate(parts, axis=0)


def output_kernel(recv_ref, x_ref, w4_ref, out_ref):
    chunks = x_ref.shape[0] // LANES
    for a in range(2):
        feats = slice(a * BS, (a + 1) * BS)
        branch = dot(model_rows(recv_ref, chunks, a), w4_ref[a], TN)
        out_ref[:, feats] = (x_ref[:, feats].astype(F32) + branch).astype(BF16)


def fourth_kernel(place_ref, recv_ref, cot_ref, x_ref, gain_ref, stats_ref, *refs):
    out_refs, normed_ref, block_ref = refs[:-2], refs[-2], refs[-1]
    chunks = cot_ref.shape[0] // LANES
    z_size = len(out_refs)
    rows = HB * EB // PEERS
    y = place_ref[0]
    for a in range(2):
        grad = dot(model_rows(recv_ref, chunks, a), cot_ref[:, a * BS : (a + 1) * BS], NN).astype(BF16)
        grad = grad.reshape(PEERS, rows, BS)
        own = slice(a * rows, (a + 1) * rows)
        block_ref[:, own, :] = jnp.where(y == 0, grad[:z_size], grad[z_size:])
        other = slice((2 + a) * rows, (3 + a) * rows)
        block_ref[:, other, :] = jnp.where(y == 0, grad[z_size:], grad[:z_size])
    for k, out_ref in enumerate(out_refs):
        out_ref[...] = block_ref[lax.rem(place_ref[1] + k, z_size)]
    inverse = lax.rsqrt(columns(stat_sum(stats_ref[...]), chunks) / MODEL_WIDTH + epsilon)
    normed_ref[...] = (x_ref[...].astype(F32) * inverse * gain_ref[...]).astype(BF16)


def fourth_sum_kernel(*refs):
    total = refs[0][...].astype(F32)
    for ref in refs[1:-2]:
        total = total + ref[...].astype(F32)
    half = total.shape[0] // 2
    refs[-2][...] = total[:half]
    refs[-1][...] = total[half:].astype(BF16)


def first_kernel(recv_hbm, normed_hbm, out_ref, recv_ref, normed_ref, sems):
    chunks = normed_ref.shape[0] // LANES
    loads = Copies(sems)
    loads.start(normed_hbm, normed_ref)
    loads.start(recv_hbm.at[:, pl.ds(0, chunks * PAIR)], recv_ref)
    loads.wait()
    rows = BS // PEERS
    for a in range(2):
        dfirst = model_rows(recv_ref, chunks, a)
        grad = dot(dfirst, normed_ref[:, a * BS : (a + 1) * BS], NN).astype(BF16).T
        for half in range(2):
            base = (2 * a + half) * rows
            value = grad[:, half * BS : (half + 1) * BS]
            out_ref[:, base : base + rows, :] = value.reshape(PEERS, rows, BS)


def token_kernel(recv_ref, stats_ref, x_ref, gain_ref, w1_ref, cot_ref, out_ref):
    chunks = x_ref.shape[0] // LANES
    inverse = lax.rsqrt(columns(stat_sum(stats_ref[...]), chunks) / MODEL_WIDTH + epsilon)
    inner = columns(stat_sum(recv_ref[:, chunks * PAIR :, :]), chunks) / MODEL_WIDTH
    for a in range(2):
        feats = slice(a * BS, (a + 1) * BS)
        dfirst = model_rows(recv_ref, chunks, a)
        dnormed = dot(dfirst, w1_ref[a], TT)
        xhat = x_ref[:, feats].astype(F32) * inverse
        change = dnormed * gain_ref[:, feats] - xhat * inner
        out_ref[:, feats] = (cot_ref[:, feats].astype(F32) + inverse * change).astype(BF16)


def first_total_kernel(scale, recv_ref, first_ref):
    total = jnp.sum(recv_ref[...].astype(F32), axis=0) * scale
    _, rows, _ = first_ref.shape
    for a in range(2):
        for half in range(2):
            base = (2 * a + half) * rows
            first_ref[a, :, half * BS : (half + 1) * BS] = total[base : base + rows]


def finish_kernel(scale, own_ref, other_ref, own4_ref, other4_ref, second_ref, third_ref, fourth_ref):
    total = (own_ref[0, 0].astype(F32) + other_ref[...].astype(F32)) * scale
    second_ref[0] = total[:, :HBS]
    third_ref[0] = total[:, HBS:]
    total = (own4_ref[...] + other4_ref[...].astype(F32)) * scale
    fourth_ref[...] = total.reshape(fourth_ref.shape)


def shards(tokens, gain, w_first, w_second, w_third, w_fourth, cotangent):
    element_count, local_width = tokens.shape
    dp = lax.axis_size("dp")
    scale = 1.0 / math.sqrt(element_count * dp)
    gain_row = gain[None, :]
    z_size = dp // 2
    z_groups = [[y * z_size + z for z in range(z_size)] for y in range(2)]
    y_pairs = [(i, (i + z_size) % dp) for i in range(dp)]
    place = lax.axis_index("dp")
    place = jnp.stack([place // z_size, place % z_size]).astype(jnp.int32)
    shape = jax.ShapeDtypeStruct
    hidden_flops = 2 * HBS * HBS * element_count
    model_flops = 2 * local_width * HB * EB * element_count
    steps = element_count // STEP
    rows = steps * 2 * PAIR
    plain_sent = shape((PEERS, rows, LANES), BF16)
    stats_sent = shape((PEERS, rows + STATS, LANES), BF16)
    stepped = shape((steps, HBS, STEP), BF16)
    hbm = pl.BlockSpec(memory_space=pltpu.HBM)
    vmem = pl.BlockSpec(memory_space=pltpu.VMEM)
    smem = pl.BlockSpec(memory_space=pltpu.SMEM)
    params = pltpu.CompilerParams(vmem_limit_bytes=VMEM)

    def cost(flops):
        return pl.CostEstimate(flops=int(flops), bytes_accessed=8 << 20, transcendentals=0)

    def whole(*dims):
        return pl.BlockSpec(dims, lambda i, *_: (0,) * len(dims))

    def exchange(value):
        return lax.all_to_all(value, "tensor", 0, 0, tiled=True)

    send = pl.pallas_call(
        head_kernel,
        out_shape=stats_sent,
        in_specs=[hbm, vmem, hbm],
        out_specs=hbm,
        scratch_shapes=[
            pltpu.VMEM(tokens.shape, BF16),
            pltpu.VMEM(w_first.shape, BF16),
            pltpu.VMEM(stats_sent.shape, BF16),
            pltpu.SemaphoreType.DMA((steps + 1,)),
            pltpu.SemaphoreType.DMA((steps + 1,)),
        ],
        compiler_params=params,
        cost_estimate=cost(model_flops),
    )(tokens, gain_row, w_first)
    recv = exchange(send)
    send = call(dgathered_kernel, plain_sent, (w_fourth, cotangent), flops=model_flops)
    dthird = exchange(lax.optimization_barrier((send, recv))[0])
    turned = shape((HBS, HBS), BF16)
    w_second_t, w_third_t = call(turn_kernel, [turned, turned], (w_second, w_third))
    pre_shape = shape(stepped.shape, F32)
    pre, act, send = pl.pallas_call(
        forward_kernel,
        out_shape=[pre_shape, stepped, plain_sent],
        in_specs=[hbm] * 3,
        out_specs=[hbm] * 3,
        scratch_shapes=[
            pltpu.VMEM(stats_sent.shape, BF16),
            pltpu.VMEM(turned.shape, BF16),
            pltpu.VMEM(turned.shape, BF16),
            pltpu.VMEM(stepped.shape, F32),
            pltpu.VMEM(stepped.shape, BF16),
            pltpu.VMEM(plain_sent.shape, BF16),
            pltpu.SemaphoreType.DMA((steps + 3,)),
            pltpu.SemaphoreType.DMA((2 * steps + 1,)),
        ],
        compiler_params=params,
        cost_estimate=cost(2 * hidden_flops),
    )(recv, w_second_t, w_third_t)
    third = exchange(lax.optimization_barrier((send, dthird))[0])
    grads = shape((z_size, 2, HBS // dp, 2 * HBS), BF16)
    hidden, dpre, inner = pl.pallas_call(
        backward_kernel,
        out_shape=[grads, stepped, shape((1, element_count), F32)],
        in_specs=[smem] + [hbm] * 5,
        out_specs=[hbm, hbm, vmem],
        scratch_shapes=[
            pltpu.VMEM(stats_sent.shape, BF16),
            pltpu.VMEM(plain_sent.shape, BF16),
            pltpu.VMEM(stepped.shape, F32),
            pltpu.VMEM(stepped.shape, BF16),
            pltpu.VMEM(w_third.shape, BF16),
            pltpu.VMEM(stepped.shape, BF16),
            pltpu.VMEM(stepped.shape, BF16),
            pltpu.VMEM(grads.shape, BF16),
            pltpu.SemaphoreType.DMA((2 * steps + 4,)),
            pltpu.SemaphoreType.DMA((5,)),
        ],
        compiler_params=params,
        cost_estimate=cost(3 * hidden_flops),
    )(place, recv, dthird, pre, act, w_third)
    hidden = lax.psum_scatter(hidden, "dp", scatter_dimension=0, axis_index_groups=z_groups, tiled=True)
    send = call(dmixed_kernel, stats_sent, (dpre, inner, w_second), flops=hidden_flops)
    send, third = lax.optimization_barrier((send, third))
    back = exchange(send)

    stats_spec = pl.BlockSpec((PEERS, STATS, LANES), lambda i: (0, rows // STATS, 0))
    all_tokens = whole(*tokens.shape)
    row = whole(1, local_width)
    block = shape((2 * PAIR, BS), BF16)
    *blocks, normed = pl.pallas_call(
        fourth_kernel,
        out_shape=[block] * z_size + [shape(tokens.shape, BF16)],
        grid=(1,),
        in_specs=[smem, whole(*plain_sent.shape), all_tokens, all_tokens, row, stats_spec],
        out_specs=[whole(*block.shape)] * z_size + [all_tokens],
        scratch_shapes=[pltpu.VMEM((z_size,) + block.shape, BF16)],
        compiler_params=params,
        cost_estimate=cost(FOURTH * model_flops),
    )(place, third, cotangent, tokens, gain_row, recv)
    first = pl.pallas_call(
        first_kernel,
        out_shape=shape((PEERS, PAIR, BS), BF16),
        in_specs=[hbm, hbm],
        out_specs=vmem,
        scratch_shapes=[
            pltpu.VMEM(plain_sent.shape, BF16),
            pltpu.VMEM(tokens.shape, BF16),
            pltpu.SemaphoreType.DMA((2,)),
        ],
        compiler_params=params,
        cost_estimate=cost(model_flops),
    )(back, normed)
    late, third, first = lax.optimization_barrier((blocks[TIE:], third, first))
    blocks[TIE:] = late
    first = lax.all_to_all(first, "dp", 0, 0, tiled=True)
    for k in range(1, z_size):
        shift = [(g[z], g[(z + k) % z_size]) for g in z_groups for z in range(z_size)]
        blocks[k] = lax.ppermute(blocks[k], "dp", shift)
    part = (PAIR, BS)
    own4, other4 = call(fourth_sum_kernel, [shape(part, F32), shape(part, BF16)], tuple(blocks), limit=SMALL)
    other4 = lax.ppermute(other4, "dp", y_pairs)
    output = call(output_kernel, shape(tokens.shape, BF16), (third, tokens, w_fourth), flops=LATE * model_flops)
    token_gradient = pl.pallas_call(
        token_kernel,
        out_shape=shape(tokens.shape, BF16),
        grid=(1,),
        in_specs=[whole(*stats_sent.shape), stats_spec, all_tokens, row, whole(*w_first.shape), all_tokens],
        out_specs=all_tokens,
        compiler_params=params,
        cost_estimate=cost(TOKEN * model_flops),
    )(back, recv, tokens, gain_row, w_first, cotangent)
    hidden, own4 = lax.optimization_barrier((hidden, own4))
    other = lax.ppermute(hidden[0, 1], "dp", y_pairs)
    part = shape((1, HBS // dp, HBS), F32)
    grad_second, grad_third, grad_fourth = call(
        functools.partial(finish_kernel, scale),
        [part, part, shape((2, HB * EB // dp, BS), F32)],
        (hidden, other, own4, other4),
        limit=SMALL,
    )
    first, grad_second, grad_third = lax.optimization_barrier((first, grad_second, grad_third))
    grad_first = call(
        functools.partial(first_total_kernel, scale),
        shape((2, BS // dp, HB * EB), F32),
        (first,),
        limit=SMALL,
    )
    return output, token_gradient, grad_first, grad_second, grad_third, grad_fourth


def solution(mesh):
    return jax.shard_map(
        shards,
        mesh=mesh,
        in_specs=(
            P("dp", "tensor"),
            P("tensor"),
            P("tensor", None, None),
            P("tensor", None, None),
            P("tensor", None, None),
            P("tensor", None, None),
            P("dp", "tensor"),
        ),
        out_specs=(
            P("dp", "tensor"),
            P("dp", "tensor"),
            P("tensor", "dp", None),
            P("tensor", "dp", None),
            P("tensor", "dp", None),
            P("tensor", "dp", None),
        ),
        check_vma=False,
    )
```

```python
import functools
import math

import jax
import jax.numpy as jnp
from jax import lax
from jax.experimental import pallas as pl
from jax.experimental.pallas import tpu as pltpu
from jax.sharding import PartitionSpec as P

MODEL_WIDTH = 8192
DIAGONAL_BLOCKS = 32
HBS = 1024
HB = 16
BS = 256
EB = 32
PEERS = 16
PAIR = 2 * EB
LANES = 128
STATS = 16
STEP = 256
LATE = 160
VMEM = 58 * 1024 * 1024
SMALL = 16 * 1024 * 1024
FIRST = 24 * 1024 * 1024

epsilon = 1e-05
root_scale = math.sqrt(2.0 / math.pi)
cubic_term = 0.044715

F32 = jnp.float32
BF16 = jnp.bfloat16

NN = (((1,), (0,)), ((), ()))
NT = (((1,), (1,)), ((), ()))
TN = (((0,), (0,)), ((), ()))
TT = (((0,), (1,)), ((), ()))


def dot(a, b, dims):
    return lax.dot_general(a, b, dims, preferred_element_type=F32)


def call(kernel, out_shape, args, scratch=(), flops=0, limit=None, **extra):
    outs = out_shape if isinstance(out_shape, (list, tuple)) else [out_shape]
    moved = sum(a.size * a.dtype.itemsize for a in args) + sum(
        math.prod(o.shape) * o.dtype.itemsize for o in outs
    )
    return pl.pallas_call(
        kernel,
        out_shape=out_shape,
        in_specs=[pl.BlockSpec(memory_space=pltpu.VMEM)] * len(args),
        out_specs=jax.tree.map(lambda _: pl.BlockSpec(memory_space=pltpu.VMEM), out_shape),
        scratch_shapes=list(scratch),
        compiler_params=pltpu.CompilerParams(vmem_limit_bytes=limit or VMEM),
        cost_estimate=pl.CostEstimate(flops=int(flops), bytes_accessed=int(moved), transcendentals=0),
        **extra,
    )(*args)


def stat_rows(value, chunks):
    high = value.astype(BF16).astype(F32)
    low = value - high
    rows = []
    for i in range(chunks):
        part = slice(i * LANES, (i + 1) * LANES)
        rows += [high[:, part], low[:, part]]
    rows.append(jnp.zeros((STATS - 2 * chunks, LANES), F32))
    return jnp.concatenate(rows, axis=0).astype(BF16)


def stat_sum(rows):
    return jnp.sum(rows.astype(F32), axis=0)


class Copies:
    def __init__(self, sems):
        self.sems = sems
        self.started = []

    def start(self, source, target):
        copy = pltpu.make_async_copy(source, target, self.sems.at[len(self.started)])
        copy.start()
        self.started.append(copy)
        return copy

    def wait(self):
        for copy in self.started:
            copy.wait()


def head_kernel(x_hbm, gain_ref, w1_hbm, out_hbm, x_ref, w1_ref, out_ref, in_sems, out_sems):
    steps = x_ref.shape[0] // STEP
    loads, stores = Copies(in_sems), Copies(out_sems)
    w1_load = loads.start(w1_hbm, w1_ref)
    parts = [pl.ds(i * STEP, STEP) for i in range(steps)]
    x_loads = [loads.start(x_hbm.at[part], x_ref.at[part]) for part in parts]
    w1_load.wait()
    turned = [w1_ref[a].T for a in range(2)]
    totals = []
    for i in range(steps):
        x_loads[i].wait()
        x = x_ref[parts[i], :].astype(F32)
        scaled = (x * gain_ref[...]).astype(BF16)
        base = i * 2 * PAIR
        for a in range(2):
            first = dot(turned[a], scaled[:, a * BS : (a + 1) * BS], NT).astype(BF16)
            for k in range(2):
                start = base + k * PAIR + a * EB
                value = first[:, k * LANES : (k + 1) * LANES]
                out_ref[:, start : start + EB, :] = value.reshape(PEERS, EB, LANES)
        part = pl.ds(base, 2 * PAIR)
        stores.start(out_ref.at[:, part], out_hbm.at[:, part])
        squares = x * x
        folded = squares[:, :LANES]
        for k in range(1, squares.shape[1] // LANES):
            folded = folded + squares[:, k * LANES : (k + 1) * LANES]
        totals.append(jnp.sum(folded.T, axis=0, keepdims=True))
    rows = steps * 2 * PAIR
    stats = stat_rows(jnp.concatenate(totals, axis=1), 2 * steps)
    out_ref[:, rows:, :] = jnp.broadcast_to(stats[None], (PEERS, STATS, LANES))
    part = pl.ds(rows, STATS)
    stores.start(out_ref.at[:, part], out_hbm.at[:, part])
    stores.wait()


def dgathered_kernel(w4_ref, cot_ref, out_ref):
    chunks = cot_ref.shape[0] // LANES
    for a in range(2):
        dgathered = dot(w4_ref[a], cot_ref[:, a * BS : (a + 1) * BS], NT).astype(BF16)
        for i in range(chunks):
            start = i * PAIR + a * EB
            value = dgathered[:, i * LANES : (i + 1) * LANES]
            out_ref[:, start : start + EB, :] = value.reshape(PEERS, EB, LANES)


def reciprocal(stats, i):
    rows = stats[4 * i : 4 * i + 4]
    total = jnp.concatenate([rows[0:1] + rows[1:2], rows[2:3] + rows[3:4]], axis=1)
    return lax.rsqrt(total / MODEL_WIDTH + epsilon)


def hidden_rows(ref):
    sources, rows, _ = ref.shape
    parts = [
        ref[:, i * PAIR : (i + 1) * PAIR, :].reshape(sources * PAIR, LANES) for i in range(rows // PAIR)
    ]
    return jnp.concatenate(parts, axis=1)


def turn_kernel(w2_ref, w3_ref, w2t_ref, w3t_ref):
    w2t_ref[...] = w2_ref[0].T
    w3t_ref[...] = w3_ref[0].T


def by_peer(value):
    parts = [value[:, k * LANES : (k + 1) * LANES].reshape(PEERS, PAIR, LANES) for k in range(2)]
    return jnp.concatenate(parts, axis=1)


def forward_kernel(
    recv_hbm, w2t_hbm, w3t_hbm, pre_hbm, act_hbm, out_hbm,
    recv_ref, w2t_ref, w3t_ref, pre_ref, act_ref, out_ref, in_sems, out_sems,
):
    steps = act_ref.shape[0]
    rows = steps * 2 * PAIR
    loads, stores = Copies(in_sems), Copies(out_sems)
    parts = [pl.ds(i * 2 * PAIR, 2 * PAIR) for i in range(steps)]
    rest = pl.ds(rows, STATS)
    stats_load = loads.start(recv_hbm.at[:, rest], recv_ref.at[:, rest])
    row_loads = [loads.start(recv_hbm.at[:, parts[0]], recv_ref.at[:, parts[0]])]
    w2t_load = loads.start(w2t_hbm, w2t_ref)
    for part in parts[1:]:
        row_loads.append(loads.start(recv_hbm.at[:, part], recv_ref.at[:, part]))
    w3t_load = loads.start(w3t_hbm, w3t_ref)
    stats_load.wait()
    stats = stat_sum(recv_ref[:, rows:, :])
    w2t_load.wait()
    for i in range(steps):
        row_loads[i].wait()
        pre = dot(w2t_ref[...], hidden_rows(recv_ref.at[:, parts[i]]), NN) * reciprocal(stats, i)
        pre_ref[i] = pre
        stores.start(pre_ref.at[i], pre_hbm.at[i])
        hyper = jnp.tanh(pre * (root_scale + (root_scale * cubic_term) * (pre * pre)))
        half = 0.5 * pre
        act_ref[i] = (half + half * hyper).astype(BF16)
    stores.start(act_ref, act_hbm)
    w3t_load.wait()
    for i in range(steps):
        third = dot(w3t_ref[...], act_ref[i], NN).astype(BF16)
        out_ref[:, i * 2 * PAIR : (i + 1) * 2 * PAIR, :] = by_peer(third)
        stores.start(out_ref.at[:, parts[i]], out_hbm.at[:, parts[i]])
    stores.wait()


def backward_kernel(
    y_ref, recv_hbm, dthird_hbm, pre_hbm, act_hbm, w3_hbm, grads_hbm, dpre_hbm, inner_ref,
    recv_ref, dthird_ref, pre_ref, act_ref, w3_ref, dpre_ref, scaled_ref, grads_ref, in_sems, out_sems,
):
    steps = act_ref.shape[0]
    rows = steps * 2 * PAIR
    y = y_ref[0]
    loads, stores = Copies(in_sems), Copies(out_sems)

    parts = [pl.ds(i * 2 * PAIR, 2 * PAIR) for i in range(steps)]
    rest = pl.ds(rows, STATS)
    stats_load = loads.start(recv_hbm.at[:, rest], recv_ref.at[:, rest])
    w3_load = loads.start(w3_hbm, w3_ref)
    third_loads = [loads.start(dthird_hbm.at[:, part], dthird_ref.at[:, part]) for part in parts]
    pre_loads = [loads.start(pre_hbm.at[i], pre_ref.at[i]) for i in range(steps)]
    act_load = loads.start(act_hbm, act_ref)
    mixed_load = loads.start(recv_hbm.at[:, pl.ds(0, rows)], recv_ref.at[:, pl.ds(0, rows)])
    stats_load.wait()
    stats = stat_sum(recv_ref[:, rows:, :])
    w3_load.wait()
    for i in range(steps):
        third_loads[i].wait()
        pre_loads[i].wait()
        dact = dot(w3_ref[0], hidden_rows(dthird_ref.at[:, parts[i]]), NN)
        pre = pre_ref[i]
        square = pre * pre
        hyper = jnp.tanh(pre * (root_scale + (root_scale * cubic_term) * square))
        slope = (0.5 + 0.5 * hyper) + (0.5 * pre) * (1.0 - hyper * hyper) * (
            root_scale + (3.0 * root_scale * cubic_term) * square
        )
        dpre = dact * slope
        inner_ref[:, i * STEP : (i + 1) * STEP] = jnp.sum(dpre * pre, axis=0, keepdims=True)
        dpre_ref[i] = dpre.astype(BF16)
        scaled_ref[i] = (dpre * reciprocal(stats, i)).astype(BF16)
    stores.start(dpre_ref, dpre_hbm)
    act_load.wait()
    mixed_load.wait()
    dthird = hidden_rows(dthird_ref)
    scaled = jnp.concatenate([scaled_ref[i] for i in range(steps)], axis=1)
    z_size, y_size, part_rows, _ = grads_ref.shape
    half = z_size // 2
    size = half * part_rows
    for r in range(2 * y_size):
        z = pl.ds(r % 2 * half, half)
        act = jnp.concatenate([act_ref[i, r * size : (r + 1) * size, :] for i in range(steps)], axis=1)
        third = dot(act, dthird, NT).astype(BF16)
        grads_ref[z, r // 2, :, HBS:] = third.reshape(half, part_rows, HBS)
        sources = pl.ds(r * (size // PAIR), size // PAIR)
        mixed = hidden_rows(recv_ref.at[sources, pl.ds(0, rows)])
        second = dot(mixed, scaled, NT).astype(BF16)
        grads_ref[z, r // 2, :, :HBS] = second.reshape(half, part_rows, HBS)
        stores.start(grads_ref.at[z, r // 2], grads_hbm.at[z, lax.rem(r // 2 + y, y_size)])
    stores.wait()


def dmixed_kernel(dpre_ref, inner_ref, w2_ref, out_ref):
    steps = dpre_ref.shape[0]
    for i in range(steps):
        dmixed = dot(w2_ref[0], dpre_ref[i], NN).astype(BF16)
        out_ref[:, i * 2 * PAIR : (i + 1) * 2 * PAIR, :] = by_peer(dmixed)
    rest = stat_rows(inner_ref[...], 2 * steps)
    out_ref[:, steps * 2 * PAIR :, :] = jnp.broadcast_to(rest[None], (PEERS, STATS, LANES))


def model_rows(ref, chunks, a):
    parts = []
    for i in range(chunks):
        start = i * PAIR + a * EB
        parts.append(ref[:, start : start + EB, :].reshape(HB * EB, LANES))
    return jnp.concatenate(parts, axis=1)


def columns(stats, chunks):
    turned = stats.T
    parts = [turned[:, 2 * i : 2 * i + 1] + turned[:, 2 * i + 1 : 2 * i + 2] for i in range(chunks)]
    return jnp.concatenate(parts, axis=0)


def output_kernel(recv_ref, x_ref, w4_ref, out_ref):
    chunks = x_ref.shape[0] // LANES
    for a in range(2):
        feats = slice(a * BS, (a + 1) * BS)
        branch = dot(model_rows(recv_ref, chunks, a), w4_ref[a], TN)
        out_ref[:, feats] = (x_ref[:, feats].astype(F32) + branch).astype(BF16)


def fourth_kernel(y_ref, recv_ref, cot_ref, x_ref, gain_ref, stats_ref, own_ref, other_ref, normed_ref):
    chunks = cot_ref.shape[0] // LANES
    z_size = own_ref.shape[0]
    rows = HB * EB // PEERS
    for a in range(2):
        grad = dot(model_rows(recv_ref, chunks, a), cot_ref[:, a * BS : (a + 1) * BS], NN).astype(BF16)
        grad = grad.reshape(PEERS, rows, BS)
        part = slice(a * rows, (a + 1) * rows)
        own_ref[:, part, :] = jnp.where(y_ref[0] == 0, grad[:z_size], grad[z_size:])
        other_ref[:, part, :] = jnp.where(y_ref[0] == 0, grad[z_size:], grad[:z_size])
    inverse = lax.rsqrt(columns(stat_sum(stats_ref[...]), chunks) / MODEL_WIDTH + epsilon)
    normed_ref[...] = (x_ref[...].astype(F32) * inverse * gain_ref[...]).astype(BF16)


def pair_kernel(first_own, first_other, fourth_own, fourth_other, out_ref):
    out_ref[:, :PAIR, :] = (first_own[...].astype(F32) + first_other[...].astype(F32)).astype(BF16)
    out_ref[:, PAIR:, :] = (fourth_own[...].astype(F32) + fourth_other[...].astype(F32)).astype(BF16)


def first_kernel(y_ref, recv_hbm, normed_hbm, own_ref, other_ref, recv_ref, normed_ref, sems):
    chunks = normed_ref.shape[0] // LANES
    z_size = own_ref.shape[0]
    loads = Copies(sems)
    loads.start(normed_hbm, normed_ref)
    loads.start(recv_hbm.at[:, pl.ds(0, chunks * PAIR)], recv_ref)
    loads.wait()
    rows = BS // PEERS
    for a in range(2):
        dfirst = model_rows(recv_ref, chunks, a)
        grad = dot(dfirst, normed_ref[:, a * BS : (a + 1) * BS], NN).astype(BF16).T
        for half in range(2):
            base = (2 * a + half) * rows
            value = grad[:, half * BS : (half + 1) * BS].reshape(PEERS, rows, BS)
            part = slice(base, base + rows)
            own_ref[:, part, :] = jnp.where(y_ref[0] == 0, value[:z_size], value[z_size:])
            other_ref[:, part, :] = jnp.where(y_ref[0] == 0, value[z_size:], value[:z_size])


def token_kernel(recv_ref, stats_ref, x_ref, gain_ref, w1_ref, cot_ref, out_ref):
    chunks = x_ref.shape[0] // LANES
    inverse = lax.rsqrt(columns(stat_sum(stats_ref[...]), chunks) / MODEL_WIDTH + epsilon)
    inner = columns(stat_sum(recv_ref[:, chunks * PAIR :, :]), chunks) / MODEL_WIDTH
    for a in range(2):
        feats = slice(a * BS, (a + 1) * BS)
        dfirst = model_rows(recv_ref, chunks, a)
        dnormed = dot(dfirst, w1_ref[a], TT)
        xhat = x_ref[:, feats].astype(F32) * inverse
        change = dnormed * gain_ref[:, feats] - xhat * inner
        out_ref[:, feats] = (cot_ref[:, feats].astype(F32) + inverse * change).astype(BF16)


def sum_kernel(scale, recv_ref, first_ref, fourth_ref):
    total = jnp.sum(recv_ref[...].astype(F32), axis=0) * scale
    _, rows, _ = first_ref.shape
    for a in range(2):
        for half in range(2):
            base = (2 * a + half) * rows
            first_ref[a, :, half * BS : (half + 1) * BS] = total[base : base + rows]
    fourth_ref[...] = total[PAIR:].reshape(fourth_ref.shape)


def finish_kernel(scale, own_ref, other_ref, second_ref, third_ref):
    total = (own_ref[0, 0].astype(F32) + other_ref[...].astype(F32)) * scale
    second_ref[0] = total[:, :HBS]
    third_ref[0] = total[:, HBS:]


def shards(tokens, gain, w_first, w_second, w_third, w_fourth, cotangent):
    element_count, local_width = tokens.shape
    dp = lax.axis_size("dp")
    scale = 1.0 / math.sqrt(element_count * dp)
    gain_row = gain[None, :]
    z_size = dp // 2
    z_groups = [[y * z_size + z for z in range(z_size)] for y in range(2)]
    y_pairs = [(i, (i + z_size) % dp) for i in range(dp)]
    y_index = (lax.axis_index("dp") // z_size).astype(jnp.int32)[None]
    shape = jax.ShapeDtypeStruct
    hidden_flops = 2 * HBS * HBS * element_count
    model_flops = 2 * local_width * HB * EB * element_count
    steps = element_count // STEP
    rows = steps * 2 * PAIR
    plain_sent = shape((PEERS, rows, LANES), BF16)
    stats_sent = shape((PEERS, rows + STATS, LANES), BF16)
    stepped = shape((steps, HBS, STEP), BF16)
    hbm = pl.BlockSpec(memory_space=pltpu.HBM)
    vmem = pl.BlockSpec(memory_space=pltpu.VMEM)
    smem = pl.BlockSpec(memory_space=pltpu.SMEM)
    params = pltpu.CompilerParams(vmem_limit_bytes=VMEM)

    def cost(flops):
        return pl.CostEstimate(flops=int(flops), bytes_accessed=8 << 20, transcendentals=0)

    def whole(*dims):
        return pl.BlockSpec(dims, lambda i, *_: (0,) * len(dims))

    def exchange(value):
        return lax.all_to_all(value, "tensor", 0, 0, tiled=True)

    send = pl.pallas_call(
        head_kernel,
        out_shape=stats_sent,
        in_specs=[hbm, vmem, hbm],
        out_specs=hbm,
        scratch_shapes=[
            pltpu.VMEM(tokens.shape, BF16),
            pltpu.VMEM(w_first.shape, BF16),
            pltpu.VMEM(stats_sent.shape, BF16),
            pltpu.SemaphoreType.DMA((steps + 1,)),
            pltpu.SemaphoreType.DMA((steps + 1,)),
        ],
        compiler_params=params,
        cost_estimate=cost(model_flops),
    )(tokens, gain_row, w_first)
    recv = exchange(send)
    send = call(dgathered_kernel, plain_sent, (w_fourth, cotangent), flops=model_flops)
    dthird = exchange(lax.optimization_barrier((send, recv))[0])
    turned = shape((HBS, HBS), BF16)
    w_second_t, w_third_t = call(turn_kernel, [turned, turned], (w_second, w_third))
    pre_shape = shape(stepped.shape, F32)
    pre, act, send = pl.pallas_call(
        forward_kernel,
        out_shape=[pre_shape, stepped, plain_sent],
        in_specs=[hbm] * 3,
        out_specs=[hbm] * 3,
        scratch_shapes=[
            pltpu.VMEM(stats_sent.shape, BF16),
            pltpu.VMEM(turned.shape, BF16),
            pltpu.VMEM(turned.shape, BF16),
            pltpu.VMEM(stepped.shape, F32),
            pltpu.VMEM(stepped.shape, BF16),
            pltpu.VMEM(plain_sent.shape, BF16),
            pltpu.SemaphoreType.DMA((steps + 3,)),
            pltpu.SemaphoreType.DMA((2 * steps + 1,)),
        ],
        compiler_params=params,
        cost_estimate=cost(2 * hidden_flops),
    )(recv, w_second_t, w_third_t)
    third = exchange(lax.optimization_barrier((send, dthird))[0])
    grads = shape((z_size, 2, HBS // dp, 2 * HBS), BF16)
    hidden, dpre, inner = pl.pallas_call(
        backward_kernel,
        out_shape=[grads, stepped, shape((1, element_count), F32)],
        in_specs=[smem] + [hbm] * 5,
        out_specs=[hbm, hbm, vmem],
        scratch_shapes=[
            pltpu.VMEM(stats_sent.shape, BF16),
            pltpu.VMEM(plain_sent.shape, BF16),
            pltpu.VMEM(stepped.shape, F32),
            pltpu.VMEM(stepped.shape, BF16),
            pltpu.VMEM(w_third.shape, BF16),
            pltpu.VMEM(stepped.shape, BF16),
            pltpu.VMEM(stepped.shape, BF16),
            pltpu.VMEM(grads.shape, BF16),
            pltpu.SemaphoreType.DMA((2 * steps + 4,)),
            pltpu.SemaphoreType.DMA((5,)),
        ],
        compiler_params=params,
        cost_estimate=cost(3 * hidden_flops),
    )(y_index, recv, dthird, pre, act, w_third)
    hidden = lax.psum_scatter(hidden, "dp", scatter_dimension=0, axis_index_groups=z_groups, tiled=True)
    send = call(dmixed_kernel, stats_sent, (dpre, inner, w_second), flops=hidden_flops)
    send, third = lax.optimization_barrier((send, third))
    back = exchange(send)

    stats_spec = pl.BlockSpec((PEERS, STATS, LANES), lambda i: (0, rows // STATS, 0))
    all_tokens = whole(*tokens.shape)
    row = whole(1, local_width)
    part = shape((z_size, PAIR, BS), BF16)
    own, other, normed = pl.pallas_call(
        fourth_kernel,
        out_shape=[part, part, shape(tokens.shape, BF16)],
        grid=(1,),
        in_specs=[smem, whole(*plain_sent.shape), all_tokens, all_tokens, row, stats_spec],
        out_specs=[whole(*part.shape), whole(*part.shape), all_tokens],
        compiler_params=params,
        cost_estimate=cost(model_flops),
    )(y_index, third, cotangent, tokens, gain_row, recv)
    fourths = (own, lax.ppermute(other, "dp", y_pairs))
    output = call(output_kernel, shape(tokens.shape, BF16), (third, tokens, w_fourth), flops=LATE * model_flops)
    own, other = pl.pallas_call(
        first_kernel,
        out_shape=[part, part],
        in_specs=[smem, hbm, hbm],
        out_specs=[vmem, vmem],
        scratch_shapes=[
            pltpu.VMEM(plain_sent.shape, BF16),
            pltpu.VMEM(tokens.shape, BF16),
            pltpu.SemaphoreType.DMA((2,)),
        ],
        compiler_params=pltpu.CompilerParams(vmem_limit_bytes=FIRST),
        cost_estimate=cost(model_flops),
    )(y_index, back, normed)
    firsts = (own, lax.ppermute(other, "dp", y_pairs))
    both = call(pair_kernel, shape((z_size, 2 * PAIR, BS), BF16), firsts + fourths, limit=SMALL)
    both = lax.all_to_all(both, "dp", 0, 0, axis_index_groups=z_groups, tiled=True)
    token_gradient = pl.pallas_call(
        token_kernel,
        out_shape=shape(tokens.shape, BF16),
        grid=(1,),
        in_specs=[whole(*stats_sent.shape), stats_spec, all_tokens, row, whole(*w_first.shape), all_tokens],
        out_specs=all_tokens,
        compiler_params=params,
        cost_estimate=cost(LATE * model_flops),
    )(back, recv, tokens, gain_row, w_first, cotangent)
    other = lax.ppermute(hidden[0, 1], "dp", y_pairs)
    part = shape((1, HBS // dp, HBS), F32)
    grad_second, grad_third = call(functools.partial(finish_kernel, scale), [part, part], (hidden, other), limit=SMALL)
    both, grad_second, grad_third = lax.optimization_barrier((both, grad_second, grad_third))
    grad_first, grad_fourth = call(
        functools.partial(sum_kernel, scale),
        [shape((2, BS // dp, HB * EB), F32), shape((2, HB * EB // dp, BS), F32)],
        (both,),
        limit=SMALL,
    )
    return output, token_gradient, grad_first, grad_second, grad_third, grad_fourth


def solution(mesh):
    return jax.shard_map(
        shards,
        mesh=mesh,
        in_specs=(
            P("dp", "tensor"),
            P("tensor"),
            P("tensor", None, None),
            P("tensor", None, None),
            P("tensor", None, None),
            P("tensor", None, None),
            P("dp", "tensor"),
        ),
        out_specs=(
            P("dp", "tensor"),
            P("dp", "tensor"),
            P("tensor", "dp", None),
            P("tensor", "dp", None),
            P("tensor", "dp", None),
            P("tensor", "dp", None),
        ),
        check_vma=False,
    )
```

```python
import functools
import math

import jax
import jax.numpy as jnp
from jax import lax
from jax.experimental import pallas as pl
from jax.experimental.pallas import tpu as pltpu
from jax.sharding import PartitionSpec as P

MODEL_WIDTH = 8192
DIAGONAL_BLOCKS = 32
HBS = 1024
HB = 16
BS = 256
EB = 32
PEERS = 16
PAIR = 2 * EB
LANES = 128
STATS = 16
STEP = 256
LATE = 160
VMEM = 58 * 1024 * 1024
SMALL = 16 * 1024 * 1024
FIRST = 24 * 1024 * 1024

epsilon = 1e-05
root_scale = math.sqrt(2.0 / math.pi)
cubic_term = 0.044715

F32 = jnp.float32
BF16 = jnp.bfloat16

NN = (((1,), (0,)), ((), ()))
NT = (((1,), (1,)), ((), ()))
TN = (((0,), (0,)), ((), ()))
TT = (((0,), (1,)), ((), ()))


def dot(a, b, dims):
    return lax.dot_general(a, b, dims, preferred_element_type=F32)


def call(kernel, out_shape, args, scratch=(), flops=0, limit=None, **extra):
    outs = out_shape if isinstance(out_shape, (list, tuple)) else [out_shape]
    moved = sum(a.size * a.dtype.itemsize for a in args) + sum(
        math.prod(o.shape) * o.dtype.itemsize for o in outs
    )
    return pl.pallas_call(
        kernel,
        out_shape=out_shape,
        in_specs=[pl.BlockSpec(memory_space=pltpu.VMEM)] * len(args),
        out_specs=jax.tree.map(lambda _: pl.BlockSpec(memory_space=pltpu.VMEM), out_shape),
        scratch_shapes=list(scratch),
        compiler_params=pltpu.CompilerParams(vmem_limit_bytes=limit or VMEM),
        cost_estimate=pl.CostEstimate(flops=int(flops), bytes_accessed=int(moved), transcendentals=0),
        **extra,
    )(*args)


def stat_rows(value, chunks):
    high = value.astype(BF16).astype(F32)
    low = value - high
    rows = []
    for i in range(chunks):
        part = slice(i * LANES, (i + 1) * LANES)
        rows += [high[:, part], low[:, part]]
    rows.append(jnp.zeros((STATS - 2 * chunks, LANES), F32))
    return jnp.concatenate(rows, axis=0).astype(BF16)


def stat_sum(rows):
    return jnp.sum(rows.astype(F32), axis=0)


class Copies:
    def __init__(self, sems):
        self.sems = sems
        self.started = []

    def start(self, source, target):
        copy = pltpu.make_async_copy(source, target, self.sems.at[len(self.started)])
        copy.start()
        self.started.append(copy)
        return copy

    def wait(self):
        for copy in self.started:
            copy.wait()


def head_kernel(x_hbm, gain_ref, w1_hbm, out_hbm, x_ref, w1_ref, out_ref, in_sems, out_sems):
    steps = x_ref.shape[0] // STEP
    loads, stores = Copies(in_sems), Copies(out_sems)
    w1_load = loads.start(w1_hbm, w1_ref)
    parts = [pl.ds(i * STEP, STEP) for i in range(steps)]
    x_loads = [loads.start(x_hbm.at[part], x_ref.at[part]) for part in parts]
    w1_load.wait()
    turned = [w1_ref[a].T for a in range(2)]
    totals = []
    for i in range(steps):
        x_loads[i].wait()
        x = x_ref[parts[i], :].astype(F32)
        scaled = (x * gain_ref[...]).astype(BF16)
        base = i * 2 * PAIR
        for a in range(2):
            first = dot(turned[a], scaled[:, a * BS : (a + 1) * BS], NT).astype(BF16)
            for k in range(2):
                start = base + k * PAIR + a * EB
                value = first[:, k * LANES : (k + 1) * LANES]
                out_ref[:, start : start + EB, :] = value.reshape(PEERS, EB, LANES)
        part = pl.ds(base, 2 * PAIR)
        stores.start(out_ref.at[:, part], out_hbm.at[:, part])
        squares = x * x
        folded = squares[:, :LANES]
        for k in range(1, squares.shape[1] // LANES):
            folded = folded + squares[:, k * LANES : (k + 1) * LANES]
        totals.append(jnp.sum(folded.T, axis=0, keepdims=True))
    rows = steps * 2 * PAIR
    stats = stat_rows(jnp.concatenate(totals, axis=1), 2 * steps)
    out_ref[:, rows:, :] = jnp.broadcast_to(stats[None], (PEERS, STATS, LANES))
    part = pl.ds(rows, STATS)
    stores.start(out_ref.at[:, part], out_hbm.at[:, part])
    stores.wait()


def dgathered_kernel(w4_ref, cot_ref, out_ref):
    chunks = cot_ref.shape[0] // LANES
    for a in range(2):
        dgathered = dot(w4_ref[a], cot_ref[:, a * BS : (a + 1) * BS], NT).astype(BF16)
        for i in range(chunks):
            start = i * PAIR + a * EB
            value = dgathered[:, i * LANES : (i + 1) * LANES]
            out_ref[:, start : start + EB, :] = value.reshape(PEERS, EB, LANES)


def reciprocal(stats, i):
    rows = stats[4 * i : 4 * i + 4]
    total = jnp.concatenate([rows[0:1] + rows[1:2], rows[2:3] + rows[3:4]], axis=1)
    return lax.rsqrt(total / MODEL_WIDTH + epsilon)


def hidden_rows(ref):
    sources, rows, _ = ref.shape
    parts = [
        ref[:, i * PAIR : (i + 1) * PAIR, :].reshape(sources * PAIR, LANES) for i in range(rows // PAIR)
    ]
    return jnp.concatenate(parts, axis=1)


def turn_kernel(w2_ref, w3_ref, w2t_ref, w3t_ref):
    w2t_ref[...] = w2_ref[0].T
    w3t_ref[...] = w3_ref[0].T


def by_peer(value):
    parts = [value[:, k * LANES : (k + 1) * LANES].reshape(PEERS, PAIR, LANES) for k in range(2)]
    return jnp.concatenate(parts, axis=1)


def forward_kernel(
    recv_hbm, w2t_hbm, w3t_hbm, slope_hbm, act_hbm, out_hbm,
    recv_ref, w2t_ref, w3t_ref, slope_ref, act_ref, out_ref, in_sems, out_sems,
):
    steps = act_ref.shape[0]
    rows = steps * 2 * PAIR
    loads, stores = Copies(in_sems), Copies(out_sems)
    parts = [pl.ds(i * 2 * PAIR, 2 * PAIR) for i in range(steps)]
    rest = pl.ds(rows, STATS)
    stats_load = loads.start(recv_hbm.at[:, rest], recv_ref.at[:, rest])
    row_loads = [loads.start(recv_hbm.at[:, parts[0]], recv_ref.at[:, parts[0]])]
    w2t_load = loads.start(w2t_hbm, w2t_ref)
    for part in parts[1:]:
        row_loads.append(loads.start(recv_hbm.at[:, part], recv_ref.at[:, part]))
    w3t_load = loads.start(w3t_hbm, w3t_ref)
    stats_load.wait()
    stats = stat_sum(recv_ref[:, rows:, :])
    w2t_load.wait()
    for i in range(steps):
        row_loads[i].wait()
        pre = dot(w2t_ref[...], hidden_rows(recv_ref.at[:, parts[i]]), NN) * reciprocal(stats, i)
        square = pre * pre
        hyper = jnp.tanh(pre * (root_scale + (root_scale * cubic_term) * square))
        half = 0.5 * pre
        act_ref[i] = (half + half * hyper).astype(BF16)
        slope = (0.5 + 0.5 * hyper) + half * (1.0 - hyper * hyper) * (
            root_scale + (3.0 * root_scale * cubic_term) * square
        )
        slope_ref[i] = slope.astype(BF16)
        stores.start(slope_ref.at[i], slope_hbm.at[i])
    stores.start(act_ref, act_hbm)
    w3t_load.wait()
    for i in range(steps):
        third = dot(w3t_ref[...], act_ref[i], NN).astype(BF16)
        out_ref[:, i * 2 * PAIR : (i + 1) * 2 * PAIR, :] = by_peer(third)
        stores.start(out_ref.at[:, parts[i]], out_hbm.at[:, parts[i]])
    stores.wait()


def backward_kernel(
    y_ref, recv_hbm, dthird_hbm, slope_hbm, act_hbm, w3_hbm, grads_hbm, dpre_hbm,
    recv_ref, dthird_ref, slope_ref, act_ref, w3_ref, dpre_ref, scaled_ref, grads_ref, in_sems, out_sems,
):
    steps = act_ref.shape[0]
    rows = steps * 2 * PAIR
    y = y_ref[0]
    loads, stores = Copies(in_sems), Copies(out_sems)

    parts = [pl.ds(i * 2 * PAIR, 2 * PAIR) for i in range(steps)]
    rest = pl.ds(rows, STATS)
    stats_load = loads.start(recv_hbm.at[:, rest], recv_ref.at[:, rest])
    w3_load = loads.start(w3_hbm, w3_ref)
    third_loads = [loads.start(dthird_hbm.at[:, part], dthird_ref.at[:, part]) for part in parts]
    slope_loads = [loads.start(slope_hbm.at[i], slope_ref.at[i]) for i in range(steps)]
    act_load = loads.start(act_hbm, act_ref)
    mixed_load = loads.start(recv_hbm.at[:, pl.ds(0, rows)], recv_ref.at[:, pl.ds(0, rows)])
    stats_load.wait()
    stats = stat_sum(recv_ref[:, rows:, :])
    w3_load.wait()
    for i in range(steps):
        third_loads[i].wait()
        slope_loads[i].wait()
        dact = dot(w3_ref[0], hidden_rows(dthird_ref.at[:, parts[i]]), NN)
        dpre = dact * slope_ref[i].astype(F32)
        dpre_ref[i] = dpre.astype(BF16)
        scaled_ref[i] = (dpre * reciprocal(stats, i)).astype(BF16)
    stores.start(dpre_ref, dpre_hbm)
    act_load.wait()
    mixed_load.wait()
    dthird = hidden_rows(dthird_ref)
    scaled = jnp.concatenate([scaled_ref[i] for i in range(steps)], axis=1)
    z_size, y_size, part_rows, _ = grads_ref.shape
    half = z_size // 2
    size = half * part_rows
    for r in range(2 * y_size):
        z = pl.ds(r % 2 * half, half)
        act = jnp.concatenate([act_ref[i, r * size : (r + 1) * size, :] for i in range(steps)], axis=1)
        third = dot(act, dthird, NT).astype(BF16)
        grads_ref[z, r // 2, :, HBS:] = third.reshape(half, part_rows, HBS)
        sources = pl.ds(r * (size // PAIR), size // PAIR)
        mixed = hidden_rows(recv_ref.at[sources, pl.ds(0, rows)])
        second = dot(mixed, scaled, NT).astype(BF16)
        grads_ref[z, r // 2, :, :HBS] = second.reshape(half, part_rows, HBS)
        stores.start(grads_ref.at[z, r // 2], grads_hbm.at[z, lax.rem(r // 2 + y, y_size)])
    stores.wait()


def dmixed_kernel(dpre_ref, recv_ref, w2_ref, out_ref):
    steps = dpre_ref.shape[0]
    rows = steps * 2 * PAIR
    stats = stat_sum(recv_ref[:, rows:, :])
    inner = []
    for i in range(steps):
        part = slice(i * 2 * PAIR, (i + 1) * 2 * PAIR)
        dmixed = dot(w2_ref[0], dpre_ref[i], NN)
        out_ref[:, part, :] = by_peer(dmixed.astype(BF16))
        mixed = hidden_rows(recv_ref.at[:, part]).astype(F32)
        inner.append(jnp.sum(dmixed * mixed, axis=0, keepdims=True) * reciprocal(stats, i))
    rest = stat_rows(jnp.concatenate(inner, axis=1), 2 * steps)
    out_ref[:, rows:, :] = jnp.broadcast_to(rest[None], (PEERS, STATS, LANES))


def model_rows(ref, chunks, a):
    parts = []
    for i in range(chunks):
        start = i * PAIR + a * EB
        parts.append(ref[:, start : start + EB, :].reshape(HB * EB, LANES))
    return jnp.concatenate(parts, axis=1)


def columns(stats, chunks):
    turned = stats.T
    parts = [turned[:, 2 * i : 2 * i + 1] + turned[:, 2 * i + 1 : 2 * i + 2] for i in range(chunks)]
    return jnp.concatenate(parts, axis=0)


def output_kernel(recv_ref, x_ref, w4_ref, out_ref):
    chunks = x_ref.shape[0] // LANES
    for a in range(2):
        feats = slice(a * BS, (a + 1) * BS)
        branch = dot(model_rows(recv_ref, chunks, a), w4_ref[a], TN)
        out_ref[:, feats] = (x_ref[:, feats].astype(F32) + branch).astype(BF16)


def fourth_kernel(y_ref, recv_ref, cot_ref, x_ref, gain_ref, stats_ref, own_ref, other_ref, normed_ref):
    chunks = cot_ref.shape[0] // LANES
    z_size = own_ref.shape[0]
    rows = HB * EB // PEERS
    for a in range(2):
        grad = dot(model_rows(recv_ref, chunks, a), cot_ref[:, a * BS : (a + 1) * BS], NN).astype(BF16)
        grad = grad.reshape(PEERS, rows, BS)
        part = slice(a * rows, (a + 1) * rows)
        own_ref[:, part, :] = jnp.where(y_ref[0] == 0, grad[:z_size], grad[z_size:])
        other_ref[:, part, :] = jnp.where(y_ref[0] == 0, grad[z_size:], grad[:z_size])
    inverse = lax.rsqrt(columns(stat_sum(stats_ref[...]), chunks) / MODEL_WIDTH + epsilon)
    normed_ref[...] = (x_ref[...].astype(F32) * inverse * gain_ref[...]).astype(BF16)


def pair_kernel(first_own, first_other, fourth_own, fourth_other, out_ref):
    out_ref[:, :PAIR, :] = (first_own[...].astype(F32) + first_other[...].astype(F32)).astype(BF16)
    out_ref[:, PAIR:, :] = (fourth_own[...].astype(F32) + fourth_other[...].astype(F32)).astype(BF16)


def first_kernel(y_ref, recv_hbm, normed_hbm, own_ref, other_ref, recv_ref, normed_ref, sems):
    chunks = normed_ref.shape[0] // LANES
    z_size = own_ref.shape[0]
    loads = Copies(sems)
    loads.start(normed_hbm, normed_ref)
    loads.start(recv_hbm.at[:, pl.ds(0, chunks * PAIR)], recv_ref)
    loads.wait()
    rows = BS // PEERS
    for a in range(2):
        dfirst = model_rows(recv_ref, chunks, a)
        grad = dot(dfirst, normed_ref[:, a * BS : (a + 1) * BS], NN).astype(BF16).T
        for half in range(2):
            base = (2 * a + half) * rows
            value = grad[:, half * BS : (half + 1) * BS].reshape(PEERS, rows, BS)
            part = slice(base, base + rows)
            own_ref[:, part, :] = jnp.where(y_ref[0] == 0, value[:z_size], value[z_size:])
            other_ref[:, part, :] = jnp.where(y_ref[0] == 0, value[z_size:], value[:z_size])


def token_kernel(recv_ref, stats_ref, x_ref, gain_ref, w1_ref, cot_ref, out_ref):
    chunks = x_ref.shape[0] // LANES
    inverse = lax.rsqrt(columns(stat_sum(stats_ref[...]), chunks) / MODEL_WIDTH + epsilon)
    inner = columns(stat_sum(recv_ref[:, chunks * PAIR :, :]), chunks) / MODEL_WIDTH
    for a in range(2):
        feats = slice(a * BS, (a + 1) * BS)
        dfirst = model_rows(recv_ref, chunks, a)
        dnormed = dot(dfirst, w1_ref[a], TT)
        xhat = x_ref[:, feats].astype(F32) * inverse
        change = dnormed * gain_ref[:, feats] - xhat * inner
        out_ref[:, feats] = (cot_ref[:, feats].astype(F32) + inverse * change).astype(BF16)


def sum_kernel(scale, recv_ref, first_ref, fourth_ref):
    total = jnp.sum(recv_ref[...].astype(F32), axis=0) * scale
    _, rows, _ = first_ref.shape
    for a in range(2):
        for half in range(2):
            base = (2 * a + half) * rows
            first_ref[a, :, half * BS : (half + 1) * BS] = total[base : base + rows]
    fourth_ref[...] = total[PAIR:].reshape(fourth_ref.shape)


def finish_kernel(scale, own_ref, other_ref, second_ref, third_ref):
    total = (own_ref[0, 0].astype(F32) + other_ref[...].astype(F32)) * scale
    second_ref[0] = total[:, :HBS]
    third_ref[0] = total[:, HBS:]


def shards(tokens, gain, w_first, w_second, w_third, w_fourth, cotangent):
    element_count, local_width = tokens.shape
    dp = lax.axis_size("dp")
    scale = 1.0 / math.sqrt(element_count * dp)
    gain_row = gain[None, :]
    z_size = dp // 2
    z_groups = [[y * z_size + z for z in range(z_size)] for y in range(2)]
    y_pairs = [(i, (i + z_size) % dp) for i in range(dp)]
    y_index = (lax.axis_index("dp") // z_size).astype(jnp.int32)[None]
    shape = jax.ShapeDtypeStruct
    hidden_flops = 2 * HBS * HBS * element_count
    model_flops = 2 * local_width * HB * EB * element_count
    steps = element_count // STEP
    rows = steps * 2 * PAIR
    plain_sent = shape((PEERS, rows, LANES), BF16)
    stats_sent = shape((PEERS, rows + STATS, LANES), BF16)
    stepped = shape((steps, HBS, STEP), BF16)
    hbm = pl.BlockSpec(memory_space=pltpu.HBM)
    vmem = pl.BlockSpec(memory_space=pltpu.VMEM)
    smem = pl.BlockSpec(memory_space=pltpu.SMEM)
    params = pltpu.CompilerParams(vmem_limit_bytes=VMEM)

    def cost(flops):
        return pl.CostEstimate(flops=int(flops), bytes_accessed=8 << 20, transcendentals=0)

    def whole(*dims):
        return pl.BlockSpec(dims, lambda i, *_: (0,) * len(dims))

    def exchange(value):
        return lax.all_to_all(value, "tensor", 0, 0, tiled=True)

    send = pl.pallas_call(
        head_kernel,
        out_shape=stats_sent,
        in_specs=[hbm, vmem, hbm],
        out_specs=hbm,
        scratch_shapes=[
            pltpu.VMEM(tokens.shape, BF16),
            pltpu.VMEM(w_first.shape, BF16),
            pltpu.VMEM(stats_sent.shape, BF16),
            pltpu.SemaphoreType.DMA((steps + 1,)),
            pltpu.SemaphoreType.DMA((steps + 1,)),
        ],
        compiler_params=params,
        cost_estimate=cost(model_flops),
    )(tokens, gain_row, w_first)
    recv = exchange(send)
    send = call(dgathered_kernel, plain_sent, (w_fourth, cotangent), flops=model_flops)
    dthird = exchange(lax.optimization_barrier((send, recv))[0])
    turned = shape((HBS, HBS), BF16)
    w_second_t, w_third_t = call(turn_kernel, [turned, turned], (w_second, w_third))
    slope, act, send = pl.pallas_call(
        forward_kernel,
        out_shape=[stepped, stepped, plain_sent],
        in_specs=[hbm] * 3,
        out_specs=[hbm] * 3,
        scratch_shapes=[
            pltpu.VMEM(stats_sent.shape, BF16),
            pltpu.VMEM(turned.shape, BF16),
            pltpu.VMEM(turned.shape, BF16),
            pltpu.VMEM(stepped.shape, BF16),
            pltpu.VMEM(stepped.shape, BF16),
            pltpu.VMEM(plain_sent.shape, BF16),
            pltpu.SemaphoreType.DMA((steps + 3,)),
            pltpu.SemaphoreType.DMA((2 * steps + 1,)),
        ],
        compiler_params=params,
        cost_estimate=cost(2 * hidden_flops),
    )(recv, w_second_t, w_third_t)
    third = exchange(lax.optimization_barrier((send, dthird))[0])
    grads = shape((z_size, 2, HBS // dp, 2 * HBS), BF16)
    hidden, dpre = pl.pallas_call(
        backward_kernel,
        out_shape=[grads, stepped],
        in_specs=[smem] + [hbm] * 5,
        out_specs=[hbm, hbm],
        scratch_shapes=[
            pltpu.VMEM(stats_sent.shape, BF16),
            pltpu.VMEM(plain_sent.shape, BF16),
            pltpu.VMEM(stepped.shape, BF16),
            pltpu.VMEM(stepped.shape, BF16),
            pltpu.VMEM(w_third.shape, BF16),
            pltpu.VMEM(stepped.shape, BF16),
            pltpu.VMEM(stepped.shape, BF16),
            pltpu.VMEM(grads.shape, BF16),
            pltpu.SemaphoreType.DMA((2 * steps + 4,)),
            pltpu.SemaphoreType.DMA((5,)),
        ],
        compiler_params=params,
        cost_estimate=cost(3 * hidden_flops),
    )(y_index, recv, dthird, slope, act, w_third)
    hidden = lax.psum_scatter(hidden, "dp", scatter_dimension=0, axis_index_groups=z_groups, tiled=True)
    send = call(dmixed_kernel, stats_sent, (dpre, recv, w_second), flops=hidden_flops)
    send, third = lax.optimization_barrier((send, third))
    back = exchange(send)

    stats_spec = pl.BlockSpec((PEERS, STATS, LANES), lambda i: (0, rows // STATS, 0))
    all_tokens = whole(*tokens.shape)
    row = whole(1, local_width)
    part = shape((z_size, PAIR, BS), BF16)
    own, other, normed = pl.pallas_call(
        fourth_kernel,
        out_shape=[part, part, shape(tokens.shape, BF16)],
        grid=(1,),
        in_specs=[smem, whole(*plain_sent.shape), all_tokens, all_tokens, row, stats_spec],
        out_specs=[whole(*part.shape), whole(*part.shape), all_tokens],
        compiler_params=params,
        cost_estimate=cost(model_flops),
    )(y_index, third, cotangent, tokens, gain_row, recv)
    fourths = (own, lax.ppermute(other, "dp", y_pairs))
    output = call(output_kernel, shape(tokens.shape, BF16), (third, tokens, w_fourth), flops=LATE * model_flops)
    own, other = pl.pallas_call(
        first_kernel,
        out_shape=[part, part],
        in_specs=[smem, hbm, hbm],
        out_specs=[vmem, vmem],
        scratch_shapes=[
            pltpu.VMEM(plain_sent.shape, BF16),
            pltpu.VMEM(tokens.shape, BF16),
            pltpu.SemaphoreType.DMA((2,)),
        ],
        compiler_params=pltpu.CompilerParams(vmem_limit_bytes=FIRST),
        cost_estimate=cost(model_flops),
    )(y_index, back, normed)
    firsts = (own, lax.ppermute(other, "dp", y_pairs))
    both = call(pair_kernel, shape((z_size, 2 * PAIR, BS), BF16), firsts + fourths, limit=SMALL)
    both = lax.all_to_all(both, "dp", 0, 0, axis_index_groups=z_groups, tiled=True)
    token_gradient = pl.pallas_call(
        token_kernel,
        out_shape=shape(tokens.shape, BF16),
        grid=(1,),
        in_specs=[whole(*stats_sent.shape), stats_spec, all_tokens, row, whole(*w_first.shape), all_tokens],
        out_specs=all_tokens,
        compiler_params=params,
        cost_estimate=cost(LATE * model_flops),
    )(back, recv, tokens, gain_row, w_first, cotangent)
    other = lax.ppermute(hidden[0, 1], "dp", y_pairs)
    part = shape((1, HBS // dp, HBS), F32)
    grad_second, grad_third = call(functools.partial(finish_kernel, scale), [part, part], (hidden, other), limit=SMALL)
    both, grad_second, grad_third = lax.optimization_barrier((both, grad_second, grad_third))
    grad_first, grad_fourth = call(
        functools.partial(sum_kernel, scale),
        [shape((2, BS // dp, HB * EB), F32), shape((2, HB * EB // dp, BS), F32)],
        (both,),
        limit=SMALL,
    )
    return output, token_gradient, grad_first, grad_second, grad_third, grad_fourth


def solution(mesh):
    return jax.shard_map(
        shards,
        mesh=mesh,
        in_specs=(
            P("dp", "tensor"),
            P("tensor"),
            P("tensor", None, None),
            P("tensor", None, None),
            P("tensor", None, None),
            P("tensor", None, None),
            P("dp", "tensor"),
        ),
        out_specs=(
            P("dp", "tensor"),
            P("dp", "tensor"),
            P("tensor", "dp", None),
            P("tensor", "dp", None),
            P("tensor", "dp", None),
            P("tensor", "dp", None),
        ),
        check_vma=False,
    )
```

```python
import functools
import math

import jax
import jax.numpy as jnp
from jax import lax
from jax.experimental import pallas as pl
from jax.experimental.pallas import tpu as pltpu
from jax.sharding import PartitionSpec as P

MODEL_WIDTH = 8192
DIAGONAL_BLOCKS = 32
HBS = 1024
HB = 16
BS = 256
EB = 32
PEERS = 16
PAIR = 2 * EB
LANES = 128
STATS = 16
STEP = 256
LATE = 160
VMEM = 58 * 1024 * 1024
SMALL = 16 * 1024 * 1024
FIRST = 24 * 1024 * 1024

epsilon = 1e-05
root_scale = math.sqrt(2.0 / math.pi)
cubic_term = 0.044715

F32 = jnp.float32
BF16 = jnp.bfloat16

NN = (((1,), (0,)), ((), ()))
NT = (((1,), (1,)), ((), ()))
TN = (((0,), (0,)), ((), ()))
TT = (((0,), (1,)), ((), ()))


def dot(a, b, dims):
    return lax.dot_general(a, b, dims, preferred_element_type=F32)


def call(kernel, out_shape, args, scratch=(), flops=0, limit=None, **extra):
    outs = out_shape if isinstance(out_shape, (list, tuple)) else [out_shape]
    moved = sum(a.size * a.dtype.itemsize for a in args) + sum(
        math.prod(o.shape) * o.dtype.itemsize for o in outs
    )
    return pl.pallas_call(
        kernel,
        out_shape=out_shape,
        in_specs=[pl.BlockSpec(memory_space=pltpu.VMEM)] * len(args),
        out_specs=jax.tree.map(lambda _: pl.BlockSpec(memory_space=pltpu.VMEM), out_shape),
        scratch_shapes=list(scratch),
        compiler_params=pltpu.CompilerParams(vmem_limit_bytes=limit or VMEM),
        cost_estimate=pl.CostEstimate(flops=int(flops), bytes_accessed=int(moved), transcendentals=0),
        **extra,
    )(*args)


def stat_rows(value, chunks):
    high = value.astype(BF16).astype(F32)
    low = value - high
    rows = []
    for i in range(chunks):
        part = slice(i * LANES, (i + 1) * LANES)
        rows += [high[:, part], low[:, part]]
    rows.append(jnp.zeros((STATS - 2 * chunks, LANES), F32))
    return jnp.concatenate(rows, axis=0).astype(BF16)


def stat_sum(rows):
    return jnp.sum(rows.astype(F32), axis=0)


class Copies:
    def __init__(self, sems):
        self.sems = sems
        self.started = []

    def start(self, source, target):
        copy = pltpu.make_async_copy(source, target, self.sems.at[len(self.started)])
        copy.start()
        self.started.append(copy)
        return copy

    def wait(self):
        for copy in self.started:
            copy.wait()


def first_factor_kernel(x_ref, gain_ref, w1_ref, out_ref, squares_ref):
    a = pl.program_id(0)
    chunks = x_ref.shape[0] // LANES
    x = x_ref[...].astype(F32)
    first = dot(w1_ref[0].T, (x * gain_ref[...]).astype(BF16), NT).astype(BF16)
    base = pl.multiple_of(a * EB, EB)
    for i in range(chunks):
        part = slice(i * LANES, (i + 1) * LANES)
        out_ref[:, pl.ds(i * PAIR + base, EB), :] = first[:, part].reshape(PEERS, EB, LANES)
    squares = x * x
    total = jnp.sum((squares[:, :LANES] + squares[:, LANES:]).T, axis=0, keepdims=True)

    @pl.when(a == 0)
    def _():
        squares_ref[...] = total

    @pl.when(a == 1)
    def _():
        rows = stat_rows(squares_ref[...] + total, chunks)
        out_ref[:, chunks * PAIR :, :] = jnp.broadcast_to(rows[None], (PEERS, STATS, LANES))


def dgathered_kernel(w4_ref, cot_ref, out_ref):
    chunks = cot_ref.shape[0] // LANES
    for a in range(2):
        dgathered = dot(w4_ref[a], cot_ref[:, a * BS : (a + 1) * BS], NT).astype(BF16)
        for i in range(chunks):
            start = i * PAIR + a * EB
            value = dgathered[:, i * LANES : (i + 1) * LANES]
            out_ref[:, start : start + EB, :] = value.reshape(PEERS, EB, LANES)


def reciprocal(stats, i):
    rows = stats[4 * i : 4 * i + 4]
    total = jnp.concatenate([rows[0:1] + rows[1:2], rows[2:3] + rows[3:4]], axis=1)
    return lax.rsqrt(total / MODEL_WIDTH + epsilon)


def hidden_rows(ref):
    sources, rows, _ = ref.shape
    parts = [
        ref[:, i * PAIR : (i + 1) * PAIR, :].reshape(sources * PAIR, LANES) for i in range(rows // PAIR)
    ]
    return jnp.concatenate(parts, axis=1)


def turn_kernel(w2_ref, w3_ref, w2t_ref, w3t_ref):
    w2t_ref[...] = w2_ref[0].T
    w3t_ref[...] = w3_ref[0].T


def by_peer(value):
    parts = [value[:, k * LANES : (k + 1) * LANES].reshape(PEERS, PAIR, LANES) for k in range(2)]
    return jnp.concatenate(parts, axis=1)


def forward_kernel(
    recv_hbm, w2t_hbm, w3t_hbm, slope_hbm, act_hbm, out_hbm,
    recv_ref, w2t_ref, w3t_ref, slope_ref, act_ref, out_ref, in_sems, out_sems,
):
    steps = act_ref.shape[0]
    rows = steps * 2 * PAIR
    loads, stores = Copies(in_sems), Copies(out_sems)
    parts = [pl.ds(i * 2 * PAIR, 2 * PAIR) for i in range(steps)]
    rest = pl.ds(rows, STATS)
    stats_load = loads.start(recv_hbm.at[:, rest], recv_ref.at[:, rest])
    row_loads = [loads.start(recv_hbm.at[:, parts[0]], recv_ref.at[:, parts[0]])]
    w2t_load = loads.start(w2t_hbm, w2t_ref)
    for part in parts[1:]:
        row_loads.append(loads.start(recv_hbm.at[:, part], recv_ref.at[:, part]))
    w3t_load = loads.start(w3t_hbm, w3t_ref)
    stats_load.wait()
    stats = stat_sum(recv_ref[:, rows:, :])
    w2t_load.wait()
    for i in range(steps):
        row_loads[i].wait()
        pre = dot(w2t_ref[...], hidden_rows(recv_ref.at[:, parts[i]]), NN) * reciprocal(stats, i)
        square = pre * pre
        hyper = jnp.tanh(pre * (root_scale + (root_scale * cubic_term) * square))
        half = 0.5 * pre
        act_ref[i] = (half + half * hyper).astype(BF16)
        slope = (0.5 + 0.5 * hyper) + half * (1.0 - hyper * hyper) * (
            root_scale + (3.0 * root_scale * cubic_term) * square
        )
        slope_ref[i] = slope.astype(BF16)
        stores.start(slope_ref.at[i], slope_hbm.at[i])
    stores.start(act_ref, act_hbm)
    w3t_load.wait()
    for i in range(steps):
        third = dot(w3t_ref[...], act_ref[i], NN).astype(BF16)
        out_ref[:, i * 2 * PAIR : (i + 1) * 2 * PAIR, :] = by_peer(third)
        stores.start(out_ref.at[:, parts[i]], out_hbm.at[:, parts[i]])
    stores.wait()


def backward_kernel(
    y_ref, recv_hbm, dthird_hbm, slope_hbm, act_hbm, w3_hbm, grads_hbm, dpre_hbm,
    recv_ref, dthird_ref, slope_ref, act_ref, w3_ref, dpre_ref, scaled_ref, grads_ref, in_sems, out_sems,
):
    steps = act_ref.shape[0]
    rows = steps * 2 * PAIR
    y = y_ref[0]
    loads, stores = Copies(in_sems), Copies(out_sems)

    parts = [pl.ds(i * 2 * PAIR, 2 * PAIR) for i in range(steps)]
    rest = pl.ds(rows, STATS)
    stats_load = loads.start(recv_hbm.at[:, rest], recv_ref.at[:, rest])
    w3_load = loads.start(w3_hbm, w3_ref)
    third_loads = [loads.start(dthird_hbm.at[:, part], dthird_ref.at[:, part]) for part in parts]
    slope_loads = [loads.start(slope_hbm.at[i], slope_ref.at[i]) for i in range(steps)]
    act_load = loads.start(act_hbm, act_ref)
    mixed_load = loads.start(recv_hbm.at[:, pl.ds(0, rows)], recv_ref.at[:, pl.ds(0, rows)])
    stats_load.wait()
    stats = stat_sum(recv_ref[:, rows:, :])
    w3_load.wait()
    for i in range(steps):
        third_loads[i].wait()
        slope_loads[i].wait()
        dact = dot(w3_ref[0], hidden_rows(dthird_ref.at[:, parts[i]]), NN)
        dpre = dact * slope_ref[i].astype(F32)
        dpre_ref[i] = dpre.astype(BF16)
        scaled_ref[i] = (dpre * reciprocal(stats, i)).astype(BF16)
    stores.start(dpre_ref, dpre_hbm)
    act_load.wait()
    mixed_load.wait()
    dthird = hidden_rows(dthird_ref)
    scaled = jnp.concatenate([scaled_ref[i] for i in range(steps)], axis=1)
    z_size, y_size, part_rows, _ = grads_ref.shape
    half = z_size // 2
    size = half * part_rows
    for r in range(2 * y_size):
        z = pl.ds(r % 2 * half, half)
        act = jnp.concatenate([act_ref[i, r * size : (r + 1) * size, :] for i in range(steps)], axis=1)
        third = dot(act, dthird, NT).astype(BF16)
        grads_ref[z, r // 2, :, HBS:] = third.reshape(half, part_rows, HBS)
        sources = pl.ds(r * (size // PAIR), size // PAIR)
        mixed = hidden_rows(recv_ref.at[sources, pl.ds(0, rows)])
        second = dot(mixed, scaled, NT).astype(BF16)
        grads_ref[z, r // 2, :, :HBS] = second.reshape(half, part_rows, HBS)
        stores.start(grads_ref.at[z, r // 2], grads_hbm.at[z, lax.rem(r // 2 + y, y_size)])
    stores.wait()


def dmixed_kernel(dpre_ref, recv_ref, w2_ref, out_ref):
    steps = dpre_ref.shape[0]
    rows = steps * 2 * PAIR
    stats = stat_sum(recv_ref[:, rows:, :])
    inner = []
    for i in range(steps):
        part = slice(i * 2 * PAIR, (i + 1) * 2 * PAIR)
        dmixed = dot(w2_ref[0], dpre_ref[i], NN)
        out_ref[:, part, :] = by_peer(dmixed.astype(BF16))
        mixed = hidden_rows(recv_ref.at[:, part]).astype(F32)
        inner.append(jnp.sum(dmixed * mixed, axis=0, keepdims=True) * reciprocal(stats, i))
    rest = stat_rows(jnp.concatenate(inner, axis=1), 2 * steps)
    out_ref[:, rows:, :] = jnp.broadcast_to(rest[None], (PEERS, STATS, LANES))


def model_rows(ref, chunks, a):
    parts = []
    for i in range(chunks):
        start = i * PAIR + a * EB
        parts.append(ref[:, start : start + EB, :].reshape(HB * EB, LANES))
    return jnp.concatenate(parts, axis=1)


def columns(stats, chunks):
    turned = stats.T
    parts = [turned[:, 2 * i : 2 * i + 1] + turned[:, 2 * i + 1 : 2 * i + 2] for i in range(chunks)]
    return jnp.concatenate(parts, axis=0)


def output_kernel(recv_ref, x_ref, w4_ref, out_ref):
    chunks = x_ref.shape[0] // LANES
    for a in range(2):
        feats = slice(a * BS, (a + 1) * BS)
        branch = dot(model_rows(recv_ref, chunks, a), w4_ref[a], TN)
        out_ref[:, feats] = (x_ref[:, feats].astype(F32) + branch).astype(BF16)


def fourth_kernel(y_ref, recv_ref, cot_ref, x_ref, gain_ref, stats_ref, own_ref, other_ref, normed_ref):
    chunks = cot_ref.shape[0] // LANES
    z_size = own_ref.shape[0]
    rows = HB * EB // PEERS
    for a in range(2):
        grad = dot(model_rows(recv_ref, chunks, a), cot_ref[:, a * BS : (a + 1) * BS], NN).astype(BF16)
        grad = grad.reshape(PEERS, rows, BS)
        part = slice(a * rows, (a + 1) * rows)
        own_ref[:, part, :] = jnp.where(y_ref[0] == 0, grad[:z_size], grad[z_size:])
        other_ref[:, part, :] = jnp.where(y_ref[0] == 0, grad[z_size:], grad[:z_size])
    inverse = lax.rsqrt(columns(stat_sum(stats_ref[...]), chunks) / MODEL_WIDTH + epsilon)
    normed_ref[...] = (x_ref[...].astype(F32) * inverse * gain_ref[...]).astype(BF16)


def pair_kernel(first_own, first_other, fourth_own, fourth_other, out_ref):
    out_ref[:, :PAIR, :] = (first_own[...].astype(F32) + first_other[...].astype(F32)).astype(BF16)
    out_ref[:, PAIR:, :] = (fourth_own[...].astype(F32) + fourth_other[...].astype(F32)).astype(BF16)


def first_kernel(y_ref, recv_hbm, normed_hbm, own_ref, other_ref, recv_ref, normed_ref, sems):
    chunks = normed_ref.shape[0] // LANES
    z_size = own_ref.shape[0]
    loads = Copies(sems)
    loads.start(normed_hbm, normed_ref)
    loads.start(recv_hbm.at[:, pl.ds(0, chunks * PAIR)], recv_ref)
    loads.wait()
    rows = BS // PEERS
    for a in range(2):
        dfirst = model_rows(recv_ref, chunks, a)
        grad = dot(dfirst, normed_ref[:, a * BS : (a + 1) * BS], NN).astype(BF16).T
        for half in range(2):
            base = (2 * a + half) * rows
            value = grad[:, half * BS : (half + 1) * BS].reshape(PEERS, rows, BS)
            part = slice(base, base + rows)
            own_ref[:, part, :] = jnp.where(y_ref[0] == 0, value[:z_size], value[z_size:])
            other_ref[:, part, :] = jnp.where(y_ref[0] == 0, value[z_size:], value[:z_size])


def token_kernel(recv_ref, stats_ref, x_ref, gain_ref, w1_ref, cot_ref, out_ref):
    chunks = x_ref.shape[0] // LANES
    inverse = lax.rsqrt(columns(stat_sum(stats_ref[...]), chunks) / MODEL_WIDTH + epsilon)
    inner = columns(stat_sum(recv_ref[:, chunks * PAIR :, :]), chunks) / MODEL_WIDTH
    for a in range(2):
        feats = slice(a * BS, (a + 1) * BS)
        dfirst = model_rows(recv_ref, chunks, a)
        dnormed = dot(dfirst, w1_ref[a], TT)
        xhat = x_ref[:, feats].astype(F32) * inverse
        change = dnormed * gain_ref[:, feats] - xhat * inner
        out_ref[:, feats] = (cot_ref[:, feats].astype(F32) + inverse * change).astype(BF16)


def sum_kernel(scale, recv_ref, first_ref, fourth_ref):
    total = jnp.sum(recv_ref[...].astype(F32), axis=0) * scale
    _, rows, _ = first_ref.shape
    for a in range(2):
        for half in range(2):
            base = (2 * a + half) * rows
            first_ref[a, :, half * BS : (half + 1) * BS] = total[base : base + rows]
    fourth_ref[...] = total[PAIR:].reshape(fourth_ref.shape)


def finish_kernel(scale, own_ref, other_ref, second_ref, third_ref):
    total = (own_ref[0, 0].astype(F32) + other_ref[...].astype(F32)) * scale
    second_ref[0] = total[:, :HBS]
    third_ref[0] = total[:, HBS:]


def shards(tokens, gain, w_first, w_second, w_third, w_fourth, cotangent):
    element_count, local_width = tokens.shape
    dp = lax.axis_size("dp")
    scale = 1.0 / math.sqrt(element_count * dp)
    gain_row = gain[None, :]
    z_size = dp // 2
    z_groups = [[y * z_size + z for z in range(z_size)] for y in range(2)]
    y_pairs = [(i, (i + z_size) % dp) for i in range(dp)]
    y_index = (lax.axis_index("dp") // z_size).astype(jnp.int32)[None]
    shape = jax.ShapeDtypeStruct
    hidden_flops = 2 * HBS * HBS * element_count
    model_flops = 2 * local_width * HB * EB * element_count
    steps = element_count // STEP
    rows = steps * 2 * PAIR
    plain_sent = shape((PEERS, rows, LANES), BF16)
    stats_sent = shape((PEERS, rows + STATS, LANES), BF16)
    stepped = shape((steps, HBS, STEP), BF16)
    hbm = pl.BlockSpec(memory_space=pltpu.HBM)
    vmem = pl.BlockSpec(memory_space=pltpu.VMEM)
    smem = pl.BlockSpec(memory_space=pltpu.SMEM)
    params = pltpu.CompilerParams(vmem_limit_bytes=VMEM)

    def cost(flops):
        return pl.CostEstimate(flops=int(flops), bytes_accessed=8 << 20, transcendentals=0)

    def whole(*dims):
        return pl.BlockSpec(dims, lambda i, *_: (0,) * len(dims))

    def exchange(value):
        return lax.all_to_all(value, "tensor", 0, 0, tiled=True)

    send = pl.pallas_call(
        first_factor_kernel,
        out_shape=stats_sent,
        grid=(2,),
        in_specs=[
            pl.BlockSpec((element_count, BS), lambda a: (0, a)),
            pl.BlockSpec((1, BS), lambda a: (0, a)),
            pl.BlockSpec((1, BS, HB * EB), lambda a: (a, 0, 0)),
        ],
        out_specs=whole(*stats_sent.shape),
        scratch_shapes=[pltpu.VMEM((1, element_count), F32)],
        compiler_params=params,
        cost_estimate=cost(model_flops),
    )(tokens, gain_row, w_first)
    recv = exchange(send)
    send = call(dgathered_kernel, plain_sent, (w_fourth, cotangent), flops=model_flops)
    dthird = exchange(lax.optimization_barrier((send, recv))[0])
    turned = shape((HBS, HBS), BF16)
    w_second_t, w_third_t = call(turn_kernel, [turned, turned], (w_second, w_third))
    slope, act, send = pl.pallas_call(
        forward_kernel,
        out_shape=[stepped, stepped, plain_sent],
        in_specs=[hbm] * 3,
        out_specs=[hbm] * 3,
        scratch_shapes=[
            pltpu.VMEM(stats_sent.shape, BF16),
            pltpu.VMEM(turned.shape, BF16),
            pltpu.VMEM(turned.shape, BF16),
            pltpu.VMEM(stepped.shape, BF16),
            pltpu.VMEM(stepped.shape, BF16),
            pltpu.VMEM(plain_sent.shape, BF16),
            pltpu.SemaphoreType.DMA((steps + 3,)),
            pltpu.SemaphoreType.DMA((2 * steps + 1,)),
        ],
        compiler_params=params,
        cost_estimate=cost(2 * hidden_flops),
    )(recv, w_second_t, w_third_t)
    third = exchange(lax.optimization_barrier((send, dthird))[0])
    grads = shape((z_size, 2, HBS // dp, 2 * HBS), BF16)
    hidden, dpre = pl.pallas_call(
        backward_kernel,
        out_shape=[grads, stepped],
        in_specs=[smem] + [hbm] * 5,
        out_specs=[hbm, hbm],
        scratch_shapes=[
            pltpu.VMEM(stats_sent.shape, BF16),
            pltpu.VMEM(plain_sent.shape, BF16),
            pltpu.VMEM(stepped.shape, BF16),
            pltpu.VMEM(stepped.shape, BF16),
            pltpu.VMEM(w_third.shape, BF16),
            pltpu.VMEM(stepped.shape, BF16),
            pltpu.VMEM(stepped.shape, BF16),
            pltpu.VMEM(grads.shape, BF16),
            pltpu.SemaphoreType.DMA((2 * steps + 4,)),
            pltpu.SemaphoreType.DMA((5,)),
        ],
        compiler_params=params,
        cost_estimate=cost(3 * hidden_flops),
    )(y_index, recv, dthird, slope, act, w_third)
    hidden = lax.psum_scatter(hidden, "dp", scatter_dimension=0, axis_index_groups=z_groups, tiled=True)
    send = call(dmixed_kernel, stats_sent, (dpre, recv, w_second), flops=hidden_flops)
    send, third = lax.optimization_barrier((send, third))
    back = exchange(send)

    stats_spec = pl.BlockSpec((PEERS, STATS, LANES), lambda i: (0, rows // STATS, 0))
    all_tokens = whole(*tokens.shape)
    row = whole(1, local_width)
    part = shape((z_size, PAIR, BS), BF16)
    own, other, normed = pl.pallas_call(
        fourth_kernel,
        out_shape=[part, part, shape(tokens.shape, BF16)],
        grid=(1,),
        in_specs=[smem, whole(*plain_sent.shape), all_tokens, all_tokens, row, stats_spec],
        out_specs=[whole(*part.shape), whole(*part.shape), all_tokens],
        compiler_params=params,
        cost_estimate=cost(model_flops),
    )(y_index, third, cotangent, tokens, gain_row, recv)
    fourths = (own, lax.ppermute(other, "dp", y_pairs))
    output = call(output_kernel, shape(tokens.shape, BF16), (third, tokens, w_fourth), flops=LATE * model_flops)
    own, other = pl.pallas_call(
        first_kernel,
        out_shape=[part, part],
        in_specs=[smem, hbm, hbm],
        out_specs=[vmem, vmem],
        scratch_shapes=[
            pltpu.VMEM(plain_sent.shape, BF16),
            pltpu.VMEM(tokens.shape, BF16),
            pltpu.SemaphoreType.DMA((2,)),
        ],
        compiler_params=pltpu.CompilerParams(vmem_limit_bytes=FIRST),
        cost_estimate=cost(model_flops),
    )(y_index, back, normed)
    firsts = (own, lax.ppermute(other, "dp", y_pairs))
    both = call(pair_kernel, shape((z_size, 2 * PAIR, BS), BF16), firsts + fourths, limit=SMALL)
    both = lax.all_to_all(both, "dp", 0, 0, axis_index_groups=z_groups, tiled=True)
    token_gradient = pl.pallas_call(
        token_kernel,
        out_shape=shape(tokens.shape, BF16),
        grid=(1,),
        in_specs=[whole(*stats_sent.shape), stats_spec, all_tokens, row, whole(*w_first.shape), all_tokens],
        out_specs=all_tokens,
        compiler_params=params,
        cost_estimate=cost(LATE * model_flops),
    )(back, recv, tokens, gain_row, w_first, cotangent)
    other = lax.ppermute(hidden[0, 1], "dp", y_pairs)
    part = shape((1, HBS // dp, HBS), F32)
    grad_second, grad_third = call(functools.partial(finish_kernel, scale), [part, part], (hidden, other), limit=SMALL)
    both, grad_second, grad_third = lax.optimization_barrier((both, grad_second, grad_third))
    grad_first, grad_fourth = call(
        functools.partial(sum_kernel, scale),
        [shape((2, BS // dp, HB * EB), F32), shape((2, HB * EB // dp, BS), F32)],
        (both,),
        limit=SMALL,
    )
    return output, token_gradient, grad_first, grad_second, grad_third, grad_fourth


def solution(mesh):
    return jax.shard_map(
        shards,
        mesh=mesh,
        in_specs=(
            P("dp", "tensor"),
            P("tensor"),
            P("tensor", None, None),
            P("tensor", None, None),
            P("tensor", None, None),
            P("tensor", None, None),
            P("dp", "tensor"),
        ),
        out_specs=(
            P("dp", "tensor"),
            P("dp", "tensor"),
            P("tensor", "dp", None),
            P("tensor", "dp", None),
            P("tensor", "dp", None),
            P("tensor", "dp", None),
        ),
        check_vma=False,
    )
```
